32 devices in a mesh: dp: 16 (over z, x, core), mp: 2 (over y).
Axes of the slice: x: 2, y: 2, z: 4, core: 2. Of those that a mesh axis runs over, the one named last changes fastest.
Arguments:
- patches: bfloat16 [192, 196, 768], P(('dp', 'mp')), may hold values from -6 to 6
- cotangent: bfloat16 [192, 196, 768], P(('dp', 'mp')), may hold values from -26 to 26
- gain_one: float32 [768], replicated, may hold values from 0.5 to 2
- shift_one: float32 [768], replicated, may hold values from -3 to 3
- token_in: bfloat16 [196, 384], P(None, 'mp'), may hold values from -0.4375 to 0.4375
- token_bias: float32 [384], P('mp'), may hold values from -3 to 3
- token_out: bfloat16 [384, 196], P('mp'), may hold values from -0.4375 to 0.4375
- token_shift: float32 [196], replicated, may hold values from -3 to 3
- gain_two: float32 [768], replicated, may hold values from 0.5 to 2
- shift_two: float32 [768], replicated, may hold values from -3 to 3
- channel_in: bfloat16 [768, 3072], P(None, 'mp'), may hold values from -0.21875 to 0.21875
- channel_bias: float32 [3072], P('mp'), may hold values from -3 to 3
- channel_out: bfloat16 [3072, 768], P('mp'), may hold values from -0.15625 to 0.15625
- channel_shift: float32 [768], replicated, may hold values from -3 to 3
Outputs:
- mixed: bfloat16 [192, 196, 768], P(('dp', 'mp'))
- inputs_grad: float32 [192, 196, 768], P(('dp', 'mp'))
- gainone_grad: float32 [768], replicated
- shiftone_grad: float32 [768], replicated
- tokenin_grad: float32 [196, 384], P(None, 'mp')
- tokenbias_grad: float32 [384], P('mp')
- tokenout_grad: float32 [384, 196], P('mp')
- tokenshift_grad: float32 [196], replicated
- gaintwo_grad: float32 [768], replicated
- shifttwo_grad: float32 [768], replicated
- channelin_grad: float32 [768, 3072], P(None, 'mp')
- channelbias_grad: float32 [3072], P('mp')
- channelout_grad: float32 [3072, 768], P('mp')
- channelshift_grad: float32 [768], replicated
The draws below stay inside these ranges and needn't reach their ends.
All inputs are finite; a program needn't handle non-finite values.
Results may differ from the reference program's by a relative error of at most 0.015.
Values may be sent and summed in bfloat16 or wider, within the bound.
A program may use at most 192 MiB of HBM per device.

```python
import math
import jax
import jax.numpy as jnp
from jax import lax

D = 768
PATCH = 196
HT = 384
HC = 3072
IMG_DEV = 6
IMAGES = 192


def draw_cotangent(key, part):
    key = jax.random.fold_in(key, 11)
    first, second = jax.random.split(key)
    ramp = jnp.arange(IMAGES, dtype=jnp.float32) / max(IMAGES - 1, 1)
    noise = jnp.clip(jax.random.normal(first, (IMAGES, PATCH, D), jnp.float32), -6.0, 6.0)
    rough = jax.random.uniform(second, (IMAGES, PATCH, 1), jnp.float32, 0.7, 1.4)
    growth = 3.0 ** ramp
    return (noise * rough * growth[:, None, None]).astype(jnp.bfloat16)


def block_scale(rng, dims, pieces, low, high):
    level = 1.0
    for position, blocks in pieces:
        draws = jax.random.uniform(jax.random.fold_in(jax.random.fold_in(rng, 6), position), (blocks,), jnp.float32, low / len(pieces), high / len(pieces))
        level = level * jnp.repeat(jnp.exp(draws), dims[position] // blocks).reshape((-1,) + (1,) * (len(dims) - 1 - position))
    return level


def normal_values(rng, shape, scale, reach, pieces=(), kind=jnp.bfloat16):
    loudness = block_scale(rng, shape, pieces, -0.22, 0.18) if pieces else 1.0
    entries = jax.random.normal(rng, shape, jnp.float32) * scale * loudness
    return jnp.minimum(jnp.maximum(entries, -reach), reach).astype(kind)


def setup_inputs(seed: int = 0) -> dict:
    streams_of = jax.random.split(jax.random.key(seed), 15)
    return {
        "patches": normal_values(streams_of[0], (IMAGES, PATCH, D), 1.0, 6.0, ((0, 32),)),
        "cotangent": draw_cotangent(jax.random.fold_in(streams_of[14], 71), 0),
        "gain_one": jnp.clip(jnp.exp(jax.random.uniform(streams_of[2], (D,), jnp.float32, math.log(0.5), math.log(2.0))), 0.5, 2.0),
        "shift_one": normal_values(streams_of[3], (D,), 0.5, 3.0, (), jnp.float32),
        "token_in": normal_values(streams_of[4], (PATCH, HT), PATCH ** -0.5, 0.4375, ((1, 2),)),
        "token_bias": normal_values(streams_of[5], (HT,), 0.5, 3.0, ((0, 2),), jnp.float32),
        "token_out": normal_values(streams_of[6], (HT, PATCH), (HT // 2) ** -0.5, 0.4375, ((0, 2),)),
        "token_shift": normal_values(streams_of[7], (PATCH,), 0.5, 3.0, (), jnp.float32),
        "gain_two": jnp.clip(jnp.exp(jax.random.uniform(streams_of[8], (D,), jnp.float32, math.log(0.5), math.log(2.0))), 0.5, 2.0),
        "shift_two": normal_values(streams_of[9], (D,), 0.5, 3.0, (), jnp.float32),
        "channel_in": normal_values(streams_of[10], (D, HC), D ** -0.5, 0.21875, ((1, 2),)),
        "channel_bias": normal_values(streams_of[11], (HC,), 0.5, 3.0, ((0, 2),), jnp.float32),
        "channel_out": normal_values(streams_of[12], (HC, D), (HC // 2) ** -0.5, 0.15625, ((0, 2),)),
        "channel_shift": normal_values(streams_of[13], (D,), 0.5, 3.0, (), jnp.float32),
    }


@jax.custom_vjp
def low(v):
    return lax.optimization_barrier(v.astype(jnp.bfloat16)).astype(jnp.float32)

@jax.custom_vjp
def low_back(v):
    return v

def low_keep(v):
    return (low(v), None)

def low_pass(kept, grad):
    return (grad,)

def back_keep(v):
    return (v, None)

def back_low(kept, grad):
    return (low(grad),)
low.defvjp(low_keep, low_pass)
low_back.defvjp(back_keep, back_low)
highest = lax.Precision.HIGHEST

def normalize(values, gain, shift):
    centred = values - lax.optimization_barrier(jnp.mean(values, -1, keepdims=True))
    scale = lax.rsqrt(lax.optimization_barrier(jnp.mean(centred * centred, -1, keepdims=True)) + 1e-06)
    return centred * scale * gain + shift

def smooth(values):
    return jax.nn.gelu(values, approximate=False)

def forward(inputs, gain_one, shift_one, token_in, token_bias, token_out, token_shift, gain_two, shift_two, channel_in, channel_bias, channel_out, channel_shift):
    first = low(normalize(inputs, gain_one, shift_one))
    token_pre = low_back(jnp.einsum('bsd,sh->bhd', first, token_in, precision=highest) + token_bias[None, :, None])
    token_hidden = low(smooth(token_pre))
    token_branch = low_back(jnp.einsum('bhd,hs->bsd', token_hidden, token_out, precision=highest) + token_shift[None, :, None])
    middle = inputs + token_branch
    second = low(normalize(middle, gain_two, shift_two))
    channel_pre = low_back(jnp.einsum('bsd,dh->bsh', second, channel_in, precision=highest) + channel_bias)
    channel_hidden = low(smooth(channel_pre))
    channel_branch = low_back(jnp.einsum('bsh,hd->bsd', channel_hidden, channel_out, precision=highest) + channel_shift)
    return middle + channel_branch

def reference(patches, cotangent, gain_one, shift_one, token_in, token_bias, token_out, token_shift, gain_two, shift_two, channel_in, channel_bias, channel_out, channel_shift):
    params = tuple((p.astype(jnp.float32) for p in (gain_one, shift_one, token_in, token_bias, token_out, token_shift, gain_two, shift_two, channel_in, channel_bias, channel_out, channel_shift)))
    blocks = IMAGES // IMG_DEV
    inputs = patches.astype(jnp.float32).reshape(blocks, IMG_DEV, PATCH, D)
    grads_out = cotangent.astype(jnp.float32).reshape(blocks, IMG_DEV, PATCH, D)

    def step(total, item):
        block_in, block_cot = item
        result, pull = jax.vjp(forward, block_in, *params)
        grads = pull(block_cot)
        summed = tuple((t + g for t, g in zip(total, grads[1:])))
        return (summed, (result.astype(jnp.bfloat16), grads[0]))
    start = tuple((jnp.zeros_like(p) for p in params))
    total, (results, input_grads) = lax.scan(step, start, (inputs, grads_out))
    return (results.reshape(IMAGES, PATCH, D), input_grads.reshape(IMAGES, PATCH, D), total[0], total[1], total[2], total[3], total[4], total[5], total[6], total[7], total[8], total[9], total[10], total[11])
```

```python
import functools

import jax
import jax.numpy as jnp
from jax import lax
from jax.experimental import pallas as pl
from jax.experimental.pallas import tpu as pltpu
from jax.sharding import PartitionSpec as P

MESH = pl.DeviceIdType.MESH
F32 = jnp.float32
BF16 = jnp.bfloat16
NT = (((1,), (1,)), ((), ()))
LANES = 128
NUM, DEN = 7, 4
OFFSETS = (5, 8, 10, 12, 14, 15)


def dot(a, b):
    return jnp.dot(a, b, preferred_element_type=F32)


def dot_nt(a, b):
    return lax.dot_general(a, b, NT, preferred_element_type=F32)


def centre(values):
    centred = values - jnp.mean(values, -1, keepdims=True)
    return centred, lax.rsqrt(jnp.mean(centred * centred, -1, keepdims=True) + 1e-06)


def norm_back(grad, normed, scale, gain):
    scaled = grad * gain
    return scale * (
        scaled
        - jnp.mean(scaled, -1, keepdims=True)
        - normed * jnp.mean(scaled * normed, -1, keepdims=True)
    )


def gelu_parts(v):
    phi = 0.5 + 0.5 * lax.erf(v * 0.7071067811865476)
    return phi, phi + v * (0.3989422804014327 * jnp.exp(-0.5 * v * v))


def layer(
    sizes,
    patches, cotangent, gain_one, shift_one, token_in, token_bias, token_out, token_shift,
    gain_two, shift_two, channel_in, channel_bias, channel_out, channel_shift,
    mixed, keep, summed, hid_out, slope_out,
    wi, wo, cbo, twi, two, twi_t, two_t,
    dys, dys_t, u2s, u2s_t, u1s, chid, dcp, dtok,
    xs, ms, hid, slope, stats,
    row_acc, cb_acc, ts_acc, tin_acc, tout_acc, small,
    grads, from_core, own, oth, from_mp, from_x, from_z, from_far,
    load_sem, stage_sem, tok_s, tok_r, w_s, w_r, c_s, c_r, y_s, y_r, x_s, x_r, z_s, z_r,
    a_s, a_r, l_sem, xa_s, xa_r, ca_s, ca_r, far_s, far_r,
):
    images, patch, width, token_half, hidden_half, ticks, dp_size = sizes
    rows = dys.shape[0]
    high = u1s.shape[1]
    step = hidden_half // ticks
    chunks = 2 * ticks
    all_chunks = chunks + 1
    eighth_in, eighth_out = width // 8, step // 8
    half, piece = width // 2, width // 8

    dp = lax.axis_index("dp")
    mp = lax.axis_index("mp")
    core = lax.rem(dp, 2)
    side = lax.rem(lax.div(dp, 2), 2)
    near = lax.rem(lax.div(dp, 2), 4)
    line = lax.rem(lax.div(dp, 4), 4)
    part = core * 4 + near

    to_mp = {"mp": 1 - mp}
    to_core = {"dp": dp + 1 - 2 * core}
    to_side = {"dp": dp + 2 - 4 * side}

    def near_of(r):
        return {"dp": dp + 2 * (lax.rem(near + r, 4) - near)}

    def line_of(r):
        return {"dp": dp + 4 * (lax.rem(line + r, 4) - line)}

    far_bits = []
    bit = 16
    while bit < dp_size:
        far_bits.append(bit)
        bit *= 2

    def far_of(i):
        b = far_bits[i]
        return {"dp": dp + b - 2 * b * lax.rem(lax.div(dp, b), 2)}

    def remote(src, dst, send, recv, device):
        return pltpu.make_async_remote_copy(
            src_ref=src, dst_ref=dst, send_sem=send, recv_sem=recv, device_id=device, device_id_type=MESH
        )

    def al(v, m):
        return pl.multiple_of(v, m)

    def own_loads(t):
        return (
            pltpu.make_async_copy(
                channel_in.at[:, pl.ds(al(t * step, step), step)],
                wi.at[:, pl.ds(al(t * 2 * step, step), step)],
                load_sem.at[t, 0],
            ),
            pltpu.make_async_copy(
                channel_out.at[pl.ds(al(t * step, step), step), :],
                wo.at[pl.ds(al(t * 2 * step, step), step), :],
                load_sem.at[t, 1],
            ),
        )

    def other_in(t, first, count):
        return wi.at[pl.ds(al(first, eighth_in), count), pl.ds(al(t * 2 * step + step, step), step)]

    def other_out(t, first, count):
        return wo.at[pl.ds(al(t * 2 * step + step + first, eighth_out), count), :]

    def gather_mp(t):
        return (
            remote(
                channel_in.at[pl.ds(al(part * eighth_in, eighth_in), eighth_in), pl.ds(al(t * step, step), step)],
                other_in(t, part * eighth_in, eighth_in),
                w_s.at[0, t, 0], w_r.at[0, t, 0], to_mp,
            ),
            remote(
                channel_out.at[pl.ds(al(t * step + part * eighth_out, eighth_out), eighth_out), :],
                other_out(t, part * eighth_out, eighth_out),
                w_s.at[0, t, 1], w_r.at[0, t, 1], to_mp,
            ),
        )

    def gather_near(t):
        copies = []
        for r in (1, 2, 3):
            a = other_in(t, part * eighth_in, eighth_in)
            b = other_out(t, part * eighth_out, eighth_out)
            copies.append(remote(a, a, w_s.at[r, t, 0], w_r.at[r, t, 0], near_of(r)))
            copies.append(remote(b, b, w_s.at[r, t, 1], w_r.at[r, t, 1], near_of(r)))
        return copies

    def gather_core(t):
        a = other_in(t, core * 4 * eighth_in, 4 * eighth_in)
        b = other_out(t, core * 4 * eighth_out, 4 * eighth_out)
        return (
            remote(a, a, w_s.at[4, t, 0], w_r.at[4, t, 0], to_core),
            remote(b, b, w_s.at[4, t, 1], w_r.at[4, t, 1], to_core),
        )

    def token_sends():
        return (
            remote(twi.at[pl.ds(0, token_half)], twi.at[pl.ds(token_half, token_half)], tok_s.at[0], tok_r.at[0], to_mp),
            remote(two.at[pl.ds(0, token_half)], two.at[pl.ds(token_half, token_half)], tok_s.at[1], tok_r.at[1], to_mp),
            remote(channel_bias, cbo, tok_s.at[2], tok_r.at[2], to_mp),
        )

    def core_copy(c):
        slot, q = lax.rem(lax.div(c, 2), 2), lax.rem(c, 2)
        return remote(grads.at[slot, 1 - core, q], from_core.at[slot, q], c_s.at[c], c_r.at[c], to_core)

    def mp_copy(c):
        return remote(oth.at[c], from_mp.at[c], y_s.at[c], y_r.at[c], to_mp)

    def side_copy(c):
        return remote(own.at[c, pl.ds(al((1 - side) * half, half), half)], from_x.at[c], x_s.at[c], x_r.at[c], to_side)

    def mine(c):
        return own.at[c, pl.ds(al(side * half + line * piece, piece), piece)]

    def my_sum(c):
        return summed.at[core, c, pl.ds(al(side * half + line * piece, piece), piece)]

    def line_copies(c):
        return [
            remote(
                own.at[c, pl.ds(al(side * half + lax.rem(line + r, 4) * piece, piece), piece)],
                from_z.at[c, r - 1], z_s.at[c, r - 1], z_r.at[c, r - 1], line_of(r),
            )
            for r in (1, 2, 3)
        ]

    def keep_copy(c):
        return pltpu.make_async_copy(mine(c), my_sum(c), l_sem.at[c])

    def spread_copies(c):
        return [
            remote(mine(c), my_sum(c), a_s.at[c, r - 1], a_r.at[c, r - 1], line_of(r)) for r in (1, 2, 3)
        ]

    def side_spread(c):
        ref = summed.at[core, c, pl.ds(al(side * half, half), half)]
        return remote(ref, ref, xa_s.at[c], xa_r.at[c], to_side)

    def core_spread(c):
        ref = summed.at[core, c]
        return remote(ref, ref, ca_s.at[c], ca_r.at[c], to_core)

    def add(a, b):
        return (a.astype(F32) + b.astype(F32)).astype(BF16)

    def after_core(c):
        core_copy(c).wait()
        slot, q = lax.rem(lax.div(c, 2), 2), lax.rem(c, 2)
        oth[c] = add(grads[slot, core, q, 1], from_core[slot, q, 1])
        mp_copy(c).start()
        own[c] = add(grads[slot, core, q, 0], from_core[slot, q, 0])

    def after_mp(c):
        mp_copy(c).wait()
        own[c] = add(own[c], from_mp[c])
        side_copy(c).start()

    def after_side(c):
        side_copy(c).wait()
        rng = pl.ds(al(side * half, half), half)
        own[c, rng] = add(own[c, rng], from_x[c])
        for copy in line_copies(c):
            copy.start()

    def after_line(c):
        for copy in line_copies(c):
            copy.wait()
        rng = pl.ds(al(side * half + line * piece, piece), piece)
        total = own[c, rng].astype(F32)
        for r in range(3):
            total = total + from_z[c, r].astype(F32)
        own[c, rng] = total.astype(BF16)
        for i in range(len(far_bits)):
            copy = remote(mine(c), from_far.at[c, i], far_s.at[c, i], far_r.at[c, i], far_of(i))
            copy.start()
            copy.wait()
            own[c, rng] = add(own[c, rng], from_far[c, i])
        keep_copy(c).start()
        for copy in spread_copies(c):
            copy.start()

    def after_spread(c):
        keep_copy(c).wait()
        for copy in spread_copies(c):
            copy.wait()
        side_spread(c).start()

    def after_side_spread(c):
        side_spread(c).wait()
        core_spread(c).start()

    def after_core_spread(c):
        core_spread(c).wait()

    stages = (after_mp, after_side, after_line, after_spread, after_side_spread, after_core_spread)

    def point(p, with_core):
        if with_core:
            c = p - 2

            @pl.when(jnp.logical_and(c >= 0, c < chunks))
            def _():
                after_core(c)

        for offset, stage in zip(OFFSETS, stages):
            k = p - offset
            c = lax.div(DEN * k + DEN - 1, NUM)
            hit = jnp.logical_and(lax.div(NUM * c, DEN) == k, jnp.logical_and(k >= 0, c < all_chunks))

            @pl.when(hit)
            def _(c=c, stage=stage):
                stage(c)

    barrier = pltpu.get_barrier_semaphore()
    greet = [to_mp, to_core] + [near_of(r) for r in (1, 2, 3)] + [line_of(r) for r in (1, 2, 3)]
    greet += [far_of(i) for i in range(len(far_bits))]
    for device in greet:
        pl.semaphore_signal(barrier, inc=1, device_id=device, device_id_type=MESH)

    def patch_copy(b):
        return pltpu.make_async_copy(patches.at[b], xs.at[lax.rem(b, 2)], stage_sem.at[0, lax.rem(b, 2)])

    def cot_copy(b):
        return pltpu.make_async_copy(cotangent.at[b], ms.at[lax.rem(b, 2)], stage_sem.at[1, lax.rem(b, 2)])

    def hid_save(b):
        s = lax.rem(b, 2)
        return (
            pltpu.make_async_copy(hid.at[s], hid_out.at[b], stage_sem.at[2, s]),
            pltpu.make_async_copy(slope.at[s], slope_out.at[b], stage_sem.at[3, s]),
        )

    def hid_load(b):
        s = lax.rem(b, 2)
        return (
            pltpu.make_async_copy(hid_out.at[b], hid.at[s], stage_sem.at[2, s]),
            pltpu.make_async_copy(slope_out.at[b], slope.at[s], stage_sem.at[3, s]),
        )

    def mixed_save(b):
        s = lax.rem(b, 2)
        return pltpu.make_async_copy(ms.at[s], mixed.at[b], stage_sem.at[4, s])

    def both(copies, what):
        for copy in copies:
            getattr(copy, what)()

    for b in (0, 1):
        cot_copy(b).start()
        patch_copy(b).start()

    def start_own(t, _):
        both(own_loads(t), "start")
        return 0

    lax.fori_loop(0, ticks, start_own, 0)

    wide = twi.shape[1]
    bias = token_bias[...]
    bias_hi = bias.astype(BF16)
    rest = bias - bias_hi.astype(F32)
    bias_mid = rest.astype(BF16)
    bias_lo = (rest - bias_mid.astype(F32)).astype(BF16)
    zero_half = jnp.zeros((token_half, wide), BF16)
    twi[pl.ds(0, token_half), :] = zero_half
    two[pl.ds(0, token_half), :] = zero_half
    twi[pl.ds(0, token_half), pl.ds(0, patch)] = token_in[...].T
    two[pl.ds(0, token_half), pl.ds(0, patch)] = token_out[...]
    lane = lax.broadcasted_iota(jnp.int32, (token_half, wide), 1)
    filled = twi[pl.ds(0, token_half), :].astype(F32)
    filled = jnp.where(lane == patch, bias_hi.astype(F32), filled)
    filled = jnp.where(lane == patch + 1, bias_mid.astype(F32), filled)
    filled = jnp.where(lane == patch + 2, bias_lo.astype(F32), filled)
    twi[pl.ds(0, token_half), :] = filled.astype(BF16)

    pl.semaphore_wait(barrier, len(greet))
    both(token_sends(), "start")

    def start_mp(t, _):
        both(gather_mp(t), "start")
        return 0

    lax.fori_loop(0, ticks, start_mp, 0)

    dys[...] = jnp.zeros_like(dys)
    u2s[...] = jnp.zeros_like(u2s)
    dtok[...] = jnp.zeros_like(dtok)
    rest_rows = rows - images * high
    if rest_rows:
        chid[pl.ds(images * high, rest_rows), :] = jnp.zeros((rest_rows, chid.shape[1]), BF16)
        dcp[pl.ds(images * high, rest_rows), :] = jnp.zeros((rest_rows, dcp.shape[1]), BF16)
    row_acc[...] = jnp.zeros_like(row_acc)
    ts_acc[...] = jnp.zeros_like(ts_acc)
    tin_acc[...] = jnp.zeros_like(tin_acc)
    tout_acc[...] = jnp.zeros_like(tout_acc)
    small[...] = jnp.zeros_like(small)
    u2s_t[pl.ds(width, 16), :] = jnp.ones((16, rows), BF16)

    below = lax.broadcasted_iota(jnp.int32, (high, width), 0)
    ones = jnp.where(jnp.logical_and(below >= patch, below < patch + 3), 1.0, 0.0).astype(BF16)
    for b in range(images):
        u1s[b] = ones

    def take_cot(b, _):
        s = lax.rem(b, 2)
        cot_copy(b).wait()
        value = ms[s]
        dys[pl.ds(al(b * high, 16), patch), :] = value
        row_acc[pl.ds(4, 1), :] += jnp.sum(value.astype(F32), 0, keepdims=True)

        @pl.when(b + 2 < images)
        def _():
            cot_copy(b + 2).start()

        return 0

    lax.fori_loop(0, images, take_cot, 0)

    def turn_dy(j, _):
        at = pl.ds(al(j * LANES, LANES), LANES)
        dys_t[:, at] = dys[at, :].T
        return 0

    lax.fori_loop(0, rows // LANES, turn_dy, 0)

    both(token_sends(), "wait")
    twi_t[...] = twi[...].T
    two_t[...] = two[...].T

    def token_forward(b, _):
        s = lax.rem(b, 2)
        patch_copy(b).wait()
        x = xs[s].astype(F32)

        @pl.when(b + 2 < images)
        def _():
            patch_copy(b + 2).start()

        mean = jnp.mean(x, -1, keepdims=True)
        centred = x - mean
        scale = lax.rsqrt(jnp.mean(centred * centred, -1, keepdims=True) + 1e-06)
        stats[b, :, 0:1] = mean
        stats[b, :, 1:2] = scale
        u1s[b, pl.ds(0, patch), :] = (centred * scale * gain_one[...] + shift_one[...]).astype(BF16)
        pre = dot(twi[:, pl.ds(0, high)], u1s[b])
        phi, deriv = gelu_parts(pre)

        @pl.when(b >= 2)
        def _():
            both(hid_save(b - 2), "wait")

        hidden = (pre * phi).astype(BF16)
        hid[s] = hidden
        slope[s] = deriv.astype(BF16)
        both(hid_save(b), "start")
        tok = dot(two_t[pl.ds(0, high), :], hidden)
        x1 = x + tok[:patch] + token_shift[...]
        keep[b] = x1
        mean = jnp.mean(x1, -1, keepdims=True)
        centred = x1 - mean
        scale = lax.rsqrt(jnp.mean(centred * centred, -1, keepdims=True) + 1e-06)
        stats[b, :, 2:3] = mean
        stats[b, :, 3:4] = scale
        u2s[pl.ds(al(b * high, 16), patch), :] = (centred * scale * gain_two[...] + shift_two[...]).astype(BF16)

        @pl.when(b < ticks)
        def _():
            both(gather_mp(b), "wait")
            both(gather_near(b), "start")

        return 0

    lax.fori_loop(0, images, token_forward, 0)
    for t in range(images, ticks):
        both(gather_mp(t), "wait")
        both(gather_near(t), "start")
    both(gather_near(0), "wait")
    both(gather_core(0), "start")

    def turn_u2(j, _):
        at = pl.ds(al(j * LANES, LANES), LANES)
        u2s_t[pl.ds(0, width), at] = u2s[at, :].T
        return 0

    lax.fori_loop(0, rows // LANES, turn_u2, 0)
    for b in range(max(images - 2, 0), images):
        both(hid_save(b), "wait")

    live = images * high
    tiles = 2 if live % 32 == 0 else 1
    tall = live // tiles

    def channel(t, _):
        both(own_loads(t), "wait")
        both(gather_core(t), "wait")
        at = pl.ds(al(t * 2 * step, 2 * step), 2 * step)
        weight_in, weight_out = wi[:, at], wo[at, :]
        here = pl.ds(al(t * step, step), step)
        bias = jnp.concatenate([channel_bias[:, here], cbo[:, here]], axis=1)
        for i in range(tiles):
            rng = pl.ds(i * tall, tall)
            pre = dot(u2s[rng, :], weight_in) + bias
            back = dot_nt(dys[rng, :], weight_out)
            phi, deriv = gelu_parts(pre)
            chid[rng, at] = (pre * phi).astype(BF16)
            dcp[rng, at] = (back * deriv).astype(BF16)

        @pl.when(t + 1 < ticks)
        def _():
            both(gather_near(t + 1), "wait")
            both(gather_core(t + 1), "start")

        point(2 * t, True)
        slot = lax.rem(t, 2)
        grad_in = dot(u2s_t[...], dcp[:, at])
        cb_acc[:, at] = grad_in[width : width + 1]
        grad_in = grad_in[:width].astype(BF16)
        grad_out = dot(dys_t[...], chid[:, at]).astype(BF16)
        for m, value in ((0, grad_in), (1, grad_out)):
            for o in (0, 1):
                for q in (0, 1):
                    first = o * step + q * LANES
                    grads[slot, m, q, o] = value[:, first : first + LANES]
        point(2 * t + 1, True)
        core_copy(2 * t).start()
        core_copy(2 * t + 1).start()
        return 0

    lax.fori_loop(0, ticks, channel, 0)

    both(hid_load(0), "start")
    patch_copy(0).start()
    ones16 = jnp.ones((16, width), BF16)

    def backward(b, _):
        s = lax.rem(b, 2)
        rng = pl.ds(al(b * high, 16), high)

        @pl.when(b + 1 < images)
        def _():
            both(hid_load(b + 1), "start")
            patch_copy(b + 1).start()

        @pl.when(b >= 2)
        def _():
            mixed_save(b - 2).wait()

        x1 = keep[b]
        ms[s] = (x1 + dot(chid[rng, :], wo[...])[:patch] + channel_shift[...]).astype(BF16)
        mixed_save(b).start()
        du2 = dot_nt(dcp[rng, :], wi[...])[:patch]
        n2 = (x1 - stats[b, :, 2:3]) * stats[b, :, 3:4]
        row_acc[pl.ds(2, 1), :] += jnp.sum(du2 * n2, 0, keepdims=True)
        row_acc[pl.ds(3, 1), :] += jnp.sum(du2, 0, keepdims=True)
        dy = dys[pl.ds(al(b * high, 16), patch), :].astype(F32)
        dx1 = dy + norm_back(du2, n2, stats[b, :, 3:4], gain_two[...])
        keep[b] = dx1
        dtok[pl.ds(0, patch), :] = dx1.astype(BF16)
        point(chunks + 2 * b, True)
        both(hid_load(b), "wait")
        dtk = dtok[...]
        hidden = hid[s]
        tout_acc[:, pl.ds(0, high)] += dot_nt(hidden, dtk)
        ts_acc[:, pl.ds(0, high)] += dot_nt(ones16, dtk)
        dpre = (dot(two[:, pl.ds(0, high)], dtk) * slope[s].astype(F32)).astype(BF16)
        tin_acc[:, pl.ds(0, high)] += dot_nt(dpre, u1s[b])
        du1 = dot(twi_t[pl.ds(0, high), :], dpre)[:patch]
        patch_copy(b).wait()
        n1 = (xs[s].astype(F32) - stats[b, :, 0:1]) * stats[b, :, 1:2]
        row_acc[pl.ds(0, 1), :] += jnp.sum(du1 * n1, 0, keepdims=True)
        row_acc[pl.ds(1, 1), :] += jnp.sum(du1, 0, keepdims=True)
        keep[b] = keep[b] + norm_back(du1, n1, stats[b, :, 1:2], gain_one[...])
        point(chunks + 2 * b + 1, True)
        return 0

    lax.fori_loop(0, images, backward, 0)

    blocks = width // LANES
    for o in (0, 1):
        for v in range(5):
            for j in range(blocks):
                small[o, pl.ds(v * blocks + j, 1), :] = row_acc[pl.ds(v, 1), pl.ds(j * LANES, LANES)]
        for j in range(2):
            small[o, pl.ds(5 * blocks + j, 1), :] = ts_acc[pl.ds(0, 1), pl.ds(j * LANES, LANES)]
        for c in range(chunks):
            first = (c // 2) * 2 * step + o * step + (c % 2) * LANES
            small[o, pl.ds(5 * blocks + 2 + c, 1), :] = cb_acc[pl.ds(0, 1), pl.ds(first, LANES)]
    last_slot = ticks % 2
    for o in (0, 1):
        for m, acc in ((0, tin_acc), (1, tout_acc)):
            for j in range(2):
                grads[last_slot, m, 0, o, pl.ds(j * token_half, token_half), :] = acc[
                    pl.ds(o * token_half, token_half), pl.ds(j * LANES, LANES)
                ].astype(BF16)
        grads[last_slot, 0, 0, o, pl.ds(2 * token_half, small.shape[1]), :] = small[o].astype(BF16)
    core_copy(chunks).start()
    after_core(chunks)

    def drain(p, _):
        point(p, False)
        return 0

    first = chunks + 2 * images
    lax.fori_loop(first, OFFSETS[-1] + (NUM * chunks) // DEN + 1, drain, 0)
    for b in range(max(images - 2, 0), images):
        mixed_save(b).wait()


def widen(sizes, chunk, last, d_in, d_out, d_tin, d_tbias, d_tout, d_tshift, d_rows, d_cbias):
    patch, width, token_half, chunks = sizes
    d_in[...] = chunk[0, 0].astype(F32)
    d_out[...] = chunk[1, 0].astype(F32).T

    @pl.when(pl.program_id(0) == 0)
    def _():
        both = [
            jnp.concatenate(
                [last[m, 0, pl.ds(0, token_half), :], last[m, 0, pl.ds(token_half, token_half), :]], axis=1
            ).astype(F32)
            for m in (0, 1)
        ]
        turned = both[0].T
        d_tin[...] = turned[:patch]
        d_tbias[...] = turned[patch : patch + 1]
        d_tout[...] = both[1][:, :patch]
        blocks = width // LANES
        rows = last[0, 0, pl.ds(2 * token_half, 64), :].astype(F32)
        for v in range(5):
            for j in range(blocks):
                i = v * blocks + j
                d_rows[pl.ds(v, 1), pl.ds(j * LANES, LANES)] = rows[i : i + 1]
        i = 5 * blocks
        d_tshift[...] = jnp.concatenate([rows[i : i + 1], rows[i + 1 : i + 2]], axis=1)[:, :patch]
        for c in range(chunks):
            i = 5 * blocks + 2 + c
            d_cbias[pl.ds(0, 1), pl.ds(c * LANES, LANES)] = rows[i : i + 1]


def per_device(
    dp_size,
    patches, cotangent, gain_one, shift_one, token_in, token_bias, token_out, token_shift,
    gain_two, shift_two, channel_in, channel_bias, channel_out, channel_shift,
):
    images, patch, width = patches.shape
    token_half = token_in.shape[1]
    hidden_half = channel_in.shape[1]
    step = 2 * LANES
    ticks = hidden_half // step
    chunks = 2 * ticks
    high = -(-(patch + 3) // 16) * 16
    rows = -(-images * high // LANES) * LANES
    wide = -(-patch // LANES) * LANES
    tokens = 2 * token_half
    far = max(sum(1 for b in range(4, 20) if 2**b < dp_size), 1)
    far_chunks = chunks + 1 if dp_size > 16 else 1
    sizes = (images, patch, width, token_half, hidden_half, ticks, dp_size)
    vmem = pl.BlockSpec(memory_space=pltpu.VMEM)
    hbm = pl.BlockSpec(memory_space=pl.ANY)
    n = chunks + 1
    dma = pltpu.SemaphoreType.DMA
    mixed, inputs_grad, summed, _, _ = pl.pallas_call(
        functools.partial(layer, sizes),
        out_shape=(
            jax.ShapeDtypeStruct((images, patch, width), BF16),
            jax.ShapeDtypeStruct((images, patch, width), F32),
            jax.ShapeDtypeStruct((2, n, width, LANES), BF16),
            jax.ShapeDtypeStruct((images, tokens, width), BF16),
            jax.ShapeDtypeStruct((images, tokens, width), BF16),
        ),
        in_specs=[hbm, hbm, vmem, vmem, vmem, vmem, vmem, vmem, vmem, vmem, hbm, vmem, hbm, vmem],
        out_specs=(hbm, vmem, hbm, hbm, hbm),
        scratch_shapes=[
            pltpu.VMEM((width, 2 * hidden_half), BF16),
            pltpu.VMEM((2 * hidden_half, width), BF16),
            pltpu.VMEM((1, hidden_half), F32),
            pltpu.VMEM((tokens, wide), BF16),
            pltpu.VMEM((tokens, wide), BF16),
            pltpu.VMEM((wide, tokens), BF16),
            pltpu.VMEM((wide, tokens), BF16),
            pltpu.VMEM((rows, width), BF16),
            pltpu.VMEM((width, rows), BF16),
            pltpu.VMEM((rows, width), BF16),
            pltpu.VMEM((width + 16, rows), BF16),
            pltpu.VMEM((images, high, width), BF16),
            pltpu.VMEM((rows, 2 * hidden_half), BF16),
            pltpu.VMEM((rows, 2 * hidden_half), BF16),
            pltpu.VMEM((high, width), BF16),
            pltpu.VMEM((2, patch, width), BF16),
            pltpu.VMEM((2, patch, width), BF16),
            pltpu.VMEM((2, tokens, width), BF16),
            pltpu.VMEM((2, tokens, width), BF16),
            pltpu.VMEM((images, patch, 4), F32),
            pltpu.VMEM((8, width), F32),
            pltpu.VMEM((1, 2 * hidden_half), F32),
            pltpu.VMEM((16, wide), F32),
            pltpu.VMEM((tokens, wide), F32),
            pltpu.VMEM((tokens, wide), F32),
            pltpu.VMEM((2, 64, LANES), F32),
            pltpu.VMEM((2, 2, 2, 2, width, LANES), BF16),
            pltpu.VMEM((2, 2, 2, width, LANES), BF16),
            pltpu.VMEM((n, width, LANES), BF16),
            pltpu.VMEM((n, width, LANES), BF16),
            pltpu.VMEM((n, width, LANES), BF16),
            pltpu.VMEM((n, width // 2, LANES), BF16),
            pltpu.VMEM((n, 3, width // 8, LANES), BF16),
            pltpu.VMEM((far_chunks, far, width // 8, LANES), BF16),
            dma((ticks, 2)),
            dma((5, 2)),
            dma((3,)), dma((3,)),
            dma((5, ticks, 2)), dma((5, ticks, 2)),
            dma((n,)), dma((n,)),
            dma((n,)), dma((n,)),
            dma((n,)), dma((n,)),
            dma((n, 3)), dma((n, 3)),
            dma((n, 3)), dma((n, 3)),
            dma((n,)),
            dma((n,)), dma((n,)),
            dma((n,)), dma((n,)),
            dma((far_chunks, far)), dma((far_chunks, far)),
        ],
        compiler_params=pltpu.CompilerParams(
            collective_id=0, has_side_effects=True, vmem_limit_bytes=63 * 2**20
        ),
        name="mixer_layer",
    )(
        patches, cotangent, gain_one.reshape(1, -1), shift_one.reshape(1, -1), token_in,
        token_bias.reshape(-1, 1), token_out, token_shift.reshape(-1, 1), gain_two.reshape(1, -1),
        shift_two.reshape(1, -1), channel_in, channel_bias.reshape(1, -1), channel_out,
        channel_shift.reshape(1, -1),
    )

    def whole(*shape):
        return pl.BlockSpec(shape, lambda c: (0,) * len(shape))

    d_in, d_out, d_tin, d_tbias, d_tout, d_tshift, d_rows, d_cbias = pl.pallas_call(
        functools.partial(widen, (patch, width, token_half, chunks)),
        grid=(chunks,),
        in_specs=[
            pl.BlockSpec((2, 1, width, LANES), lambda c: (0, c, 0, 0)),
            pl.BlockSpec((2, 1, width, LANES), lambda c: (0, chunks, 0, 0)),
        ],
        out_specs=(
            pl.BlockSpec((width, LANES), lambda c: (0, c)),
            pl.BlockSpec((LANES, width), lambda c: (c, 0)),
            whole(patch, token_half), whole(1, token_half), whole(token_half, patch), whole(1, patch),
            whole(8, width), whole(1, hidden_half),
        ),
        out_shape=(
            jax.ShapeDtypeStruct((width, hidden_half), F32),
            jax.ShapeDtypeStruct((hidden_half, width), F32),
            jax.ShapeDtypeStruct((patch, token_half), F32),
            jax.ShapeDtypeStruct((1, token_half), F32),
            jax.ShapeDtypeStruct((token_half, patch), F32),
            jax.ShapeDtypeStruct((1, patch), F32),
            jax.ShapeDtypeStruct((8, width), F32),
            jax.ShapeDtypeStruct((1, hidden_half), F32),
        ),
        compiler_params=pltpu.CompilerParams(vmem_limit_bytes=32 * 2**20),
        name="widen",
    )(summed, summed)
    return (
        mixed, inputs_grad, d_rows[0], d_rows[1], d_tin, d_tbias[0], d_tout, d_tshift[0],
        d_rows[2], d_rows[3], d_in, d_cbias[0], d_out, d_rows[4],
    )


def solution(mesh):
    split = P(("dp", "mp"), None, None)
    columns, rows, vector = P(None, "mp"), P("mp", None), P("mp")
    return jax.shard_map(
        functools.partial(per_device, mesh.shape["dp"]),
        mesh=mesh,
        in_specs=(
            split, split, P(), P(), columns, vector, rows, P(), P(), P(), columns, vector, rows, P(),
        ),
        out_specs=(
            split, split, P(), P(), columns, vector, rows, P(), P(), P(), columns, vector, rows, P(),
        ),
        check_vma=False,
    )
```

```python
import functools

import jax
import jax.numpy as jnp
from jax import lax
from jax.experimental import pallas as pl
from jax.experimental.pallas import tpu as pltpu
from jax.sharding import PartitionSpec as P

MESH = pl.DeviceIdType.MESH
F32 = jnp.float32
BF16 = jnp.bfloat16
NT = (((1,), (1,)), ((), ()))
LANES = 128
RING = 4

STRAIGHT = (0, 2, 3, 5, 6, 10, 12)
POINTS = (
    ("core_mp", ((0, 2), (2, 4), (3, 5), (5, 7), (6, 8), (7, 9), (8, 10), (9, 11), (10, 12))),
    ("core_both", ((1, 3), (4, 6), (11, 13))),
    ("mp", ((0, 6), (2, 8), (3, 10), (5, 12), (6, 14), (7, 16), (8, 18), (9, 20), (10, 22))),
    ("both", ((1, 7), (4, 10), (11, 16))),
    ("side", ((7, 18), (8, 20), (9, 23))),
    ("side_line", ((0, 11), (2, 12), (3, 13), (5, 14), (6, 17))),
    ("then_mp", ((1, 12), (4, 18), (11, 23))),
    ("low", ((1, 14), (7, 20), (4, 21), (8, 22))),
    ("high", ((1, 18), (7, 22), (4, 23))),
    ("line", ((0, 13), (2, 14), (3, 15), (5, 17), (6, 20))),
    ("high_spread", ((1, 22),)),
    ("spread", ((0, 16), (2, 18), (3, 20), (5, 21), (6, 23))),
    ("side_spread", ((0, 19), (2, 21), (3, 22))),
    ("core_spread", ((0, 20), (2, 22), (3, 23))),
)
REST = (
    ("low_spread", 1), ("side_spread", 5), ("high_spread", 7), ("core_mp", 12), ("high", 8), ("core_spread", 5),
    ("low", 11), ("side_line", 10), ("low", 9), ("high_spread", 4), ("side_spread", 6), ("low_spread", 7),
    ("high_spread", 8), ("mp", 12), ("core_spread", 6), ("high", 11), ("side_spread", 1), ("line", 10),
    ("core_spread", 1), ("side_spread", 7), ("low_spread", 4), ("high", 9), ("low_spread", 8), ("core_spread", 7),
    ("side_line", 12), ("high_spread", 11), ("spread", 10), ("side_spread", 4), ("high_spread", 9),
    ("core_spread", 4), ("low_spread", 11), ("line", 12), ("side_spread", 8), ("low_spread", 9), ("core_spread", 8),
    ("side_spread", 10), ("spread", 12), ("core_spread", 10), ("side_spread", 11), ("core_spread", 11),
    ("side_spread", 9), ("core_spread", 9), ("side_spread", 12), ("core_spread", 12),
)


def dot(a, b):
    return jnp.dot(a, b, preferred_element_type=F32)


def dot_nt(a, b):
    return lax.dot_general(a, b, NT, preferred_element_type=F32)


def centre(values):
    centred = values - jnp.mean(values, -1, keepdims=True)
    return centred, lax.rsqrt(jnp.mean(centred * centred, -1, keepdims=True) + 1e-06)


def norm_back(grad, normed, scale, gain):
    scaled = grad * gain
    return scale * (
        scaled
        - jnp.mean(scaled, -1, keepdims=True)
        - normed * jnp.mean(scaled * normed, -1, keepdims=True)
    )


def gelu_parts(v):
    phi = 0.5 + 0.5 * lax.erf(v * 0.7071067811865476)
    return phi, phi + v * (0.3989422804014327 * jnp.exp(-0.5 * v * v))


def layer(
    sizes,
    patches, cotangent, gain_one, shift_one, token_in, token_bias, token_out, token_shift,
    gain_two, shift_two, channel_in, channel_bias, channel_out, channel_shift,
    mixed, inputs_grad, summed, hid_out, slope_out,
    wi, wo, vecs, cbs, cbo, tbs, tss, tins, touts, tw, twi_t, two_t, keep,
    dys, dys_t, u2s, u2s_t, u1s, chid, dcp, dtok,
    xs, ms, hid, slope, stats,
    row_acc, cb_acc, tin_acc, tout_acc, small,
    grads, from_core, acc, from_mp, from_x, from_z, from_far,
    load_sem, stage_sem, small_sem, grad_sem, tok_s, tok_r, w_s, w_r, wc_s, wc_r, c_s, c_r, y_s, y_r, x_s, x_r, z_s, z_r, zh_s, zh_r, zl_s, zl_r,
    a_s, a_r, al_s, al_r, sl_s, sl_r, l_sem, xa_s, xa_r, ca_s, ca_r, far_s, far_r,
):
    images, patch, width, token_half, hidden_half, ticks, dp_size, last_half = sizes
    rows = dys.shape[0]
    high = u1s.shape[1]
    step = hidden_half // ticks
    half = width // 2
    chunks = 2 * ticks
    eighth_in = width // 8

    dp = lax.axis_index("dp")
    mp = lax.axis_index("mp")
    core = lax.rem(dp, 2)
    side = lax.rem(lax.div(dp, 2), 2)
    near = lax.rem(lax.div(dp, 2), 4)
    line = lax.rem(lax.div(dp, 4), 4)
    part = core * 4 + near
    low = lax.rem(line, 2)

    to_mp = {"mp": 1 - mp}
    to_core = {"dp": dp + 1 - 2 * core}
    to_side = {"dp": dp + 2 - 4 * side}

    def near_of(r):
        return {"dp": dp + 2 * (lax.rem(near + r, 4) - near)}

    def line_of(r):
        return {"dp": dp + 4 * (lax.rem(line + r, 4) - line)}

    far_bits = []
    bit = 16
    while bit < dp_size:
        far_bits.append(bit)
        bit *= 2

    def far_of(i):
        b = far_bits[i]
        return {"dp": dp + b - 2 * b * lax.rem(lax.div(dp, b), 2)}

    def remote(src, dst, send, recv, device):
        return pltpu.make_async_remote_copy(
            src_ref=src, dst_ref=dst, send_sem=send, recv_sem=recv, device_id=device, device_id_type=MESH
        )

    def al(v, m):
        return pl.multiple_of(v, m)

    def own_loads(t):
        return (
            pltpu.make_async_copy(
                channel_in.at[:, pl.ds(al(t * step, step), step)],
                wi.at[:, pl.ds(al(t * 2 * step, step), step)],
                load_sem.at[t, 0],
            ),
            pltpu.make_async_copy(
                channel_out.at[pl.ds(al(t * step, step), step), :],
                wo.at[pl.ds(al(t * 2 * step, step), step), :],
                load_sem.at[t, 1],
            ),
        )

    def other_in(t, first, count):
        return wi.at[pl.ds(al(first, eighth_in), count), pl.ds(al(t * 2 * step + step, step), step)]

    def other_out(t, first, count):
        return wo.at[pl.ds(al(t * 2 * step + step + first, 16), count), :]

    which = side + core * (low - side)
    quarter_out = step // 4
    to_pair = {"dp": dp + (2 - 4 * side) * (1 - core) + (4 - 8 * low) * core}

    def gather_mp(t):
        first = core * 2 * quarter_out + which * quarter_out
        return (
            remote(
                channel_in.at[pl.ds(al(part * eighth_in, eighth_in), eighth_in), pl.ds(al(t * step, step), step)],
                other_in(t, part * eighth_in, eighth_in),
                w_s.at[t, 0], w_r.at[t, 0], to_mp,
            ),
            remote(
                channel_out.at[pl.ds(al(t * step + first, 16), quarter_out), :],
                other_out(t, first, quarter_out),
                w_s.at[t, 1], w_r.at[t, 1], to_mp,
            ),
        )

    def gather_near(t):
        a = other_in(t, part * eighth_in, eighth_in)
        b = other_out(t, core * 2 * quarter_out + which * quarter_out, quarter_out)
        copies = [remote(a, a, w_s.at[t, r + 1], w_r.at[t, r + 1], near_of(r)) for r in (1, 2, 3)]
        return copies + [remote(b, b, w_s.at[t, 5], w_r.at[t, 5], to_pair)]

    def gather_core(t):
        a = other_in(t, core * 4 * eighth_in, 4 * eighth_in)
        b = other_out(t, core * 2 * quarter_out, 2 * quarter_out)
        s = lax.rem(t, 2)
        return (
            remote(a, a, wc_s.at[s, 0], wc_r.at[s, 0], to_core),
            remote(b, b, wc_s.at[s, 1], wc_r.at[s, 1], to_core),
        )

    def token_mp():
        return (
            remote(
                tw.at[core, pl.ds(0, token_half)], tw.at[core, pl.ds(token_half, token_half)], tok_s.at[0], tok_r.at[0], to_mp
            ),
        )

    def bias_mp():
        return (remote(cbs, cbo, tok_s.at[1], tok_r.at[1], to_mp),)

    def token_core():
        ref = tw.at[core, pl.ds(token_half, token_half)]
        return (remote(ref, ref, tok_s.at[2], tok_r.at[2], to_core),)

    high_bit = lax.div(line, 2)
    to_low = {"dp": dp + 4 - 8 * low}
    to_high = {"dp": dp + 8 - 16 * high_bit}

    def rows_at(first, count):
        return pl.ds(al(first, 16), count)

    def core_copy(c, h):
        slot, q, i = lax.rem(lax.div(c, 2), 2), lax.rem(c, 2), lax.rem(c, RING)
        rng = pl.ds(0, h)
        return remote(
            grads.at[slot, 1 - core, q, :, :, rng], from_core.at[slot, q, :, :, rng], c_s.at[i], c_r.at[i], to_core
        )

    def mp_copy(c, h):
        rng = pl.ds(0, h)
        return remote(acc.at[c, 1, :, rng], from_mp.at[c, :, rng], y_s.at[c], y_r.at[c], to_mp)

    def side_copy(c, h):
        rng = pl.ds(0, h)
        return remote(acc.at[c, 0, 1 - side, rng], from_x.at[c, rng], x_s.at[c], x_r.at[c], to_side)

    def both_copy(c):
        return remote(acc.at[c, :, 1 - side], from_mp.at[c], x_s.at[c], x_r.at[c], to_side)

    def then_mp_copy(c):
        return remote(acc.at[c, 1, side], from_x.at[c], y_s.at[c], y_r.at[c], to_mp)

    def low_copy(c, h):
        n = h // 2
        src = acc.at[c, 0, side, rows_at((1 - low) * n, n)]
        return remote(src, from_z.at[c, pl.ds(0, n)], z_s.at[c], z_r.at[c], to_low)

    def high_copy(c, h):
        n = h // 4
        src = acc.at[c, 0, side, rows_at(low * 2 * n + (1 - high_bit) * n, n)]
        return remote(src, from_z.at[c, pl.ds(2 * n, n)], zh_s.at[c], zh_r.at[c], to_high)

    def at_place(c, h):
        return rows_at(low * (h // 2) + high_bit * (h // 4), h // 4)

    def at_line(h, place):
        return rows_at(place * (h // 4), h // 4)

    def line_sems(c, d, first, second, third):
        return ((first.at[c], second.at[c], third.at[d])[r] for r in range(3))

    def line_copies(c, h, d):
        sends = line_sems(c, d, z_s, zh_s, zl_s)
        recvs = line_sems(c, d, z_r, zh_r, zl_r)
        return [
            remote(
                acc.at[c, 0, side, at_line(h, lax.rem(line + r, 4))],
                from_z.at[c, pl.ds((r - 1) * (h // 4), h // 4)], send, recv, line_of(r),
            )
            for r, send, recv in zip((1, 2, 3), sends, recvs)
        ]

    def keep_copy(c, rng):
        return pltpu.make_async_copy(acc.at[c, 0, side, rng], summed.at[core, c, side, rng], l_sem.at[c])

    def high_spread_copy(c, h):
        rng = at_place(c, h)
        return remote(acc.at[c, 0, side, rng], summed.at[core, c, side, rng], a_s.at[c], a_r.at[c], to_high)

    def low_spread_copy(c, h):
        ref = summed.at[core, c, side, rows_at(low * (h // 2), h // 2)]
        return remote(ref, ref, al_s.at[c], al_r.at[c], to_low)

    def spread_copies(c, h, d):
        rng = at_line(h, line)
        src, dst = acc.at[c, 0, side, rng], summed.at[core, c, side, rng]
        sends = line_sems(c, d, a_s, al_s, sl_s)
        recvs = line_sems(c, d, a_r, al_r, sl_r)
        return [remote(src, dst, send, recv, line_of(r)) for r, send, recv in zip((1, 2, 3), sends, recvs)]

    def side_spread_copy(c, h):
        ref = summed.at[core, c, side, pl.ds(0, h)]
        return remote(ref, ref, xa_s.at[c], xa_r.at[c], to_side)

    def core_spread_copy(c, h):
        ref = summed.at[core, c, :, pl.ds(0, h)]
        return remote(ref, ref, ca_s.at[c], ca_r.at[c], to_core)

    def add(a, b):
        return (a.astype(F32) + b.astype(F32)).astype(BF16)

    def core_step(c, h, send):
        core_copy(c, h).wait()
        slot, q, rng = lax.rem(lax.div(c, 2), 2), lax.rem(c, 2), pl.ds(0, h)
        acc[c, 1, :, rng] = add(grads[slot, core, q, 1, :, rng], from_core[slot, q, 1, :, rng])
        if send is mp_copy:
            send(c, h).start()
        acc[c, 0, :, rng] = add(grads[slot, core, q, 0, :, rng], from_core[slot, q, 0, :, rng])
        if send is both_copy:
            send(c).start()

    def core_mp(c, h, d):
        core_step(c, h, mp_copy)

    def core_both(c, h, d):
        core_step(c, h, both_copy)

    def mp_step(c, h, d):
        mp_copy(c, h).wait()
        rng = pl.ds(0, h)
        acc[c, 0, 1 - side, rng] = add(acc[c, 0, 1 - side, rng], from_mp[c, 1 - side, rng])
        side_copy(c, h).start()
        acc[c, 0, side, rng] = add(acc[c, 0, side, rng], from_mp[c, side, rng])

    def side_step(c, h, d):
        side_copy(c, h).wait()
        rng = pl.ds(0, h)
        acc[c, 0, side, rng] = add(acc[c, 0, side, rng], from_x[c, rng])
        low_copy(c, h).start()

    def side_line(c, h, d):
        side_copy(c, h).wait()
        rng = pl.ds(0, h)
        acc[c, 0, side, rng] = add(acc[c, 0, side, rng], from_x[c, rng])
        for copy in line_copies(c, h, d):
            copy.start()

    def both_step(c, h, d):
        both_copy(c).wait()
        acc[c, 1, side] = add(acc[c, 1, side], from_mp[c, 1])
        then_mp_copy(c).start()
        acc[c, 0, side] = add(acc[c, 0, side], from_mp[c, 0])

    def then_mp_step(c, h, d):
        then_mp_copy(c).wait()
        acc[c, 0, side] = add(acc[c, 0, side], from_x[c])
        low_copy(c, h).start()

    def low_step(c, h, d):
        low_copy(c, h).wait()
        rng = rows_at(low * (h // 2), h // 2)
        acc[c, 0, side, rng] = add(acc[c, 0, side, rng], from_z[c, pl.ds(0, h // 2)])
        high_copy(c, h).start()

    def over_far(c, rng, count):
        for i in range(len(far_bits)):
            dst = from_far.at[c, i, pl.ds(0, count)]
            copy = remote(acc.at[c, 0, side, rng], dst, far_s.at[c, i], far_r.at[c, i], far_of(i))
            copy.start()
            copy.wait()
            acc[c, 0, side, rng] = add(acc[c, 0, side, rng], from_far[c, i, pl.ds(0, count)])

    def high_step(c, h, d):
        high_copy(c, h).wait()
        rng = at_place(c, h)
        acc[c, 0, side, rng] = add(acc[c, 0, side, rng], from_z[c, pl.ds(h // 2, h // 4)])
        over_far(c, rng, h // 4)
        high_spread_copy(c, h).start()
        keep_copy(c, rng).start()

    def high_spread_step(c, h, d):
        keep_copy(c, at_place(c, h)).wait()
        high_spread_copy(c, h).wait()
        low_spread_copy(c, h).start()

    def low_spread_step(c, h, d):
        low_spread_copy(c, h).wait()
        side_spread_copy(c, h).start()

    def line_step(c, h, d):
        for copy in line_copies(c, h, d):
            copy.wait()
        rng = at_line(h, line)
        total = acc[c, 0, side, rng].astype(F32)
        for r in range(3):
            total = total + from_z[c, pl.ds(r * (h // 4), h // 4)].astype(F32)
        acc[c, 0, side, rng] = total.astype(BF16)
        over_far(c, rng, h // 4)
        for copy in spread_copies(c, h, d):
            copy.start()
        keep_copy(c, rng).start()

    def spread_step(c, h, d):
        keep_copy(c, at_line(h, line)).wait()
        for copy in spread_copies(c, h, d):
            copy.wait()
        side_spread_copy(c, h).start()

    def side_spread_step(c, h, d):
        side_spread_copy(c, h).wait()
        core_spread_copy(c, h).start()

    def core_spread_step(c, h, d):
        core_spread_copy(c, h).wait()

    steps = {
        "core_mp": core_mp, "core_both": core_both, "mp": mp_step, "side": side_step, "side_line": side_line, "both": both_step,
        "then_mp": then_mp_step, "low": low_step, "high": high_step, "high_spread": high_spread_step,
        "low_spread": low_spread_step, "line": line_step, "spread": spread_step,
        "side_spread": side_spread_step, "core_spread": core_spread_step,
    }

    def point(p, places):
        for name, entries in POINTS:
            here = [(c, at) for c, at in entries if at in places]
            if here:
                now = [(p == at).astype(jnp.int32) for _, at in here]
                c = sum(c * one for (c, _), one in zip(here, now))
                d = sum(STRAIGHT.index(c) * one for (c, _), one in zip(here, now) if c in STRAIGHT)

                @pl.when(sum(now) > 0)
                def _(c=c, d=d, name=name):
                    steps[name](c, half, d)

    barrier = pltpu.get_barrier_semaphore()
    greet = [to_mp, to_core] + [near_of(r) for r in (1, 2, 3)] + [line_of(r) for r in (1, 2, 3)]
    greet += [far_of(i) for i in range(len(far_bits))]
    for device in greet:
        pl.semaphore_signal(barrier, inc=1, device_id=device, device_id_type=MESH)

    def patch_copy(b):
        return pltpu.make_async_copy(patches.at[b], xs.at[lax.rem(b, 2)], stage_sem.at[0, lax.rem(b, 2)])

    def cot_copy(b):
        return pltpu.make_async_copy(cotangent.at[b], ms.at[lax.rem(b, 2)], stage_sem.at[1, lax.rem(b, 2)])

    def hid_save(b):
        s = lax.rem(b, 2)
        return (
            pltpu.make_async_copy(hid.at[s, pl.ds(0, 2 * token_half)], hid_out.at[b], stage_sem.at[2, s]),
            pltpu.make_async_copy(slope.at[s], slope_out.at[b], stage_sem.at[3, s]),
        )

    def hid_load(b):
        s = lax.rem(b, 2)
        return (
            pltpu.make_async_copy(hid_out.at[b], hid.at[s, pl.ds(0, 2 * token_half)], stage_sem.at[2, s]),
            pltpu.make_async_copy(slope_out.at[b], slope.at[s], stage_sem.at[3, s]),
        )

    def grad_save(b):
        return pltpu.make_async_copy(keep.at[b], inputs_grad.at[b], grad_sem.at[b])

    def mixed_save(b):
        s = lax.rem(b, 2)
        return pltpu.make_async_copy(ms.at[s], mixed.at[b], stage_sem.at[4, s])

    def both(copies, what):
        for copy in copies:
            getattr(copy, what)()

    def small_loads():
        pairs = [(token_in, tins), (token_out, touts), (token_bias, tbs), (token_shift, tss), (channel_bias, cbs.at[0])]
        vectors = (gain_one, shift_one, gain_two, shift_two, channel_shift)
        pairs += [(ref, vecs.at[i]) for i, ref in enumerate(vectors)]
        return [pltpu.make_async_copy(src, dst, small_sem.at[i]) for i, (src, dst) in enumerate(pairs)]

    both(small_loads(), "start")
    for b in (0, 1):
        patch_copy(b).start()
        cot_copy(b).start()

    wide = tw.shape[2]
    twi, two = tw.at[0], tw.at[1]

    def three(row):
        hi = row.astype(BF16).astype(F32)
        mid = (row - hi).astype(BF16).astype(F32)
        return hi, mid, row - hi - mid

    twi[pl.ds(0, token_half), :] = jnp.zeros((token_half, wide), BF16)
    two[pl.ds(0, token_half), :] = jnp.zeros((token_half, wide), BF16)
    at_row = lax.broadcasted_iota(jnp.int32, (16, wide), 0)
    at_lane = lax.broadcasted_iota(jnp.int32, (token_half, wide), 1)
    both(small_loads(), "wait")
    twi[pl.ds(0, token_half), pl.ds(0, patch)] = tins[...]
    two[pl.ds(0, token_half), pl.ds(0, patch)] = touts[...]
    padded = jnp.zeros((1, wide - token_half), F32)
    bias_row = jnp.concatenate([tbs[...].reshape(1, token_half), padded], axis=1)
    column = jnp.broadcast_to(bias_row, (LANES, wide)).T[:token_half, 0:1]
    filled = twi[pl.ds(0, token_half), :].astype(F32)
    for i, value in enumerate(three(column)):
        filled = jnp.where(at_lane == patch + i, value, filled)
    twi[pl.ds(0, token_half), :] = filled.astype(BF16)
    shift_row = jnp.concatenate([tss[...].reshape(1, patch), jnp.zeros((1, wide - patch), F32)], axis=1)
    extra = jnp.zeros((16, wide), F32)
    for i, value in enumerate(three(shift_row)):
        extra = jnp.where(at_row == i, value, extra)
    tokens = 2 * token_half
    two[pl.ds(tokens, 16), :] = extra.astype(BF16)

    pl.semaphore_wait(barrier, len(greet))
    both(token_mp(), "start")
    both(gather_mp(0), "start")
    both(bias_mp(), "start")

    def start_own(t, _):
        both(own_loads(t), "start")
        return 0

    lax.fori_loop(0, ticks, start_own, 0)

    dys[...] = jnp.zeros_like(dys)
    u2s[...] = jnp.zeros_like(u2s)
    dtok[...] = jnp.zeros_like(dtok)
    rest_rows = rows - images * high
    if rest_rows:
        chid[pl.ds(images * high, rest_rows), :] = jnp.zeros((rest_rows, chid.shape[1]), BF16)
        dcp[pl.ds(images * high, rest_rows), :] = jnp.zeros((rest_rows, dcp.shape[1]), BF16)
    row_acc[...] = jnp.zeros_like(row_acc)
    tin_acc[...] = jnp.zeros_like(tin_acc)
    tout_acc[...] = jnp.zeros_like(tout_acc)
    small[...] = jnp.zeros_like(small)
    u2s_t[pl.ds(width, 16), :] = jnp.ones((16, rows), BF16)
    for s in (0, 1):
        hid[s, pl.ds(tokens, 16), :] = jnp.ones((16, width), BF16)

    below = lax.broadcasted_iota(jnp.int32, (high, width), 0)
    ones = jnp.where(jnp.logical_and(below >= patch, below < patch + 3), 1.0, 0.0).astype(BF16)
    for b in range(images):
        u1s[b] = ones

    gain1, shift1, gain2, shift2 = (vecs[i : i + 1] for i in range(4))

    def first_norm(b, _):
        s = lax.rem(b, 2)
        patch_copy(b).wait()
        x = xs[s].astype(F32)

        @pl.when(b + 2 < images)
        def _():
            patch_copy(b + 2).start()

        keep[b] = x
        mean = jnp.mean(x, -1, keepdims=True)
        centred = x - mean
        scale = lax.rsqrt(jnp.mean(centred * centred, -1, keepdims=True) + 1e-06)
        stats[b, :, 0:1] = mean
        stats[b, :, 1:2] = scale
        u1s[b, pl.ds(0, patch), :] = (centred * scale * gain1 + shift1).astype(BF16)
        pre = dot(twi[pl.ds(0, token_half), pl.ds(0, high)], u1s[b])
        phi, deriv = gelu_parts(pre)
        at = pl.ds(al(b * token_half, 16), token_half)
        chid[at, pl.ds(0, width)] = (pre * phi).astype(BF16)
        dcp[at, pl.ds(0, width)] = deriv.astype(BF16)
        cot_copy(b).wait()
        value = ms[s]

        @pl.when(b + 2 < images)
        def _():
            cot_copy(b + 2).start()

        @pl.when(b + 1 < ticks)
        def _():
            both(gather_mp(b + 1), "start")

        @pl.when(b == images // 2)
        def _():
            both(token_mp(), "wait")
            both(token_core(), "start")

        dys[pl.ds(al(b * high, 16), patch), :] = value
        row_acc[pl.ds(4, 1), :] += jnp.sum(value.astype(F32), 0, keepdims=True)
        return 0

    lax.fori_loop(0, images, first_norm, 0)
    for t in range(images + 1, ticks):
        both(gather_mp(t), "start")

    def turn_dy(j, _):
        at = pl.ds(al(j * LANES, LANES), LANES)
        dys_t[:, at] = dys[at, :].T
        return 0

    lax.fori_loop(0, rows // LANES, turn_dy, 0)

    both(token_core(), "wait")
    two_t[...] = two[...].T

    def token_forward(b, _):
        s = lax.rem(b, 2)
        pre = dot(twi[pl.ds(token_half, token_half), pl.ds(0, high)], u1s[b])
        phi, deriv = gelu_parts(pre)

        @pl.when(b >= 2)
        def _():
            both(hid_save(b - 2), "wait")

        at = pl.ds(al(b * token_half, 16), token_half)
        hid[s, pl.ds(0, token_half), :] = chid[at, pl.ds(0, width)]
        slope[s, pl.ds(0, token_half), :] = dcp[at, pl.ds(0, width)]
        hid[s, pl.ds(token_half, token_half), :] = (pre * phi).astype(BF16)
        slope[s, pl.ds(token_half, token_half), :] = deriv.astype(BF16)
        both(hid_save(b), "start")
        x1 = keep[b] + dot(two_t[pl.ds(0, high), :], hid[s])[:patch]
        keep[b] = x1
        mean = jnp.mean(x1, -1, keepdims=True)
        centred = x1 - mean
        scale = lax.rsqrt(jnp.mean(centred * centred, -1, keepdims=True) + 1e-06)
        stats[b, :, 2:3] = mean
        stats[b, :, 3:4] = scale
        u2s[pl.ds(al(b * high, 16), patch), :] = (centred * scale * gain2 + shift2).astype(BF16)

        for t, when in enumerate((0, images // 2, images - 1)):

            @pl.when(b == when)
            def _(t=t):
                both(gather_mp(t), "wait")
                both(gather_near(t), "start")

        return 0

    lax.fori_loop(0, images, token_forward, 0)
    both(gather_near(0), "wait")
    both(gather_core(0), "start")
    both(bias_mp(), "wait")

    def turn_u2(j, _):
        at = pl.ds(al(j * LANES, LANES), LANES)
        u2s_t[pl.ds(0, width), at] = u2s[at, :].T
        return 0

    lax.fori_loop(0, rows // LANES, turn_u2, 0)
    for b in range(max(images - 2, 0), images):
        both(hid_save(b), "wait")

    live = images * high
    tiles = 2 if live % 32 == 0 else 1
    tall = live // tiles

    def channel(t, _):
        both(own_loads(t), "wait")
        both(gather_core(t), "wait")
        at = pl.ds(al(t * 2 * step, 2 * step), 2 * step)
        weight_in, weight_out = wi[:, at], wo[at, :]
        here = pl.ds(al(t * step, step), step)
        bias = jnp.concatenate([cbs[:, here], cbo[:, here]], axis=1)
        for i in range(tiles):
            rng = pl.ds(i * tall, tall)
            pre = dot(u2s[rng, :], weight_in) + bias
            back = dot_nt(dys[rng, :], weight_out)
            phi, deriv = gelu_parts(pre)
            chid[rng, at] = (pre * phi).astype(BF16)
            dcp[rng, at] = (back * deriv).astype(BF16)

        @pl.when(t + 3 < ticks)
        def _():
            both(gather_mp(t + 3), "wait")
            both(gather_near(t + 3), "start")

        @pl.when(t + 1 < ticks)
        def _():
            both(gather_near(t + 1), "wait")
            both(gather_core(t + 1), "start")

        point(2 * t, range(0, chunks, 2))
        slot = lax.rem(t, 2)
        grad_in = dot(u2s_t[...], dcp[:, at])
        cb_acc[:, at] = grad_in[width : width + 1]
        grad_in = grad_in[:width].astype(BF16)
        grad_out = dot(dys_t[...], chid[:, at]).astype(BF16)
        for m, value in ((0, grad_in), (1, grad_out)):
            for o in (0, 1):
                for q in (0, 1):
                    first = o * step + q * LANES
                    for k in (0, 1):
                        grads[slot, m, q, o, k] = value[k * half : (k + 1) * half, first : first + LANES]
        point(2 * t + 1, range(1, chunks, 2))
        core_copy(2 * t, width // 2).start()
        core_copy(2 * t + 1, width // 2).start()
        return 0

    lax.fori_loop(0, ticks, channel, 0)

    both(hid_load(0), "start")
    patch_copy(0).start()
    twi_t[...] = twi[pl.ds(0, tokens), :].T
    gain1, gain2, out_shift = vecs[0:1], vecs[2:3], vecs[4:5]

    def backward(b, _):
        s = lax.rem(b, 2)
        rng = pl.ds(al(b * high, 16), high)

        @pl.when(b + 1 < images)
        def _():
            both(hid_load(b + 1), "start")
            patch_copy(b + 1).start()

        @pl.when(b >= 2)
        def _():
            mixed_save(b - 2).wait()

        x1 = keep[b]
        ms[s] = (x1 + dot(chid[rng, :], wo[...])[:patch] + out_shift).astype(BF16)
        mixed_save(b).start()
        du2 = dot_nt(dcp[rng, :], wi[...])[:patch]
        n2 = (x1 - stats[b, :, 2:3]) * stats[b, :, 3:4]
        row_acc[pl.ds(2, 1), :] += jnp.sum(du2 * n2, 0, keepdims=True)
        row_acc[pl.ds(3, 1), :] += jnp.sum(du2, 0, keepdims=True)
        dy = dys[pl.ds(al(b * high, 16), patch), :].astype(F32)
        dx1 = dy + norm_back(du2, n2, stats[b, :, 3:4], gain2)
        keep[b] = dx1
        dtok[pl.ds(0, patch), :] = dx1.astype(BF16)
        point(chunks + 2 * b, range(chunks, chunks + 2 * images, 2))
        both(hid_load(b), "wait")
        dtk = dtok[...]
        hidden = hid[s]
        tout_acc[:, pl.ds(0, high)] += dot_nt(hidden, dtk)
        dpre = (dot(two[pl.ds(0, tokens), pl.ds(0, high)], dtk) * slope[s].astype(F32)).astype(BF16)
        tin_acc[:, pl.ds(0, high)] += dot_nt(dpre, u1s[b])
        du1 = dot(twi_t[pl.ds(0, high), :], dpre)[:patch]
        patch_copy(b).wait()
        n1 = (xs[s].astype(F32) - stats[b, :, 0:1]) * stats[b, :, 1:2]
        row_acc[pl.ds(0, 1), :] += jnp.sum(du1 * n1, 0, keepdims=True)
        row_acc[pl.ds(1, 1), :] += jnp.sum(du1, 0, keepdims=True)
        keep[b] = keep[b] + norm_back(du1, n1, stats[b, :, 1:2], gain1)
        grad_save(b).start()
        point(chunks + 2 * b + 1, range(chunks + 1, chunks + 2 * images, 2))
        return 0

    lax.fori_loop(0, images, backward, 0)

    blocks = width // LANES
    for o in (0, 1):
        for v in range(5):
            for j in range(blocks):
                small[o, pl.ds(v * blocks + j, 1), :] = row_acc[pl.ds(v, 1), pl.ds(j * LANES, LANES)]
        for j in range(2):
            small[o, pl.ds(5 * blocks + j, 1), :] = tout_acc[pl.ds(tokens, 1), pl.ds(j * LANES, LANES)]
        for c in range(chunks):
            first = (c // 2) * 2 * step + o * step + (c % 2) * LANES
            small[o, pl.ds(5 * blocks + 2 + c, 1), :] = cb_acc[pl.ds(0, 1), pl.ds(first, LANES)]
    last_slot = ticks % 2
    for o in (0, 1):
        for m, total in ((0, tin_acc), (1, tout_acc)):
            for j in range(2):
                grads[last_slot, m, 0, o, j, pl.ds(0, token_half), :] = total[
                    pl.ds(o * token_half, token_half), pl.ds(j * LANES, LANES)
                ].astype(BF16)
        grads[last_slot, 0, 0, o, 0, pl.ds(token_half, small.shape[1]), :] = small[o].astype(BF16)
    core_copy(chunks, last_half).start()
    for name, c in REST:
        steps[name](c, half if c < chunks else last_half, STRAIGHT.index(c) if c in STRAIGHT else 0)
    for b in range(max(images - 2, 0), images):
        mixed_save(b).wait()
    for b in range(images):
        grad_save(b).wait()


def widen(
    sizes, summed, mixed_in, grad_in,
    mixed, inputs_grad, d_in, d_out, d_tin, d_tbias, d_tout, d_tshift, d_gain1, d_shift1, d_gain2, d_shift2, d_cbias, d_cshift,
    sums, last, wide_in, wide_out, hold_mixed, hold_grad, in_sem, out_sem, last_sem, through_sem,
):
    images, patch, width, token_half, chunks = sizes

    def at(c):
        return pl.ds(c * LANES, LANES)

    loads = [[pltpu.make_async_copy(summed.at[m, c], sums.at[m, c], in_sem.at[m, c]) for m in (0, 1)] for c in range(chunks)]
    stores = [
        (
            pltpu.make_async_copy(wide_in.at[:, at(c)], d_in.at[:, at(c)], out_sem.at[0, c]),
            pltpu.make_async_copy(wide_out.at[at(c)], d_out.at[at(c)], out_sem.at[1, c]),
        )
        for c in range(chunks)
    ]
    load_last = [
        pltpu.make_async_copy(summed.at[m, chunks, :, pl.ds(0, last.shape[2])], last.at[m], last_sem.at[m]) for m in (0, 1)
    ]
    ins, outs = [], []
    for i, (src, hold, dst) in enumerate(((mixed_in, hold_mixed, mixed), (grad_in, hold_grad, inputs_grad))):
        for b in range(images):
            ins.append(pltpu.make_async_copy(src.at[b], hold.at[b], through_sem.at[i, b]))
            outs.append(pltpu.make_async_copy(hold.at[b], dst.at[b], through_sem.at[i + 2, b]))
    for pair in loads:
        for copy in pair:
            copy.start()
    for copy in load_last + ins:
        copy.start()
    through = iter(zip(ins, outs))
    for c in range(chunks):
        for copy in loads[c]:
            copy.wait()
        wide_in[:, c * LANES : (c + 1) * LANES] = sums[0, c].reshape(width, LANES).astype(F32)
        stores[c][0].start()
        wide_out[c * LANES : (c + 1) * LANES, :] = sums[1, c].reshape(width, LANES).T.astype(F32)
        stores[c][1].start()
        for arrived, leave in [pair for pair in (next(through, None),) if pair]:
            arrived.wait()
            leave.start()
    for arrived, leave in through:
        arrived.wait()
        leave.start()
    for copy in load_last:
        copy.wait()

    def token_block(m):
        halves = [last[m, j, pl.ds(0, token_half), :] for j in (0, 1)]
        return jnp.concatenate(halves, axis=1).astype(F32)

    grad = token_block(0)
    d_tin[...] = grad[:, :patch]
    d_tbias[...] = grad.T[patch : patch + 1].reshape(token_half)
    d_tout[...] = token_block(1)[:, :patch]
    blocks = width // LANES
    rows = last[0, 0, pl.ds(token_half, 64), :].astype(F32)

    def vector(first, count):
        return jnp.concatenate([rows[first + j : first + j + 1] for j in range(count)], axis=1)

    for v, ref in enumerate((d_gain1, d_shift1, d_gain2, d_shift2, d_cshift)):
        ref[...] = vector(v * blocks, blocks).reshape(width)
    d_tshift[...] = vector(5 * blocks, 2)[:, :patch].reshape(patch)
    d_cbias[...] = vector(5 * blocks + 2, chunks).reshape(chunks * LANES)
    for pair in stores:
        for copy in pair:
            copy.wait()
    for copy in outs:
        copy.wait()


def per_device(
    dp_size,
    patches, cotangent, gain_one, shift_one, token_in, token_bias, token_out, token_shift,
    gain_two, shift_two, channel_in, channel_bias, channel_out, channel_shift,
):
    images, patch, width = patches.shape
    token_half = token_in.shape[1]
    hidden_half = channel_in.shape[1]
    step = 2 * LANES
    ticks = hidden_half // step
    chunks = 2 * ticks
    high = -(-(patch + 3) // 16) * 16
    rows = -(-images * high // LANES) * LANES
    wide = -(-patch // LANES) * LANES
    tokens = 2 * token_half
    far = max(sum(1 for b in range(4, 20) if 2**b < dp_size), 1)
    far_chunks = chunks + 1 if dp_size > 16 else 1
    last_half = -(-(token_half + 64) // 64) * 64
    sizes = (images, patch, width, token_half, hidden_half, ticks, dp_size, last_half)
    hbm = pl.BlockSpec(memory_space=pl.ANY)
    n = chunks + 1
    half = width // 2
    dma = pltpu.SemaphoreType.DMA
    mixed, inputs_grad, summed, _, _ = pl.pallas_call(
        functools.partial(layer, sizes),
        out_shape=(
            jax.ShapeDtypeStruct((images, patch, width), BF16),
            jax.ShapeDtypeStruct((images, patch, width), F32),
            jax.ShapeDtypeStruct((2, n, 2, half, LANES), BF16),
            jax.ShapeDtypeStruct((images, tokens, width), BF16),
            jax.ShapeDtypeStruct((images, tokens, width), BF16),
        ),
        in_specs=[hbm] * 14,
        out_specs=(hbm,) * 5,
        scratch_shapes=[
            pltpu.VMEM((width, 2 * hidden_half), BF16),
            pltpu.VMEM((2 * hidden_half, width), BF16),
            pltpu.VMEM((8, width), F32),
            pltpu.VMEM((1, hidden_half), F32),
            pltpu.VMEM((1, hidden_half), F32),
            pltpu.VMEM((token_half,), F32),
            pltpu.VMEM((patch,), F32),
            pltpu.VMEM((token_half, patch), BF16),
            pltpu.VMEM((token_half, patch), BF16),
            pltpu.VMEM((2, tokens + 16, wide), BF16),
            pltpu.VMEM((wide, tokens), BF16),
            pltpu.VMEM((wide, tokens + 16), BF16),
            pltpu.VMEM((images, patch, width), F32),
            pltpu.VMEM((rows, width), BF16),
            pltpu.VMEM((width, rows), BF16),
            pltpu.VMEM((rows, width), BF16),
            pltpu.VMEM((width + 16, rows), BF16),
            pltpu.VMEM((images, high, width), BF16),
            pltpu.VMEM((rows, 2 * hidden_half), BF16),
            pltpu.VMEM((rows, 2 * hidden_half), BF16),
            pltpu.VMEM((high, width), BF16),
            pltpu.VMEM((2, patch, width), BF16),
            pltpu.VMEM((2, patch, width), BF16),
            pltpu.VMEM((2, tokens + 16, width), BF16),
            pltpu.VMEM((2, tokens, width), BF16),
            pltpu.VMEM((images, patch, 4), F32),
            pltpu.VMEM((8, width), F32),
            pltpu.VMEM((1, 2 * hidden_half), F32),
            pltpu.VMEM((tokens, wide), F32),
            pltpu.VMEM((tokens + 16, wide), F32),
            pltpu.VMEM((2, 64, LANES), F32),
            pltpu.VMEM((2, 2, 2, 2, 2, half, LANES), BF16),
            pltpu.VMEM((2, 2, 2, 2, half, LANES), BF16),
            pltpu.VMEM((n, 2, 2, half, LANES), BF16),
            pltpu.VMEM((n, 2, half, LANES), BF16),
            pltpu.VMEM((n, half, LANES), BF16),
            pltpu.VMEM((n, 3 * (half // 4), LANES), BF16),
            pltpu.VMEM((far_chunks, far, half // 4, LANES), BF16),
            dma((ticks, 2)),
            dma((5, 2)),
            dma((10,)),
            dma((images,)),
            dma((3,)), dma((3,)),
            dma((ticks, 6)), dma((ticks, 6)),
            dma((2, 2)), dma((2, 2)),
            dma((RING,)), dma((RING,)),
            dma((n,)), dma((n,)),
            dma((n,)), dma((n,)),
            dma((n,)), dma((n,)),
            dma((n,)), dma((n,)),
            dma((len(STRAIGHT),)), dma((len(STRAIGHT),)),
            dma((n,)), dma((n,)),
            dma((n,)), dma((n,)),
            dma((len(STRAIGHT),)), dma((len(STRAIGHT),)),
            dma((n,)),
            dma((n,)), dma((n,)),
            dma((n,)), dma((n,)),
            dma((far_chunks, far)), dma((far_chunks, far)),
        ],
        compiler_params=pltpu.CompilerParams(
            collective_id=0, has_side_effects=True, vmem_limit_bytes=63 * 2**20
        ),
        name="mixer_layer",
    )(
        patches, cotangent, gain_one, shift_one, token_in.T, token_bias, token_out, token_shift,
        gain_two, shift_two, channel_in, channel_bias, channel_out, channel_shift,
    )

    vmem = pl.BlockSpec(memory_space=pltpu.VMEM)
    shapes = (
        (token_half, patch), (token_half,), (token_half, patch), (patch,),
        (width,), (width,), (width,), (width,), (hidden_half,), (width,),
    )
    (
        mixed, inputs_grad, d_in, d_out, d_tin, d_tbias, d_tout, d_tshift,
        d_gain1, d_shift1, d_gain2, d_shift2, d_cbias, d_cshift,
    ) = pl.pallas_call(
        functools.partial(widen, (images, patch, width, token_half, chunks)),
        in_specs=[hbm] * 3,
        out_specs=(hbm,) * 4 + (vmem,) * len(shapes),
        out_shape=(
            jax.ShapeDtypeStruct((images, patch, width), BF16),
            jax.ShapeDtypeStruct((images, patch, width), F32),
            jax.ShapeDtypeStruct((width, hidden_half), F32),
            jax.ShapeDtypeStruct((hidden_half, width), F32),
        ) + tuple(jax.ShapeDtypeStruct(shape, F32) for shape in shapes),
        scratch_shapes=[
            pltpu.VMEM((2, chunks, 2, half, LANES), BF16),
            pltpu.VMEM((2, 2, last_half, LANES), BF16),
            pltpu.VMEM((width, hidden_half), F32),
            pltpu.VMEM((hidden_half, width), F32),
            pltpu.VMEM((images, patch, width), BF16),
            pltpu.VMEM((images, patch, width), F32),
            dma((2, chunks)), dma((2, chunks)), dma((2,)), dma((4, images)),
        ],
        compiler_params=pltpu.CompilerParams(vmem_limit_bytes=60 * 2**20),
        name="widen",
    )(summed, mixed, inputs_grad)
    return (
        mixed, inputs_grad, d_gain1, d_shift1, d_tin.T, d_tbias, d_tout, d_tshift,
        d_gain2, d_shift2, d_in, d_cbias, d_out, d_cshift,
    )


def solution(mesh):
    split = P(("dp", "mp"), None, None)
    columns, rows, vector = P(None, "mp"), P("mp", None), P("mp")
    return jax.shard_map(
        functools.partial(per_device, mesh.shape["dp"]),
        mesh=mesh,
        in_specs=(
            split, split, P(), P(), columns, vector, rows, P(), P(), P(), columns, vector, rows, P(),
        ),
        out_specs=(
            split, split, P(), P(), columns, vector, rows, P(), P(), P(), columns, vector, rows, P(),
        ),
        check_vma=False,
    )
```

```python
import functools

import jax
import jax.numpy as jnp
from jax import lax
from jax.experimental import pallas as pl
from jax.experimental.pallas import tpu as pltpu
from jax.sharding import PartitionSpec as P

MESH = pl.DeviceIdType.MESH
F32 = jnp.float32
BF16 = jnp.bfloat16
NT = (((1,), (1,)), ((), ()))
LANES = 128
RING = 4

STRAIGHT = (0, 2, 4, 8, 11, 12)
POINTS = (
    ("core_mp", ((0, 2), (2, 4), (3, 5), (4, 6), (5, 7), (6, 8), (8, 10), (9, 11), (11, 13))),
    ("core_both", ((1, 3), (7, 9), (10, 12))),
    ("mp", ((0, 6), (2, 8), (3, 10), (4, 12), (5, 13), (6, 16), (8, 17), (9, 19), (11, 22))),
    ("both", ((1, 7), (7, 12), (10, 15))),
    ("side", ((3, 13), (5, 17), (6, 18), (9, 21))),
    ("side_line", ((0, 10), (2, 11), (4, 16), (8, 20))),
    ("then_mp", ((1, 14), (7, 20), (10, 22))),
    ("low", ((3, 15), (1, 16), (5, 19), (6, 20), (7, 22), (9, 23))),
    ("high", ((3, 17), (1, 19), (5, 21), (6, 23))),
    ("line", ((0, 13), (2, 14), (4, 18), (8, 22))),
    ("high_spread", ((3, 19), (1, 21), (5, 23))),
    ("low_spread", ((3, 21),)),
    ("spread", ((0, 15), (2, 16), (4, 20))),
    ("side_spread", ((0, 18), (2, 19), (4, 22), (3, 23))),
    ("core_spread", ((0, 19), (2, 20), (4, 23))),
)
REST = (
    ("low_spread", 1), ("core_spread", 3), ("high", 7), ("side_line", 11), ("core_mp", 12), ("low", 10),
    ("spread", 8), ("high_spread", 6), ("side_spread", 1), ("low_spread", 5), ("high", 9), ("core_spread", 1),
    ("high_spread", 7), ("mp", 12), ("side_spread", 8), ("line", 11), ("core_spread", 8), ("low_spread", 6),
    ("high", 10), ("side_spread", 5), ("high_spread", 9), ("low_spread", 7), ("core_spread", 5), ("side_line", 12),
    ("spread", 11), ("side_spread", 6), ("high_spread", 10), ("low_spread", 9), ("core_spread", 6), ("line", 12),
    ("side_spread", 7), ("core_spread", 7), ("low_spread", 10), ("side_spread", 11), ("core_spread", 11),
    ("spread", 12), ("side_spread", 9), ("core_spread", 9), ("side_spread", 10), ("core_spread", 10),
    ("side_spread", 12), ("core_spread", 12),
)


def dot(a, b):
    return jnp.dot(a, b, preferred_element_type=F32)


def dot_nt(a, b):
    return lax.dot_general(a, b, NT, preferred_element_type=F32)


def centre(values):
    centred = values - jnp.mean(values, -1, keepdims=True)
    return centred, lax.rsqrt(jnp.mean(centred * centred, -1, keepdims=True) + 1e-06)


def norm_back(grad, normed, scale, gain):
    scaled = grad * gain
    return scale * (
        scaled
        - jnp.mean(scaled, -1, keepdims=True)
        - normed * jnp.mean(scaled * normed, -1, keepdims=True)
    )


def gelu_parts(v):
    phi = 0.5 + 0.5 * lax.erf(v * 0.7071067811865476)
    return phi, phi + v * (0.3989422804014327 * jnp.exp(-0.5 * v * v))


def layer(
    sizes,
    patches, cotangent, gain_one, shift_one, token_in, token_bias, token_out, token_shift,
    gain_two, shift_two, channel_in, channel_bias, channel_out, channel_shift,
    mixed, inputs_grad, summed, hid_out, slope_out,
    wi, wo, vecs, cbs, cbo, tbs, tss, tins, touts, tw, twi_t, two_t, keep,
    dys, dys_t, u2s, u2s_t, u1s, chid, dcp, dtok,
    xs, ms, hid, slope, stats,
    row_acc, cb_acc, tin_acc, tout_acc, small,
    grads, from_core, acc, from_mp, from_x, from_z, from_far,
    load_sem, stage_sem, small_sem, grad_sem, tok_s, tok_r, w_s, w_r, wc_s, wc_r, c_s, c_r, g_s, line_s, l_sem, y_r, x_r, z_r, zh_r, zl_r,
    a_r, al_r, sl_r, xa_r, ca_r, far_s, far_r, hello,
):
    images, patch, width, token_half, hidden_half, ticks, dp_size, last_half = sizes
    rows = dys.shape[0]
    high = u1s.shape[1]
    step = hidden_half // ticks
    half = width // 2
    chunks = 2 * ticks
    eighth_in = width // 8

    dp = lax.axis_index("dp")
    mp = lax.axis_index("mp")
    core = lax.rem(dp, 2)
    side = lax.rem(lax.div(dp, 2), 2)
    near = lax.rem(lax.div(dp, 2), 4)
    line = lax.rem(lax.div(dp, 4), 4)
    part = core * 4 + near
    low = lax.rem(line, 2)

    to_mp = {"mp": 1 - mp}
    to_core = {"dp": dp + 1 - 2 * core}
    to_side = {"dp": dp + 2 - 4 * side}

    def near_of(r):
        return {"dp": dp + 2 * (lax.rem(near + r, 4) - near)}

    def line_of(r):
        return {"dp": dp + 4 * (lax.rem(line + r, 4) - line)}

    far_bits = []
    bit = 16
    while bit < dp_size:
        far_bits.append(bit)
        bit *= 2

    def far_of(i):
        b = far_bits[i]
        return {"dp": dp + b - 2 * b * lax.rem(lax.div(dp, b), 2)}

    def remote(src, dst, send, recv, device):
        return pltpu.make_async_remote_copy(
            src_ref=src, dst_ref=dst, send_sem=send, recv_sem=recv, device_id=device, device_id_type=MESH
        )

    def al(v, m):
        return pl.multiple_of(v, m)

    def own_loads(t):
        return (
            pltpu.make_async_copy(
                channel_in.at[:, pl.ds(al(t * step, step), step)],
                wi.at[:, pl.ds(al(t * 2 * step, step), step)],
                load_sem.at[t, 0],
            ),
            pltpu.make_async_copy(
                channel_out.at[pl.ds(al(t * step, step), step), :],
                wo.at[pl.ds(al(t * 2 * step, step), step), :],
                load_sem.at[t, 1],
            ),
        )

    def other_in(t, first, count):
        return wi.at[pl.ds(al(first, eighth_in), count), pl.ds(al(t * 2 * step + step, step), step)]

    def other_out(t, first, count):
        return wo.at[pl.ds(al(t * 2 * step + step + first, 16), count), :]

    which = side + core * (low - side)
    quarter_out = step // 4
    to_pair = {"dp": dp + (2 - 4 * side) * (1 - core) + (4 - 8 * low) * core}

    def gather_mp(t):
        first = core * 2 * quarter_out + which * quarter_out
        return (
            remote(
                channel_in.at[pl.ds(al(part * eighth_in, eighth_in), eighth_in), pl.ds(al(t * step, step), step)],
                other_in(t, part * eighth_in, eighth_in),
                w_s.at[t, 0], w_r.at[t, 0], to_mp,
            ),
            remote(
                channel_out.at[pl.ds(al(t * step + first, 16), quarter_out), :],
                other_out(t, first, quarter_out),
                w_s.at[t, 1], w_r.at[t, 1], to_mp,
            ),
        )

    def gather_near(t):
        a = other_in(t, part * eighth_in, eighth_in)
        b = other_out(t, core * 2 * quarter_out + which * quarter_out, quarter_out)
        copies = [remote(a, a, w_s.at[t, r - 1], w_r.at[t, r + 1], near_of(r)) for r in (1, 2, 3)]
        return copies + [remote(b, b, w_s.at[t, 3], w_r.at[t, 5], to_pair)]

    def gather_core(t):
        a = other_in(t, core * 4 * eighth_in, 4 * eighth_in)
        b = other_out(t, core * 2 * quarter_out, 2 * quarter_out)
        s = lax.rem(t, 2)
        return (
            remote(a, a, wc_s.at[s, 0], wc_r.at[s, 0], to_core),
            remote(b, b, wc_s.at[s, 1], wc_r.at[s, 1], to_core),
        )

    def token_mp():
        return (
            remote(
                tw.at[core, pl.ds(0, token_half)], tw.at[core, pl.ds(token_half, token_half)], tok_s.at[0], tok_r.at[0], to_mp
            ),
        )

    def bias_mp():
        return (remote(cbs, cbo, tok_s.at[1], tok_r.at[1], to_mp),)

    def token_core():
        ref = tw.at[core, pl.ds(token_half, token_half)]
        return (remote(ref, ref, tok_s.at[2], tok_r.at[2], to_core),)

    high_bit = lax.div(line, 2)
    to_low = {"dp": dp + 4 - 8 * low}
    to_high = {"dp": dp + 8 - 16 * high_bit}

    def rows_at(first, count):
        return pl.ds(al(first, 16), count)

    def core_copy(c, h):
        slot, q, i = lax.rem(lax.div(c, 2), 2), lax.rem(c, 2), lax.rem(c, RING)
        rng = pl.ds(0, h)
        return remote(
            grads.at[slot, 1 - core, q, :, :, rng], from_core.at[slot, q, :, :, rng], c_s.at[i], c_r.at[i], to_core
        )

    def mp_copy(c, h):
        rng = pl.ds(0, h)
        return remote(acc.at[c, 1, :, rng], from_mp.at[c, :, rng], g_s.at[0, c], y_r.at[c], to_mp)

    def side_copy(c, h):
        rng = pl.ds(0, h)
        return remote(acc.at[c, 0, 1 - side, rng], from_x.at[c, rng], g_s.at[0, c], x_r.at[c], to_side)

    def both_copy(c):
        return remote(acc.at[c, :, 1 - side], from_mp.at[c], g_s.at[0, c], x_r.at[c], to_side)

    def then_mp_copy(c):
        return remote(acc.at[c, 1, side], from_x.at[c], g_s.at[0, c], y_r.at[c], to_mp)

    def low_copy(c, h):
        n = h // 2
        src = acc.at[c, 0, side, rows_at((1 - low) * n, n)]
        return remote(src, from_z.at[c, pl.ds(0, n)], g_s.at[0, c], z_r.at[c], to_low)

    def high_copy(c, h):
        n = h // 4
        src = acc.at[c, 0, side, rows_at(low * 2 * n + (1 - high_bit) * n, n)]
        return remote(src, from_z.at[c, pl.ds(2 * n, n)], g_s.at[0, c], zh_r.at[c], to_high)

    def at_place(c, h):
        return rows_at(low * (h // 2) + high_bit * (h // 4), h // 4)

    def at_line(h, place):
        return rows_at(place * (h // 4), h // 4)

    def line_sems(c, d, first, second, third):
        return ((first.at[c], second.at[c], third.at[d])[r] for r in range(3))

    def line_copies(c, h, d):
        sends = line_sems(c, d, g_s.at[0], g_s.at[1], line_s)
        recvs = line_sems(c, d, z_r, zh_r, zl_r)
        return [
            remote(
                acc.at[c, 0, side, at_line(h, lax.rem(line + r, 4))],
                from_z.at[c, pl.ds((r - 1) * (h // 4), h // 4)], send, recv, line_of(r),
            )
            for r, send, recv in zip((1, 2, 3), sends, recvs)
        ]

    def sums_of(c, rng):
        return from_mp.at[c, 0, rng]

    def keep_copy(c, h):
        rng = pl.ds(0, h)
        return pltpu.make_async_copy(sums_of(c, rng), summed.at[core, c, side, rng], l_sem.at[c])

    def high_spread_copy(c, h):
        ref = sums_of(c, at_place(c, h))
        return remote(ref, ref, g_s.at[0, c], a_r.at[c], to_high)

    def low_spread_copy(c, h):
        ref = sums_of(c, rows_at(low * (h // 2), h // 2))
        return remote(ref, ref, g_s.at[0, c], al_r.at[c], to_low)

    def spread_copies(c, h, d):
        ref = sums_of(c, at_line(h, line))
        sends = line_sems(c, d, g_s.at[0], g_s.at[1], line_s)
        recvs = line_sems(c, d, a_r, al_r, sl_r)
        return [remote(ref, ref, send, recv, line_of(r)) for r, send, recv in zip((1, 2, 3), sends, recvs)]

    def side_spread_copy(c, h):
        rng = pl.ds(0, h)
        return remote(sums_of(c, rng), summed.at[core, c, side, rng], g_s.at[0, c], xa_r.at[c], to_side)

    def core_own_copy(c, h):
        rng = pl.ds(0, h)
        return remote(sums_of(c, rng), summed.at[core, c, side, rng], g_s.at[1, c], ca_r.at[0, c], to_core)

    def core_other_copy(c, h):
        ref = summed.at[core, c, 1 - side, pl.ds(0, h)]
        return remote(ref, ref, g_s.at[0, c], ca_r.at[1, c], to_core)

    def add(a, b):
        return (a.astype(F32) + b.astype(F32)).astype(BF16)

    def core_step(c, h, send):
        core_copy(c, h).wait()
        slot, q, rng = lax.rem(lax.div(c, 2), 2), lax.rem(c, 2), pl.ds(0, h)
        acc[c, 1, :, rng] = add(grads[slot, core, q, 1, :, rng], from_core[slot, q, 1, :, rng])
        if send is mp_copy:
            send(c, h).start()
        acc[c, 0, :, rng] = add(grads[slot, core, q, 0, :, rng], from_core[slot, q, 0, :, rng])
        if send is both_copy:
            send(c).start()

    def core_mp(c, h, d):
        core_step(c, h, mp_copy)

    def core_both(c, h, d):
        core_step(c, h, both_copy)

    def mp_step(c, h, d):
        mp_copy(c, h).wait()
        rng = pl.ds(0, h)
        acc[c, 0, 1 - side, rng] = add(acc[c, 0, 1 - side, rng], from_mp[c, 1 - side, rng])
        side_copy(c, h).start()
        acc[c, 0, side, rng] = add(acc[c, 0, side, rng], from_mp[c, side, rng])

    def side_step(c, h, d):
        side_copy(c, h).wait()
        rng = pl.ds(0, h)
        acc[c, 0, side, rng] = add(acc[c, 0, side, rng], from_x[c, rng])
        low_copy(c, h).start()

    def side_line(c, h, d):
        side_copy(c, h).wait()
        rng = pl.ds(0, h)
        acc[c, 0, side, rng] = add(acc[c, 0, side, rng], from_x[c, rng])
        for copy in line_copies(c, h, d):
            copy.start()

    def both_step(c, h, d):
        both_copy(c).wait()
        acc[c, 1, side] = add(acc[c, 1, side], from_mp[c, 1])
        then_mp_copy(c).start()
        acc[c, 0, side] = add(acc[c, 0, side], from_mp[c, 0])

    def then_mp_step(c, h, d):
        then_mp_copy(c).wait()
        acc[c, 0, side] = add(acc[c, 0, side], from_x[c])
        low_copy(c, h).start()

    def low_step(c, h, d):
        low_copy(c, h).wait()
        rng = rows_at(low * (h // 2), h // 2)
        acc[c, 0, side, rng] = add(acc[c, 0, side, rng], from_z[c, pl.ds(0, h // 2)])
        high_copy(c, h).start()

    def over_far(c, rng, count):
        for i in range(len(far_bits)):
            dst = from_far.at[c, i, pl.ds(0, count)]
            copy = remote(sums_of(c, rng), dst, far_s.at[c, i], far_r.at[c, i], far_of(i))
            copy.start()
            copy.wait()
            from_mp[c, 0, rng] = add(from_mp[c, 0, rng], from_far[c, i, pl.ds(0, count)])

    def high_step(c, h, d):
        high_copy(c, h).wait()
        rng = at_place(c, h)
        from_mp[c, 0, rng] = add(acc[c, 0, side, rng], from_z[c, pl.ds(h // 2, h // 4)])
        over_far(c, rng, h // 4)
        high_spread_copy(c, h).start()

    def high_spread_step(c, h, d):
        high_spread_copy(c, h).wait()
        low_spread_copy(c, h).start()

    def low_spread_step(c, h, d):
        low_spread_copy(c, h).wait()
        side_spread_copy(c, h).start()
        core_own_copy(c, h).start()
        keep_copy(c, h).start()

    def line_step(c, h, d):
        for copy in line_copies(c, h, d):
            copy.wait()
        rng = at_line(h, line)
        total = acc[c, 0, side, rng].astype(F32)
        for r in range(3):
            total = total + from_z[c, pl.ds(r * (h // 4), h // 4)].astype(F32)
        from_mp[c, 0, rng] = total.astype(BF16)
        over_far(c, rng, h // 4)
        for copy in spread_copies(c, h, d):
            copy.start()

    def spread_step(c, h, d):
        for copy in spread_copies(c, h, d):
            copy.wait()
        side_spread_copy(c, h).start()
        core_own_copy(c, h).start()
        keep_copy(c, h).start()

    def side_spread_step(c, h, d):
        side_spread_copy(c, h).wait()
        core_other_copy(c, h).start()

    def core_spread_step(c, h, d):
        core_own_copy(c, h).wait()
        keep_copy(c, h).wait()
        core_other_copy(c, h).wait()

    steps = {
        "core_mp": core_mp, "core_both": core_both, "mp": mp_step, "side": side_step, "side_line": side_line, "both": both_step,
        "then_mp": then_mp_step, "low": low_step, "high": high_step, "high_spread": high_spread_step,
        "low_spread": low_spread_step, "line": line_step, "spread": spread_step,
        "side_spread": side_spread_step, "core_spread": core_spread_step,
    }

    def point(p, places):
        for name, entries in POINTS:
            here = [(c, at) for c, at in entries if at in places]
            if here:
                now = [(p == at).astype(jnp.int32) for _, at in here]
                c = sum(c * one for (c, _), one in zip(here, now))
                d = sum(STRAIGHT.index(c) * one for (c, _), one in zip(here, now) if c in STRAIGHT)

                @pl.when(sum(now) > 0)
                def _(c=c, d=d, name=name):
                    steps[name](c, half, d)

    barrier = pltpu.get_barrier_semaphore()
    to_mid = {"dp": dp + 4 * (3 - 2 * line)}
    is_mid = lax.rem(lax.div(line + 1, 2), 2)
    greet = [to_mp, to_core, to_side, to_low] + [far_of(i) for i in range(len(far_bits))]
    for device in greet:
        pl.semaphore_signal(barrier, inc=1, device_id=device, device_id_type=MESH)

    @pl.when(is_mid == 1)
    def _():
        pl.semaphore_signal(barrier, inc=1, device_id=to_mid, device_id_type=MESH)

    def tell(i, device):
        pl.semaphore_signal(hello.at[i], inc=1, device_id=device, device_id_type=MESH)

    def first_word():
        tell(0, to_side)
        tell(1, to_low)

        @pl.when(is_mid == 1)
        def _():
            tell(2, to_mid)

    def second_word():
        for i in (0, 1):
            pl.semaphore_wait(hello.at[i], 1)

        @pl.when(is_mid == 1)
        def _():
            pl.semaphore_wait(hello.at[2], 1)

        tell(3, to_low)

    def last_word():
        pl.semaphore_wait(hello.at[3], 1)


    def patch_copy(b):
        return pltpu.make_async_copy(patches.at[b], xs.at[lax.rem(b, 2)], stage_sem.at[0, lax.rem(b, 2)])

    def cot_copy(b):
        return pltpu.make_async_copy(cotangent.at[b], ms.at[lax.rem(b, 2)], stage_sem.at[1, lax.rem(b, 2)])

    def hid_save(b):
        s = lax.rem(b, 2)
        return (
            pltpu.make_async_copy(hid.at[s, pl.ds(0, 2 * token_half)], hid_out.at[b], stage_sem.at[2, s]),
            pltpu.make_async_copy(slope.at[s], slope_out.at[b], stage_sem.at[3, s]),
        )

    def hid_load(b):
        s = lax.rem(b, 2)
        return (
            pltpu.make_async_copy(hid_out.at[b], hid.at[s, pl.ds(0, 2 * token_half)], stage_sem.at[2, s]),
            pltpu.make_async_copy(slope_out.at[b], slope.at[s], stage_sem.at[3, s]),
        )

    def grad_save(b):
        return pltpu.make_async_copy(keep.at[b], inputs_grad.at[b], grad_sem.at[b])

    def mixed_save(b):
        s = lax.rem(b, 2)
        return pltpu.make_async_copy(ms.at[s], mixed.at[b], stage_sem.at[4, s])

    def both(copies, what):
        for copy in copies:
            getattr(copy, what)()

    def small_loads():
        pairs = [(token_in, tins), (token_out, touts), (token_bias, tbs), (token_shift, tss), (channel_bias, cbs.at[0])]
        vectors = (gain_one, shift_one, gain_two, shift_two, channel_shift)
        pairs += [(ref, vecs.at[i]) for i, ref in enumerate(vectors)]
        return [pltpu.make_async_copy(src, dst, small_sem.at[i]) for i, (src, dst) in enumerate(pairs)]

    both(small_loads(), "start")
    for b in (0, 1):
        patch_copy(b).start()
        cot_copy(b).start()

    wide = tw.shape[2]
    twi, two = tw.at[0], tw.at[1]

    def three(row):
        hi = row.astype(BF16).astype(F32)
        mid = (row - hi).astype(BF16).astype(F32)
        return hi, mid, row - hi - mid

    twi[pl.ds(0, token_half), :] = jnp.zeros((token_half, wide), BF16)
    two[pl.ds(0, token_half), :] = jnp.zeros((token_half, wide), BF16)
    at_row = lax.broadcasted_iota(jnp.int32, (16, wide), 0)
    at_lane = lax.broadcasted_iota(jnp.int32, (token_half, wide), 1)
    both(small_loads(), "wait")
    twi[pl.ds(0, token_half), pl.ds(0, patch)] = tins[...]
    two[pl.ds(0, token_half), pl.ds(0, patch)] = touts[...]
    padded = jnp.zeros((1, wide - token_half), F32)
    bias_row = jnp.concatenate([tbs[...].reshape(1, token_half), padded], axis=1)
    column = jnp.broadcast_to(bias_row, (LANES, wide)).T[:token_half, 0:1]
    filled = twi[pl.ds(0, token_half), :].astype(F32)
    for i, value in enumerate(three(column)):
        filled = jnp.where(at_lane == patch + i, value, filled)
    twi[pl.ds(0, token_half), :] = filled.astype(BF16)
    shift_row = jnp.concatenate([tss[...].reshape(1, patch), jnp.zeros((1, wide - patch), F32)], axis=1)
    extra = jnp.zeros((16, wide), F32)
    for i, value in enumerate(three(shift_row)):
        extra = jnp.where(at_row == i, value, extra)
    tokens = 2 * token_half
    two[pl.ds(tokens, 16), :] = extra.astype(BF16)

    pl.semaphore_wait(barrier, len(greet) + is_mid)
    both(token_mp(), "start")
    both(gather_mp(0), "start")
    first_word()
    both(bias_mp(), "start")

    def start_own(t, _):
        both(own_loads(t), "start")
        return 0

    lax.fori_loop(0, ticks, start_own, 0)

    dys[...] = jnp.zeros_like(dys)
    u2s[...] = jnp.zeros_like(u2s)
    dtok[...] = jnp.zeros_like(dtok)
    rest_rows = rows - images * high
    if rest_rows:
        chid[pl.ds(images * high, rest_rows), :] = jnp.zeros((rest_rows, chid.shape[1]), BF16)
        dcp[pl.ds(images * high, rest_rows), :] = jnp.zeros((rest_rows, dcp.shape[1]), BF16)
    row_acc[...] = jnp.zeros_like(row_acc)
    tin_acc[...] = jnp.zeros_like(tin_acc)
    tout_acc[...] = jnp.zeros_like(tout_acc)
    small[...] = jnp.zeros_like(small)
    u2s_t[pl.ds(width, 16), :] = jnp.ones((16, rows), BF16)
    for s in (0, 1):
        hid[s, pl.ds(tokens, 16), :] = jnp.ones((16, width), BF16)

    below = lax.broadcasted_iota(jnp.int32, (high, width), 0)
    ones = jnp.where(jnp.logical_and(below >= patch, below < patch + 3), 1.0, 0.0).astype(BF16)
    for b in range(images):
        u1s[b] = ones

    gain1, shift1, gain2, shift2 = (vecs[i : i + 1] for i in range(4))

    def first_norm(b, _):
        s = lax.rem(b, 2)
        patch_copy(b).wait()
        x = xs[s].astype(F32)

        @pl.when(b + 2 < images)
        def _():
            patch_copy(b + 2).start()

        keep[b] = x
        mean = jnp.mean(x, -1, keepdims=True)
        centred = x - mean
        scale = lax.rsqrt(jnp.mean(centred * centred, -1, keepdims=True) + 1e-06)
        stats[b, :, 0:1] = mean
        stats[b, :, 1:2] = scale
        u1s[b, pl.ds(0, patch), :] = (centred * scale * gain1 + shift1).astype(BF16)
        pre = dot(twi[pl.ds(0, token_half), pl.ds(0, high)], u1s[b])
        phi, deriv = gelu_parts(pre)
        at = pl.ds(al(b * token_half, 16), token_half)
        chid[at, pl.ds(0, width)] = (pre * phi).astype(BF16)
        dcp[at, pl.ds(0, width)] = deriv.astype(BF16)
        cot_copy(b).wait()
        value = ms[s]

        @pl.when(b + 2 < images)
        def _():
            cot_copy(b + 2).start()

        @pl.when(b + 1 < ticks)
        def _():
            both(gather_mp(b + 1), "start")

        @pl.when(b == images // 2)
        def _():
            both(token_mp(), "wait")
            both(token_core(), "start")

        dys[pl.ds(al(b * high, 16), patch), :] = value
        row_acc[pl.ds(4, 1), :] += jnp.sum(value.astype(F32), 0, keepdims=True)
        return 0

    lax.fori_loop(0, images, first_norm, 0)
    for t in range(images + 1, ticks):
        both(gather_mp(t), "start")

    def turn_dy(j, _):
        at = pl.ds(al(j * LANES, LANES), LANES)
        dys_t[:, at] = dys[at, :].T
        return 0

    lax.fori_loop(0, rows // LANES, turn_dy, 0)

    second_word()
    both(token_core(), "wait")
    two_t[...] = two[...].T

    def token_forward(b, _):
        s = lax.rem(b, 2)
        pre = dot(twi[pl.ds(token_half, token_half), pl.ds(0, high)], u1s[b])
        phi, deriv = gelu_parts(pre)

        @pl.when(b >= 2)
        def _():
            both(hid_save(b - 2), "wait")

        at = pl.ds(al(b * token_half, 16), token_half)
        hid[s, pl.ds(0, token_half), :] = chid[at, pl.ds(0, width)]
        slope[s, pl.ds(0, token_half), :] = dcp[at, pl.ds(0, width)]
        hid[s, pl.ds(token_half, token_half), :] = (pre * phi).astype(BF16)
        slope[s, pl.ds(token_half, token_half), :] = deriv.astype(BF16)
        both(hid_save(b), "start")
        x1 = keep[b] + dot(two_t[pl.ds(0, high), :], hid[s])[:patch]
        keep[b] = x1
        mean = jnp.mean(x1, -1, keepdims=True)
        centred = x1 - mean
        scale = lax.rsqrt(jnp.mean(centred * centred, -1, keepdims=True) + 1e-06)
        stats[b, :, 2:3] = mean
        stats[b, :, 3:4] = scale
        u2s[pl.ds(al(b * high, 16), patch), :] = (centred * scale * gain2 + shift2).astype(BF16)

        for t, when in enumerate((0, images // 2, images - 1)):

            @pl.when(b == when)
            def _(t=t):
                both(gather_mp(t), "wait")
                both(gather_near(t), "start")

        return 0

    lax.fori_loop(0, images, token_forward, 0)
    both(gather_near(0), "wait")
    both(gather_core(0), "start")
    both(bias_mp(), "wait")
    last_word()

    def turn_u2(j, _):
        at = pl.ds(al(j * LANES, LANES), LANES)
        u2s_t[pl.ds(0, width), at] = u2s[at, :].T
        return 0

    lax.fori_loop(0, rows // LANES, turn_u2, 0)
    for b in range(max(images - 2, 0), images):
        both(hid_save(b), "wait")

    live = images * high
    tiles = 2 if live % 32 == 0 else 1
    tall = live // tiles

    def channel(t, _):
        both(own_loads(t), "wait")
        both(gather_core(t), "wait")
        at = pl.ds(al(t * 2 * step, 2 * step), 2 * step)
        weight_in, weight_out = wi[:, at], wo[at, :]
        here = pl.ds(al(t * step, step), step)
        bias = jnp.concatenate([cbs[:, here], cbo[:, here]], axis=1)
        for i in range(tiles):
            rng = pl.ds(i * tall, tall)
            pre = dot(u2s[rng, :], weight_in) + bias
            back = dot_nt(dys[rng, :], weight_out)
            phi, deriv = gelu_parts(pre)
            chid[rng, at] = (pre * phi).astype(BF16)
            dcp[rng, at] = (back * deriv).astype(BF16)

        @pl.when(t + 3 < ticks)
        def _():
            both(gather_mp(t + 3), "wait")
            both(gather_near(t + 3), "start")

        @pl.when(t + 1 < ticks)
        def _():
            both(gather_near(t + 1), "wait")
            both(gather_core(t + 1), "start")

        point(2 * t, range(0, chunks, 2))
        slot = lax.rem(t, 2)
        grad_in = dot(u2s_t[...], dcp[:, at])
        cb_acc[:, at] = grad_in[width : width + 1]
        grad_in = grad_in[:width].astype(BF16)
        grad_out = dot(dys_t[...], chid[:, at]).astype(BF16)
        for m, value in ((0, grad_in), (1, grad_out)):
            for o in (0, 1):
                for q in (0, 1):
                    first = o * step + q * LANES
                    for k in (0, 1):
                        grads[slot, m, q, o, k] = value[k * half : (k + 1) * half, first : first + LANES]
        point(2 * t + 1, range(1, chunks, 2))
        core_copy(2 * t, width // 2).start()
        core_copy(2 * t + 1, width // 2).start()
        return 0

    lax.fori_loop(0, ticks, channel, 0)

    both(hid_load(0), "start")
    patch_copy(0).start()
    twi_t[...] = twi[pl.ds(0, tokens), :].T
    gain1, gain2, out_shift = vecs[0:1], vecs[2:3], vecs[4:5]

    def backward(b, _):
        s = lax.rem(b, 2)
        rng = pl.ds(al(b * high, 16), high)

        @pl.when(b + 1 < images)
        def _():
            both(hid_load(b + 1), "start")
            patch_copy(b + 1).start()

        @pl.when(b >= 2)
        def _():
            mixed_save(b - 2).wait()

        x1 = keep[b]
        ms[s] = (x1 + dot(chid[rng, :], wo[...])[:patch] + out_shift).astype(BF16)
        mixed_save(b).start()
        du2 = dot_nt(dcp[rng, :], wi[...])[:patch]
        n2 = (x1 - stats[b, :, 2:3]) * stats[b, :, 3:4]
        row_acc[pl.ds(2, 1), :] += jnp.sum(du2 * n2, 0, keepdims=True)
        row_acc[pl.ds(3, 1), :] += jnp.sum(du2, 0, keepdims=True)
        dy = dys[pl.ds(al(b * high, 16), patch), :].astype(F32)
        dx1 = dy + norm_back(du2, n2, stats[b, :, 3:4], gain2)
        keep[b] = dx1
        dtok[pl.ds(0, patch), :] = dx1.astype(BF16)
        point(chunks + 2 * b, range(chunks, chunks + 2 * images, 2))
        both(hid_load(b), "wait")
        dtk = dtok[...]
        hidden = hid[s]
        tout_acc[:, pl.ds(0, high)] += dot_nt(hidden, dtk)
        dpre = (dot(two[pl.ds(0, tokens), pl.ds(0, high)], dtk) * slope[s].astype(F32)).astype(BF16)
        tin_acc[:, pl.ds(0, high)] += dot_nt(dpre, u1s[b])
        du1 = dot(twi_t[pl.ds(0, high), :], dpre)[:patch]
        patch_copy(b).wait()
        n1 = (xs[s].astype(F32) - stats[b, :, 0:1]) * stats[b, :, 1:2]
        row_acc[pl.ds(0, 1), :] += jnp.sum(du1 * n1, 0, keepdims=True)
        row_acc[pl.ds(1, 1), :] += jnp.sum(du1, 0, keepdims=True)
        keep[b] = keep[b] + norm_back(du1, n1, stats[b, :, 1:2], gain1)
        grad_save(b).start()
        point(chunks + 2 * b + 1, range(chunks + 1, chunks + 2 * images, 2))
        return 0

    lax.fori_loop(0, images, backward, 0)

    blocks = width // LANES
    for o in (0, 1):
        for v in range(5):
            for j in range(blocks):
                small[o, pl.ds(v * blocks + j, 1), :] = row_acc[pl.ds(v, 1), pl.ds(j * LANES, LANES)]
        for j in range(2):
            small[o, pl.ds(5 * blocks + j, 1), :] = tout_acc[pl.ds(tokens, 1), pl.ds(j * LANES, LANES)]
        for c in range(chunks):
            first = (c // 2) * 2 * step + o * step + (c % 2) * LANES
            small[o, pl.ds(5 * blocks + 2 + c, 1), :] = cb_acc[pl.ds(0, 1), pl.ds(first, LANES)]
    last_slot = ticks % 2
    for o in (0, 1):
        for m, total in ((0, tin_acc), (1, tout_acc)):
            for j in range(2):
                grads[last_slot, m, 0, o, j, pl.ds(0, token_half), :] = total[
                    pl.ds(o * token_half, token_half), pl.ds(j * LANES, LANES)
                ].astype(BF16)
        grads[last_slot, 0, 0, o, 0, pl.ds(token_half, small.shape[1]), :] = small[o].astype(BF16)
    core_copy(chunks, last_half).start()
    for name, c in REST:
        steps[name](c, half if c < chunks else last_half, STRAIGHT.index(c) if c in STRAIGHT else 0)
    for b in range(max(images - 2, 0), images):
        mixed_save(b).wait()
    for b in range(images):
        grad_save(b).wait()


def widen(
    sizes, summed, mixed_in, grad_in,
    mixed, inputs_grad, d_in, d_out, d_tin, d_tbias, d_tout, d_tshift, d_gain1, d_shift1, d_gain2, d_shift2, d_cbias, d_cshift,
    sums, last, wide_in, wide_out, hold_mixed, hold_grad, in_sem, out_sem, last_sem, through_sem,
):
    images, patch, width, token_half, chunks = sizes

    def at(c):
        return pl.ds(c * LANES, LANES)

    loads = [[pltpu.make_async_copy(summed.at[m, c], sums.at[m, c], in_sem.at[m, c]) for m in (0, 1)] for c in range(chunks)]
    stores = [
        (
            pltpu.make_async_copy(wide_in.at[:, at(c)], d_in.at[:, at(c)], out_sem.at[0, c]),
            pltpu.make_async_copy(wide_out.at[at(c)], d_out.at[at(c)], out_sem.at[1, c]),
        )
        for c in range(chunks)
    ]
    load_last = [
        pltpu.make_async_copy(summed.at[m, chunks, :, pl.ds(0, last.shape[2])], last.at[m], last_sem.at[m]) for m in (0, 1)
    ]
    ins, outs = [], []
    for i, (src, hold, dst) in enumerate(((mixed_in, hold_mixed, mixed), (grad_in, hold_grad, inputs_grad))):
        for b in range(images):
            ins.append(pltpu.make_async_copy(src.at[b], hold.at[b], through_sem.at[i, b]))
            outs.append(pltpu.make_async_copy(hold.at[b], dst.at[b], through_sem.at[i + 2, b]))
    for pair in loads:
        for copy in pair:
            copy.start()
    for copy in load_last + ins:
        copy.start()
    through = iter(zip(ins, outs))
    for c in range(chunks):
        for copy in loads[c]:
            copy.wait()
        wide_in[:, c * LANES : (c + 1) * LANES] = sums[0, c].reshape(width, LANES).astype(F32)
        stores[c][0].start()
        wide_out[c * LANES : (c + 1) * LANES, :] = sums[1, c].reshape(width, LANES).T.astype(F32)
        stores[c][1].start()
        for arrived, leave in [pair for pair in (next(through, None),) if pair]:
            arrived.wait()
            leave.start()
    for arrived, leave in through:
        arrived.wait()
        leave.start()
    for copy in load_last:
        copy.wait()

    def token_block(m):
        halves = [last[m, j, pl.ds(0, token_half), :] for j in (0, 1)]
        return jnp.concatenate(halves, axis=1).astype(F32)

    grad = token_block(0)
    d_tin[...] = grad[:, :patch]
    d_tbias[...] = grad.T[patch : patch + 1].reshape(token_half)
    d_tout[...] = token_block(1)[:, :patch]
    blocks = width // LANES
    rows = last[0, 0, pl.ds(token_half, 64), :].astype(F32)

    def vector(first, count):
        return jnp.concatenate([rows[first + j : first + j + 1] for j in range(count)], axis=1)

    for v, ref in enumerate((d_gain1, d_shift1, d_gain2, d_shift2, d_cshift)):
        ref[...] = vector(v * blocks, blocks).reshape(width)
    d_tshift[...] = vector(5 * blocks, 2)[:, :patch].reshape(patch)
    d_cbias[...] = vector(5 * blocks + 2, chunks).reshape(chunks * LANES)
    for pair in stores:
        for copy in pair:
            copy.wait()
    for copy in outs:
        copy.wait()


def per_device(
    dp_size,
    patches, cotangent, gain_one, shift_one, token_in, token_bias, token_out, token_shift,
    gain_two, shift_two, channel_in, channel_bias, channel_out, channel_shift,
):
    images, patch, width = patches.shape
    token_half = token_in.shape[1]
    hidden_half = channel_in.shape[1]
    step = 2 * LANES
    ticks = hidden_half // step
    chunks = 2 * ticks
    high = -(-(patch + 3) // 16) * 16
    rows = -(-images * high // LANES) * LANES
    wide = -(-patch // LANES) * LANES
    tokens = 2 * token_half
    far = max(sum(1 for b in range(4, 20) if 2**b < dp_size), 1)
    far_chunks = chunks + 1 if dp_size > 16 else 1
    last_half = -(-(token_half + 64) // 64) * 64
    sizes = (images, patch, width, token_half, hidden_half, ticks, dp_size, last_half)
    hbm = pl.BlockSpec(memory_space=pl.ANY)
    n = chunks + 1
    half = width // 2
    dma = pltpu.SemaphoreType.DMA
    mixed, inputs_grad, summed, _, _ = pl.pallas_call(
        functools.partial(layer, sizes),
        out_shape=(
            jax.ShapeDtypeStruct((images, patch, width), BF16),
            jax.ShapeDtypeStruct((images, patch, width), F32),
            jax.ShapeDtypeStruct((2, n, 2, half, LANES), BF16),
            jax.ShapeDtypeStruct((images, tokens, width), BF16),
            jax.ShapeDtypeStruct((images, tokens, width), BF16),
        ),
        in_specs=[hbm] * 14,
        out_specs=(hbm,) * 5,
        scratch_shapes=[
            pltpu.VMEM((width, 2 * hidden_half), BF16),
            pltpu.VMEM((2 * hidden_half, width), BF16),
            pltpu.VMEM((8, width), F32),
            pltpu.VMEM((1, hidden_half), F32),
            pltpu.VMEM((1, hidden_half), F32),
            pltpu.VMEM((token_half,), F32),
            pltpu.VMEM((patch,), F32),
            pltpu.VMEM((token_half, patch), BF16),
            pltpu.VMEM((token_half, patch), BF16),
            pltpu.VMEM((2, tokens + 16, wide), BF16),
            pltpu.VMEM((wide, tokens), BF16),
            pltpu.VMEM((wide, tokens + 16), BF16),
            pltpu.VMEM((images, patch, width), F32),
            pltpu.VMEM((rows, width), BF16),
            pltpu.VMEM((width, rows), BF16),
            pltpu.VMEM((rows, width), BF16),
            pltpu.VMEM((width + 16, rows), BF16),
            pltpu.VMEM((images, high, width), BF16),
            pltpu.VMEM((rows, 2 * hidden_half), BF16),
            pltpu.VMEM((rows, 2 * hidden_half), BF16),
            pltpu.VMEM((high, width), BF16),
            pltpu.VMEM((2, patch, width), BF16),
            pltpu.VMEM((2, patch, width), BF16),
            pltpu.VMEM((2, tokens + 16, width), BF16),
            pltpu.VMEM((2, tokens, width), BF16),
            pltpu.VMEM((images, patch, 4), F32),
            pltpu.VMEM((8, width), F32),
            pltpu.VMEM((1, 2 * hidden_half), F32),
            pltpu.VMEM((tokens, wide), F32),
            pltpu.VMEM((tokens + 16, wide), F32),
            pltpu.VMEM((2, 64, LANES), F32),
            pltpu.VMEM((2, 2, 2, 2, 2, half, LANES), BF16),
            pltpu.VMEM((2, 2, 2, 2, half, LANES), BF16),
            pltpu.VMEM((n, 2, 2, half, LANES), BF16),
            pltpu.VMEM((n, 2, half, LANES), BF16),
            pltpu.VMEM((n, half, LANES), BF16),
            pltpu.VMEM((n, 3 * (half // 4), LANES), BF16),
            pltpu.VMEM((far_chunks, far, half // 4, LANES), BF16),
            dma((ticks, 2)),
            dma((5, 2)),
            dma((10,)),
            dma((images,)),
            dma((3,)), dma((3,)),
            dma((ticks, 4)), dma((ticks, 6)),
            dma((2, 2)), dma((2, 2)),
            dma((RING,)), dma((RING,)),
            dma((2, n)), dma((len(STRAIGHT),)), dma((n,)),
            dma((n,)), dma((n,)), dma((n,)), dma((n,)), dma((len(STRAIGHT),)),
            dma((n,)), dma((n,)), dma((len(STRAIGHT),)), dma((n,)), dma((2, n)),
            dma((far_chunks, far)), dma((far_chunks, far)),
            pltpu.SemaphoreType.REGULAR((4,)),
        ],
        compiler_params=pltpu.CompilerParams(
            collective_id=0, has_side_effects=True, vmem_limit_bytes=63 * 2**20
        ),
        name="mixer_layer",
    )(
        patches, cotangent, gain_one, shift_one, token_in.T, token_bias, token_out, token_shift,
        gain_two, shift_two, channel_in, channel_bias, channel_out, channel_shift,
    )

    vmem = pl.BlockSpec(memory_space=pltpu.VMEM)
    shapes = (
        (token_half, patch), (token_half,), (token_half, patch), (patch,),
        (width,), (width,), (width,), (width,), (hidden_half,), (width,),
    )
    (
        mixed, inputs_grad, d_in, d_out, d_tin, d_tbias, d_tout, d_tshift,
        d_gain1, d_shift1, d_gain2, d_shift2, d_cbias, d_cshift,
    ) = pl.pallas_call(
        functools.partial(widen, (images, patch, width, token_half, chunks)),
        in_specs=[hbm] * 3,
        out_specs=(hbm,) * 4 + (vmem,) * len(shapes),
        out_shape=(
            jax.ShapeDtypeStruct((images, patch, width), BF16),
            jax.ShapeDtypeStruct((images, patch, width), F32),
            jax.ShapeDtypeStruct((width, hidden_half), F32),
            jax.ShapeDtypeStruct((hidden_half, width), F32),
        ) + tuple(jax.ShapeDtypeStruct(shape, F32) for shape in shapes),
        scratch_shapes=[
            pltpu.VMEM((2, chunks, 2, half, LANES), BF16),
            pltpu.VMEM((2, 2, last_half, LANES), BF16),
            pltpu.VMEM((width, hidden_half), F32),
            pltpu.VMEM((hidden_half, width), F32),
            pltpu.VMEM((images, patch, width), BF16),
            pltpu.VMEM((images, patch, width), F32),
            dma((2, chunks)), dma((2, chunks)), dma((2,)), dma((4, images)),
        ],
        compiler_params=pltpu.CompilerParams(vmem_limit_bytes=60 * 2**20),
        name="widen",
    )(summed, mixed, inputs_grad)
    return (
        mixed, inputs_grad, d_gain1, d_shift1, d_tin.T, d_tbias, d_tout, d_tshift,
        d_gain2, d_shift2, d_in, d_cbias, d_out, d_cshift,
    )


def solution(mesh):
    split = P(("dp", "mp"), None, None)
    columns, rows, vector = P(None, "mp"), P("mp", None), P("mp")
    return jax.shard_map(
        functools.partial(per_device, mesh.shape["dp"]),
        mesh=mesh,
        in_specs=(
            split, split, P(), P(), columns, vector, rows, P(), P(), P(), columns, vector, rows, P(),
        ),
        out_specs=(
            split, split, P(), P(), columns, vector, rows, P(), P(), P(), columns, vector, rows, P(),
        ),
        check_vma=False,
    )
```

```python
import functools

import jax
import jax.numpy as jnp
from jax import lax
from jax.experimental import pallas as pl
from jax.experimental.pallas import tpu as pltpu
from jax.sharding import PartitionSpec as P

MESH = pl.DeviceIdType.MESH
F32 = jnp.float32
BF16 = jnp.bfloat16
NT = (((1,), (1,)), ((), ()))
LANES = 128
RING = 4

STRAIGHT = (4, 5, 8, 9, 11, 12)
POINTS = (
    ("core_mp", ((0, 2), (2, 4), (3, 5), (4, 6), (5, 7), (6, 8), (8, 10), (9, 11), (11, 13))),
    ("core_both", ((1, 3), (7, 9), (10, 12))),
    ("mp", ((0, 6), (2, 7), (3, 10), (4, 11), (5, 13), (6, 16), (8, 17), (9, 19), (11, 21))),
    ("both", ((1, 7), (7, 12), (10, 16))),
    ("side", ((0, 10), (2, 11), (3, 13), (6, 18))),
    ("side_line", ((4, 14), (5, 17), (8, 19), (9, 21))),
    ("then_mp", ((1, 14), (7, 19), (10, 23))),
    ("low", ((0, 12), (2, 13), (3, 15), (1, 16), (6, 20), (7, 22))),
    ("high", ((0, 14), (2, 15), (3, 17), (1, 18), (6, 23))),
    ("line", ((4, 16), (5, 19), (8, 21))),
    ("high_spread", ((0, 16), (2, 17), (3, 20), (1, 21))),
    ("low_spread", ((0, 18), (2, 20), (3, 23))),
    ("spread", ((4, 20), (5, 22))),
    ("side_spread", ((0, 20), (2, 22), (4, 23))),
    ("core_spread", ((0, 21), (2, 23))),
)
REST = (
    ("side_line", 11), ("low_spread", 1), ("core_mp", 12), ("core_spread", 4), ("line", 9), ("side_spread", 5),
    ("spread", 8), ("low", 10), ("core_spread", 5), ("high_spread", 6), ("high", 7), ("line", 11),
    ("side_spread", 3), ("mp", 12), ("spread", 9), ("side_spread", 1), ("core_spread", 3), ("high", 10),
    ("core_spread", 1), ("low_spread", 6), ("high_spread", 7), ("side_spread", 8), ("side_line", 12),
    ("core_spread", 8), ("spread", 11), ("high_spread", 10), ("side_spread", 9), ("low_spread", 7),
    ("side_spread", 6), ("line", 12), ("low_spread", 10), ("side_spread", 11), ("core_spread", 9), ("spread", 12),
    ("core_spread", 6), ("side_spread", 7), ("side_spread", 10), ("core_spread", 7), ("side_spread", 12),
    ("core_spread", 11), ("core_spread", 10), ("core_spread", 12),
)


def dot(a, b):
    return jnp.dot(a, b, preferred_element_type=F32)


def dot_nt(a, b):
    return lax.dot_general(a, b, NT, preferred_element_type=F32)


def centre(values):
    centred = values - jnp.mean(values, -1, keepdims=True)
    return centred, lax.rsqrt(jnp.mean(centred * centred, -1, keepdims=True) + 1e-06)


def norm_back(grad, normed, scale, gain):
    scaled = grad * gain
    return scale * (
        scaled
        - jnp.mean(scaled, -1, keepdims=True)
        - normed * jnp.mean(scaled * normed, -1, keepdims=True)
    )


def gelu_parts(v):
    phi = 0.5 + 0.5 * lax.erf(v * 0.7071067811865476)
    return phi, phi + v * (0.3989422804014327 * jnp.exp(-0.5 * v * v))


def layer(
    sizes,
    patches, cotangent, gain_one, shift_one, token_in, token_bias, token_out, token_shift,
    gain_two, shift_two, channel_in, channel_bias, channel_out, channel_shift,
    mixed, inputs_grad, summed, hid_out, slope_out,
    wi, wo, vecs, cbs, cbo, tbs, tss, tins, touts, tw, twi_t, two_t, keep,
    dys, dys_t, u2s, u2s_t, u1s, chid, dcp, dtok,
    xs, ms, hid, slope, stats,
    row_acc, cb_acc, tin_acc, tout_acc, small,
    grads, from_core, acc, from_mp, from_x, from_z, from_far,
    load_sem, stage_sem, small_sem, grad_sem, tok_s, tok_r, w_s, w_r, wc_s, wc_r, c_s, c_r, g_s, line_s, l_sem, y_r, x_r, z_r, zh_r, zl_r,
    a_r, al_r, sl_r, xa_r, ca_r, far_s, far_r, hello,
):
    images, patch, width, token_half, hidden_half, ticks, dp_size, last_half = sizes
    rows = dys.shape[0]
    high = u1s.shape[1]
    step = hidden_half // ticks
    half = width // 2
    chunks = 2 * ticks
    eighth_in = width // 8

    dp = lax.axis_index("dp")
    mp = lax.axis_index("mp")
    core = lax.rem(dp, 2)
    side = lax.rem(lax.div(dp, 2), 2)
    near = lax.rem(lax.div(dp, 2), 4)
    line = lax.rem(lax.div(dp, 4), 4)
    part = core * 4 + near
    low = lax.rem(line, 2)

    to_mp = {"mp": 1 - mp}
    to_core = {"dp": dp + 1 - 2 * core}
    to_side = {"dp": dp + 2 - 4 * side}

    def near_of(r):
        return {"dp": dp + 2 * (lax.rem(near + r, 4) - near)}

    def line_of(r):
        return {"dp": dp + 4 * (lax.rem(line + r, 4) - line)}

    far_bits = []
    bit = 16
    while bit < dp_size:
        far_bits.append(bit)
        bit *= 2

    def far_of(i):
        b = far_bits[i]
        return {"dp": dp + b - 2 * b * lax.rem(lax.div(dp, b), 2)}

    def remote(src, dst, send, recv, device):
        return pltpu.make_async_remote_copy(
            src_ref=src, dst_ref=dst, send_sem=send, recv_sem=recv, device_id=device, device_id_type=MESH
        )

    def al(v, m):
        return pl.multiple_of(v, m)

    def own_loads(t):
        return (
            pltpu.make_async_copy(
                channel_in.at[:, pl.ds(al(t * step, step), step)],
                wi.at[:, pl.ds(al(t * 2 * step, step), step)],
                load_sem.at[t, 0],
            ),
            pltpu.make_async_copy(
                channel_out.at[pl.ds(al(t * step, step), step), :],
                wo.at[pl.ds(al(t * 2 * step, step), step), :],
                load_sem.at[t, 1],
            ),
        )

    def other_in(t, first, count):
        return wi.at[pl.ds(al(first, eighth_in), count), pl.ds(al(t * 2 * step + step, step), step)]

    def other_out(t, first, count):
        return wo.at[pl.ds(al(t * 2 * step + step + first, 16), count), :]

    which = side + core * (low - side)
    quarter_out = step // 4
    to_pair = {"dp": dp + (2 - 4 * side) * (1 - core) + (4 - 8 * low) * core}

    def gather_mp(t):
        first = core * 2 * quarter_out + which * quarter_out
        return (
            remote(
                channel_in.at[pl.ds(al(part * eighth_in, eighth_in), eighth_in), pl.ds(al(t * step, step), step)],
                other_in(t, part * eighth_in, eighth_in),
                w_s.at[t, 0], w_r.at[t, 0], to_mp,
            ),
            remote(
                channel_out.at[pl.ds(al(t * step + first, 16), quarter_out), :],
                other_out(t, first, quarter_out),
                w_s.at[t, 1], w_r.at[t, 1], to_mp,
            ),
        )

    def gather_near(t):
        a = other_in(t, part * eighth_in, eighth_in)
        b = other_out(t, core * 2 * quarter_out + which * quarter_out, quarter_out)
        copies = [remote(a, a, w_s.at[t, r - 1], w_r.at[t, r + 1], near_of(r)) for r in (1, 2, 3)]
        return copies + [remote(b, b, w_s.at[t, 3], w_r.at[t, 5], to_pair)]

    def gather_core(t):
        a = other_in(t, core * 4 * eighth_in, 4 * eighth_in)
        b = other_out(t, core * 2 * quarter_out, 2 * quarter_out)
        s = lax.rem(t, 2)
        return (
            remote(a, a, wc_s.at[s, 0], wc_r.at[s, 0], to_core),
            remote(b, b, wc_s.at[s, 1], wc_r.at[s, 1], to_core),
        )

    def token_mp():
        return (
            remote(
                tw.at[core, pl.ds(0, token_half)], tw.at[core, pl.ds(token_half, token_half)], tok_s.at[0], tok_r.at[0], to_mp
            ),
        )

    def bias_mp():
        return (remote(cbs, cbo, tok_s.at[1], tok_r.at[1], to_mp),)

    def token_core():
        ref = tw.at[core, pl.ds(token_half, token_half)]
        return (remote(ref, ref, tok_s.at[2], tok_r.at[2], to_core),)

    high_bit = lax.div(line, 2)
    to_low = {"dp": dp + 4 - 8 * low}
    to_high = {"dp": dp + 8 - 16 * high_bit}

    def rows_at(first, count):
        return pl.ds(al(first, 16), count)

    def core_copy(c, h):
        slot, q, i = lax.rem(lax.div(c, 2), 2), lax.rem(c, 2), lax.rem(c, RING)
        rng = pl.ds(0, h)
        return remote(
            grads.at[slot, 1 - core, q, :, :, rng], from_core.at[slot, q, :, :, rng], c_s.at[i], c_r.at[i], to_core
        )

    def mp_copy(c, h):
        rng = pl.ds(0, h)
        return remote(acc.at[c, 1, :, rng], from_mp.at[c, :, rng], g_s.at[0, c], y_r.at[c], to_mp)

    def side_copy(c, h):
        rng = pl.ds(0, h)
        return remote(acc.at[c, 0, 1 - side, rng], from_x.at[c, rng], g_s.at[0, c], x_r.at[c], to_side)

    def both_copy(c):
        return remote(acc.at[c, :, 1 - side], from_mp.at[c], g_s.at[0, c], x_r.at[c], to_side)

    def then_mp_copy(c):
        return remote(acc.at[c, 1, side], from_x.at[c], g_s.at[0, c], y_r.at[c], to_mp)

    def low_copy(c, h):
        n = h // 2
        src = acc.at[c, 0, side, rows_at((1 - low) * n, n)]
        return remote(src, from_z.at[c, pl.ds(0, n)], g_s.at[0, c], z_r.at[c], to_low)

    def high_copy(c, h):
        n = h // 4
        src = acc.at[c, 0, side, rows_at(low * 2 * n + (1 - high_bit) * n, n)]
        return remote(src, from_z.at[c, pl.ds(2 * n, n)], g_s.at[0, c], zh_r.at[c], to_high)

    def at_place(c, h):
        return rows_at(low * (h // 2) + high_bit * (h // 4), h // 4)

    def at_line(h, place):
        return rows_at(place * (h // 4), h // 4)

    def line_sems(c, d, first, second, third):
        return ((first.at[c], second.at[c], third.at[d])[r] for r in range(3))

    def line_copies(c, h, d):
        sends = line_sems(c, d, g_s.at[0], g_s.at[1], line_s)
        recvs = line_sems(c, d, z_r, zh_r, zl_r)
        return [
            remote(
                acc.at[c, 0, side, at_line(h, lax.rem(line + r, 4))],
                from_z.at[c, pl.ds((r - 1) * (h // 4), h // 4)], send, recv, line_of(r),
            )
            for r, send, recv in zip((1, 2, 3), sends, recvs)
        ]

    def sums_of(c, rng):
        return from_mp.at[c, 0, rng]

    def keep_copy(c, h):
        rng = pl.ds(0, h)
        return pltpu.make_async_copy(sums_of(c, rng), summed.at[core, c, side, rng], l_sem.at[c])

    def high_spread_copy(c, h):
        ref = sums_of(c, at_place(c, h))
        return remote(ref, ref, g_s.at[0, c], a_r.at[c], to_high)

    def low_spread_copy(c, h):
        ref = sums_of(c, rows_at(low * (h // 2), h // 2))
        return remote(ref, ref, g_s.at[0, c], al_r.at[c], to_low)

    def spread_copies(c, h, d):
        ref = sums_of(c, at_line(h, line))
        sends = line_sems(c, d, g_s.at[0], g_s.at[1], line_s)
        recvs = line_sems(c, d, a_r, al_r, sl_r)
        return [remote(ref, ref, send, recv, line_of(r)) for r, send, recv in zip((1, 2, 3), sends, recvs)]

    def side_spread_copy(c, h):
        rng = pl.ds(0, h)
        return remote(sums_of(c, rng), summed.at[core, c, side, rng], g_s.at[0, c], xa_r.at[c], to_side)

    def core_own_copy(c, h):
        rng = pl.ds(0, h)
        return remote(sums_of(c, rng), summed.at[core, c, side, rng], g_s.at[1, c], ca_r.at[0, c], to_core)

    def core_other_copy(c, h):
        ref = summed.at[core, c, 1 - side, pl.ds(0, h)]
        return remote(ref, ref, g_s.at[0, c], ca_r.at[1, c], to_core)

    def add(a, b):
        return (a.astype(F32) + b.astype(F32)).astype(BF16)

    def core_step(c, h, send):
        core_copy(c, h).wait()
        slot, q, rng = lax.rem(lax.div(c, 2), 2), lax.rem(c, 2), pl.ds(0, h)
        acc[c, 1, :, rng] = add(grads[slot, core, q, 1, :, rng], from_core[slot, q, 1, :, rng])
        if send is mp_copy:
            send(c, h).start()
        acc[c, 0, :, rng] = add(grads[slot, core, q, 0, :, rng], from_core[slot, q, 0, :, rng])
        if send is both_copy:
            send(c).start()

    def core_mp(c, h, d):
        core_step(c, h, mp_copy)

    def core_both(c, h, d):
        core_step(c, h, both_copy)

    def mp_step(c, h, d):
        mp_copy(c, h).wait()
        rng = pl.ds(0, h)
        acc[c, 0, 1 - side, rng] = add(acc[c, 0, 1 - side, rng], from_mp[c, 1 - side, rng])
        side_copy(c, h).start()
        acc[c, 0, side, rng] = add(acc[c, 0, side, rng], from_mp[c, side, rng])

    def side_step(c, h, d):
        side_copy(c, h).wait()
        rng = pl.ds(0, h)
        acc[c, 0, side, rng] = add(acc[c, 0, side, rng], from_x[c, rng])
        low_copy(c, h).start()

    def side_line(c, h, d):
        side_copy(c, h).wait()
        rng = pl.ds(0, h)
        acc[c, 0, side, rng] = add(acc[c, 0, side, rng], from_x[c, rng])
        for copy in line_copies(c, h, d):
            copy.start()

    def both_step(c, h, d):
        both_copy(c).wait()
        acc[c, 1, side] = add(acc[c, 1, side], from_mp[c, 1])
        then_mp_copy(c).start()
        acc[c, 0, side] = add(acc[c, 0, side], from_mp[c, 0])

    def then_mp_step(c, h, d):
        then_mp_copy(c).wait()
        acc[c, 0, side] = add(acc[c, 0, side], from_x[c])
        low_copy(c, h).start()

    def low_step(c, h, d):
        low_copy(c, h).wait()
        rng = rows_at(low * (h // 2), h // 2)
        acc[c, 0, side, rng] = add(acc[c, 0, side, rng], from_z[c, pl.ds(0, h // 2)])
        high_copy(c, h).start()

    def over_far(c, rng, count):
        for i in range(len(far_bits)):
            dst = from_far.at[c, i, pl.ds(0, count)]
            copy = remote(sums_of(c, rng), dst, far_s.at[c, i], far_r.at[c, i], far_of(i))
            copy.start()
            copy.wait()
            from_mp[c, 0, rng] = add(from_mp[c, 0, rng], from_far[c, i, pl.ds(0, count)])

    def high_step(c, h, d):
        high_copy(c, h).wait()
        rng = at_place(c, h)
        from_mp[c, 0, rng] = add(acc[c, 0, side, rng], from_z[c, pl.ds(h // 2, h // 4)])
        over_far(c, rng, h // 4)
        high_spread_copy(c, h).start()

    def high_spread_step(c, h, d):
        high_spread_copy(c, h).wait()
        low_spread_copy(c, h).start()

    def low_spread_step(c, h, d):
        low_spread_copy(c, h).wait()
        side_spread_copy(c, h).start()
        core_own_copy(c, h).start()
        keep_copy(c, h).start()

    def line_step(c, h, d):
        for copy in line_copies(c, h, d):
            copy.wait()
        rng = at_line(h, line)
        total = acc[c, 0, side, rng].astype(F32)
        for r in range(3):
            total = total + from_z[c, pl.ds(r * (h // 4), h // 4)].astype(F32)
        from_mp[c, 0, rng] = total.astype(BF16)
        over_far(c, rng, h // 4)
        for copy in spread_copies(c, h, d):
            copy.start()

    def spread_step(c, h, d):
        for copy in spread_copies(c, h, d):
            copy.wait()
        side_spread_copy(c, h).start()
        core_own_copy(c, h).start()
        keep_copy(c, h).start()

    def side_spread_step(c, h, d):
        side_spread_copy(c, h).wait()
        core_other_copy(c, h).start()

    def core_spread_step(c, h, d):
        core_own_copy(c, h).wait()
        keep_copy(c, h).wait()
        core_other_copy(c, h).wait()

    steps = {
        "core_mp": core_mp, "core_both": core_both, "mp": mp_step, "side": side_step, "side_line": side_line, "both": both_step,
        "then_mp": then_mp_step, "low": low_step, "high": high_step, "high_spread": high_spread_step,
        "low_spread": low_spread_step, "line": line_step, "spread": spread_step,
        "side_spread": side_spread_step, "core_spread": core_spread_step,
    }

    def point(p, places):
        for name, entries in POINTS:
            here = [(c, at) for c, at in entries if at in places]
            if here:
                now = [(p == at).astype(jnp.int32) for _, at in here]
                c = sum(c * one for (c, _), one in zip(here, now))
                d = sum(STRAIGHT.index(c) * one for (c, _), one in zip(here, now) if c in STRAIGHT)

                @pl.when(sum(now) > 0)
                def _(c=c, d=d, name=name):
                    steps[name](c, half, d)

    barrier = pltpu.get_barrier_semaphore()
    to_mid = {"dp": dp + 4 * (3 - 2 * line)}
    is_mid = lax.rem(lax.div(line + 1, 2), 2)
    greet = [to_mp, to_core, to_side, to_low] + [far_of(i) for i in range(len(far_bits))]
    for device in greet:
        pl.semaphore_signal(barrier, inc=1, device_id=device, device_id_type=MESH)

    @pl.when(is_mid == 1)
    def _():
        pl.semaphore_signal(barrier, inc=1, device_id=to_mid, device_id_type=MESH)

    def tell(i, device):
        pl.semaphore_signal(hello.at[i], inc=1, device_id=device, device_id_type=MESH)

    def first_word():
        tell(0, to_side)
        tell(1, to_low)

        @pl.when(is_mid == 1)
        def _():
            tell(2, to_mid)

    def second_word():
        for i in (0, 1):
            pl.semaphore_wait(hello.at[i], 1)

        @pl.when(is_mid == 1)
        def _():
            pl.semaphore_wait(hello.at[2], 1)

        tell(3, to_low)

    def last_word():
        pl.semaphore_wait(hello.at[3], 1)


    def patch_copy(b):
        return pltpu.make_async_copy(patches.at[b], xs.at[lax.rem(b, 2)], stage_sem.at[0, lax.rem(b, 2)])

    def cot_copy(b):
        return pltpu.make_async_copy(cotangent.at[b], ms.at[lax.rem(b, 2)], stage_sem.at[1, lax.rem(b, 2)])

    def hid_save(b):
        s = lax.rem(b, 2)
        return (
            pltpu.make_async_copy(hid.at[s, pl.ds(0, 2 * token_half)], hid_out.at[b], stage_sem.at[2, s]),
            pltpu.make_async_copy(slope.at[s], slope_out.at[b], stage_sem.at[3, s]),
        )

    def hid_load(b):
        s = lax.rem(b, 2)
        return (
            pltpu.make_async_copy(hid_out.at[b], hid.at[s, pl.ds(0, 2 * token_half)], stage_sem.at[2, s]),
            pltpu.make_async_copy(slope_out.at[b], slope.at[s], stage_sem.at[3, s]),
        )

    def grad_save(b):
        rng = pl.ds(al(b * high, 16), high)
        return pltpu.make_async_copy(u2s.at[rng], inputs_grad.at[rng], grad_sem.at[lax.rem(b, 2)])

    def mixed_save(b):
        s = lax.rem(b, 2)
        return pltpu.make_async_copy(ms.at[s], mixed.at[b], stage_sem.at[4, s])

    def both(copies, what):
        for copy in copies:
            getattr(copy, what)()

    def small_loads():
        pairs = [(token_in, tins), (token_out, touts), (token_bias, tbs), (token_shift, tss), (channel_bias, cbs.at[0])]
        vectors = (gain_one, shift_one, gain_two, shift_two, channel_shift)
        pairs += [(ref, vecs.at[i]) for i, ref in enumerate(vectors)]
        return [pltpu.make_async_copy(src, dst, small_sem.at[i]) for i, (src, dst) in enumerate(pairs)]

    both(small_loads(), "start")
    for b in (0, 1):
        patch_copy(b).start()
        cot_copy(b).start()

    wide = tw.shape[2]
    twi, two = tw.at[0], tw.at[1]

    def three(row):
        hi = row.astype(BF16).astype(F32)
        mid = (row - hi).astype(BF16).astype(F32)
        return hi, mid, row - hi - mid

    twi[pl.ds(0, token_half), :] = jnp.zeros((token_half, wide), BF16)
    two[pl.ds(0, token_half), :] = jnp.zeros((token_half, wide), BF16)
    at_row = lax.broadcasted_iota(jnp.int32, (16, wide), 0)
    at_lane = lax.broadcasted_iota(jnp.int32, (token_half, wide), 1)
    both(small_loads(), "wait")
    twi[pl.ds(0, token_half), pl.ds(0, patch)] = tins[...]
    two[pl.ds(0, token_half), pl.ds(0, patch)] = touts[...]
    padded = jnp.zeros((1, wide - token_half), F32)
    bias_row = jnp.concatenate([tbs[...].reshape(1, token_half), padded], axis=1)
    column = jnp.broadcast_to(bias_row, (LANES, wide)).T[:token_half, 0:1]
    filled = twi[pl.ds(0, token_half), :].astype(F32)
    for i, value in enumerate(three(column)):
        filled = jnp.where(at_lane == patch + i, value, filled)
    twi[pl.ds(0, token_half), :] = filled.astype(BF16)
    shift_row = jnp.concatenate([tss[...].reshape(1, patch), jnp.zeros((1, wide - patch), F32)], axis=1)
    extra = jnp.zeros((16, wide), F32)
    for i, value in enumerate(three(shift_row)):
        extra = jnp.where(at_row == i, value, extra)
    tokens = 2 * token_half
    two[pl.ds(tokens, 16), :] = extra.astype(BF16)

    pl.semaphore_wait(barrier, len(greet) + is_mid)
    both(token_mp(), "start")
    both(gather_mp(0), "start")
    first_word()
    both(bias_mp(), "start")

    def start_own(t, _):
        both(own_loads(t), "start")
        return 0

    lax.fori_loop(0, ticks, start_own, 0)

    dys[...] = jnp.zeros_like(dys)
    u2s[...] = jnp.zeros_like(u2s)
    dtok[...] = jnp.zeros_like(dtok)
    rest_rows = rows - images * high
    if rest_rows:
        chid[pl.ds(images * high, rest_rows), :] = jnp.zeros((rest_rows, chid.shape[1]), BF16)
        dcp[pl.ds(images * high, rest_rows), :] = jnp.zeros((rest_rows, dcp.shape[1]), BF16)
    row_acc[...] = jnp.zeros_like(row_acc)
    tin_acc[...] = jnp.zeros_like(tin_acc)
    tout_acc[...] = jnp.zeros_like(tout_acc)
    small[...] = jnp.zeros_like(small)
    u2s_t[pl.ds(width, 16), :] = jnp.ones((16, rows), BF16)
    for s in (0, 1):
        hid[s, pl.ds(tokens, 16), :] = jnp.ones((16, width), BF16)

    below = lax.broadcasted_iota(jnp.int32, (high, width), 0)
    ones = jnp.where(jnp.logical_and(below >= patch, below < patch + 3), 1.0, 0.0).astype(BF16)
    for b in range(images):
        u1s[b] = ones

    gain1, shift1, gain2, shift2 = (vecs[i : i + 1] for i in range(4))

    def first_norm(b, _):
        s = lax.rem(b, 2)
        patch_copy(b).wait()
        x = xs[s].astype(F32)

        @pl.when(b + 2 < images)
        def _():
            patch_copy(b + 2).start()

        keep[b] = x
        mean = jnp.mean(x, -1, keepdims=True)
        centred = x - mean
        scale = lax.rsqrt(jnp.mean(centred * centred, -1, keepdims=True) + 1e-06)
        stats[b, :, 0:1] = mean
        stats[b, :, 1:2] = scale
        u1s[b, pl.ds(0, patch), :] = (centred * scale * gain1 + shift1).astype(BF16)
        pre = dot(twi[pl.ds(0, token_half), pl.ds(0, high)], u1s[b])
        phi, deriv = gelu_parts(pre)
        at = pl.ds(al(b * token_half, 16), token_half)
        chid[at, pl.ds(0, width)] = (pre * phi).astype(BF16)
        dcp[at, pl.ds(0, width)] = deriv.astype(BF16)
        cot_copy(b).wait()
        value = ms[s]

        @pl.when(b + 2 < images)
        def _():
            cot_copy(b + 2).start()

        @pl.when(b + 1 < ticks)
        def _():
            both(gather_mp(b + 1), "start")

        @pl.when(b == images // 2)
        def _():
            both(token_mp(), "wait")
            both(token_core(), "start")

        dys[pl.ds(al(b * high, 16), patch), :] = value
        row_acc[pl.ds(4, 1), :] += jnp.sum(value.astype(F32), 0, keepdims=True)
        return 0

    lax.fori_loop(0, images, first_norm, 0)
    for t in range(images + 1, ticks):
        both(gather_mp(t), "start")

    def turn_dy(j, _):
        at = pl.ds(al(j * LANES, LANES), LANES)
        dys_t[:, at] = dys[at, :].T
        return 0

    lax.fori_loop(0, rows // LANES, turn_dy, 0)

    second_word()
    both(token_core(), "wait")
    two_t[...] = two[...].T

    def token_forward(b, _):
        s = lax.rem(b, 2)
        pre = dot(twi[pl.ds(token_half, token_half), pl.ds(0, high)], u1s[b])
        phi, deriv = gelu_parts(pre)

        @pl.when(b >= 2)
        def _():
            both(hid_save(b - 2), "wait")

        at = pl.ds(al(b * token_half, 16), token_half)
        hid[s, pl.ds(0, token_half), :] = chid[at, pl.ds(0, width)]
        slope[s, pl.ds(0, token_half), :] = dcp[at, pl.ds(0, width)]
        hid[s, pl.ds(token_half, token_half), :] = (pre * phi).astype(BF16)
        slope[s, pl.ds(token_half, token_half), :] = deriv.astype(BF16)
        both(hid_save(b), "start")
        x1 = keep[b] + dot(two_t[pl.ds(0, high), :], hid[s])[:patch]
        keep[b] = x1
        mean = jnp.mean(x1, -1, keepdims=True)
        centred = x1 - mean
        scale = lax.rsqrt(jnp.mean(centred * centred, -1, keepdims=True) + 1e-06)
        stats[b, :, 2:3] = mean
        stats[b, :, 3:4] = scale
        u2s[pl.ds(al(b * high, 16), patch), :] = (centred * scale * gain2 + shift2).astype(BF16)

        for t, when in enumerate((0, images // 2, images - 1)):

            @pl.when(b == when)
            def _(t=t):
                both(gather_mp(t), "wait")
                both(gather_near(t), "start")

        return 0

    lax.fori_loop(0, images, token_forward, 0)
    both(gather_near(0), "wait")
    both(gather_core(0), "start")
    both(bias_mp(), "wait")
    last_word()

    def turn_u2(j, _):
        at = pl.ds(al(j * LANES, LANES), LANES)
        u2s_t[pl.ds(0, width), at] = u2s[at, :].T
        return 0

    lax.fori_loop(0, rows // LANES, turn_u2, 0)
    for b in range(max(images - 2, 0), images):
        both(hid_save(b), "wait")

    live = images * high
    tiles = 2 if live % 32 == 0 else 1
    tall = live // tiles

    def channel(t, _):
        both(own_loads(t), "wait")
        both(gather_core(t), "wait")
        at = pl.ds(al(t * 2 * step, 2 * step), 2 * step)
        weight_in, weight_out = wi[:, at], wo[at, :]
        here = pl.ds(al(t * step, step), step)
        bias = jnp.concatenate([cbs[:, here], cbo[:, here]], axis=1)
        for i in range(tiles):
            rng = pl.ds(i * tall, tall)
            pre = dot(u2s[rng, :], weight_in) + bias
            back = dot_nt(dys[rng, :], weight_out)
            phi, deriv = gelu_parts(pre)
            chid[rng, at] = (pre * phi).astype(BF16)
            dcp[rng, at] = (back * deriv).astype(BF16)

        @pl.when(t + 3 < ticks)
        def _():
            both(gather_mp(t + 3), "wait")
            both(gather_near(t + 3), "start")

        @pl.when(t + 1 < ticks)
        def _():
            both(gather_near(t + 1), "wait")
            both(gather_core(t + 1), "start")

        point(2 * t, range(0, chunks, 2))
        slot = lax.rem(t, 2)
        grad_in = dot(u2s_t[...], dcp[:, at])
        cb_acc[:, at] = grad_in[width : width + 1]
        grad_in = grad_in[:width].astype(BF16)
        grad_out = dot(dys_t[...], chid[:, at]).astype(BF16)
        for m, value in ((0, grad_in), (1, grad_out)):
            for o in (0, 1):
                for q in (0, 1):
                    first = o * step + q * LANES
                    for k in (0, 1):
                        grads[slot, m, q, o, k] = value[k * half : (k + 1) * half, first : first + LANES]
        point(2 * t + 1, range(1, chunks, 2))
        core_copy(2 * t, width // 2).start()
        core_copy(2 * t + 1, width // 2).start()
        return 0

    lax.fori_loop(0, ticks, channel, 0)

    both(hid_load(0), "start")
    patch_copy(0).start()
    twi_t[...] = twi[pl.ds(0, tokens), :].T
    gain1, gain2, out_shift = vecs[0:1], vecs[2:3], vecs[4:5]

    def backward(b, _):
        s = lax.rem(b, 2)
        rng = pl.ds(al(b * high, 16), high)

        @pl.when(b + 1 < images)
        def _():
            both(hid_load(b + 1), "start")
            patch_copy(b + 1).start()

        @pl.when(b >= 2)
        def _():
            mixed_save(b - 2).wait()
            grad_save(b - 2).wait()

        x1 = keep[b]
        ms[s] = (x1 + dot(chid[rng, :], wo[...])[:patch] + out_shift).astype(BF16)
        mixed_save(b).start()
        du2 = dot_nt(dcp[rng, :], wi[...])[:patch]
        n2 = (x1 - stats[b, :, 2:3]) * stats[b, :, 3:4]
        row_acc[pl.ds(2, 1), :] += jnp.sum(du2 * n2, 0, keepdims=True)
        row_acc[pl.ds(3, 1), :] += jnp.sum(du2, 0, keepdims=True)
        dy = dys[pl.ds(al(b * high, 16), patch), :].astype(F32)
        dx1 = dy + norm_back(du2, n2, stats[b, :, 3:4], gain2)
        keep[b] = dx1
        dtok[pl.ds(0, patch), :] = dx1.astype(BF16)
        point(chunks + 2 * b, range(chunks, chunks + 2 * images, 2))
        both(hid_load(b), "wait")
        dtk = dtok[...]
        hidden = hid[s]
        tout_acc[:, pl.ds(0, high)] += dot_nt(hidden, dtk)
        dpre = (dot(two[pl.ds(0, tokens), pl.ds(0, high)], dtk) * slope[s].astype(F32)).astype(BF16)
        tin_acc[:, pl.ds(0, high)] += dot_nt(dpre, u1s[b])
        du1 = dot(twi_t[pl.ds(0, high), :], dpre)[:patch]
        patch_copy(b).wait()
        n1 = (xs[s].astype(F32) - stats[b, :, 0:1]) * stats[b, :, 1:2]
        row_acc[pl.ds(0, 1), :] += jnp.sum(du1 * n1, 0, keepdims=True)
        row_acc[pl.ds(1, 1), :] += jnp.sum(du1, 0, keepdims=True)
        dx = keep[b] + norm_back(du1, n1, stats[b, :, 1:2], gain1)
        u2s[pl.ds(al(b * high, 16), patch), :] = dx.astype(BF16)
        grad_save(b).start()
        point(chunks + 2 * b + 1, range(chunks + 1, chunks + 2 * images, 2))
        return 0

    lax.fori_loop(0, images, backward, 0)

    blocks = width // LANES
    for o in (0, 1):
        for v in range(5):
            for j in range(blocks):
                small[o, pl.ds(v * blocks + j, 1), :] = row_acc[pl.ds(v, 1), pl.ds(j * LANES, LANES)]
        for j in range(2):
            small[o, pl.ds(5 * blocks + j, 1), :] = tout_acc[pl.ds(tokens, 1), pl.ds(j * LANES, LANES)]
        for c in range(chunks):
            first = (c // 2) * 2 * step + o * step + (c % 2) * LANES
            small[o, pl.ds(5 * blocks + 2 + c, 1), :] = cb_acc[pl.ds(0, 1), pl.ds(first, LANES)]
    last_slot = ticks % 2
    for o in (0, 1):
        for m, total in ((0, tin_acc), (1, tout_acc)):
            for j in range(2):
                grads[last_slot, m, 0, o, j, pl.ds(0, token_half), :] = total[
                    pl.ds(o * token_half, token_half), pl.ds(j * LANES, LANES)
                ].astype(BF16)
        grads[last_slot, 0, 0, o, 0, pl.ds(token_half, small.shape[1]), :] = small[o].astype(BF16)
    core_copy(chunks, last_half).start()
    for name, c in REST:
        steps[name](c, half if c < chunks else last_half, STRAIGHT.index(c) if c in STRAIGHT else 0)
    for b in range(max(images - 2, 0), images):
        mixed_save(b).wait()
        grad_save(b).wait()


def widen(
    sizes, summed, mixed_in, grad_in,
    mixed, inputs_grad, d_in, d_out, d_tin, d_tbias, d_tout, d_tshift, d_gain1, d_shift1, d_gain2, d_shift2, d_cbias, d_cshift,
    sums, last, wide_in, wide_out, hold_mixed, hold_grad, wide_grad, in_sem, out_sem, last_sem, through_sem,
):
    images, patch, high, width, token_half, chunks = sizes

    def at(c):
        return pl.ds(c * LANES, LANES)

    loads = [[pltpu.make_async_copy(summed.at[m, c], sums.at[m, c], in_sem.at[m, c]) for m in (0, 1)] for c in range(chunks)]
    stores = [
        (
            pltpu.make_async_copy(wide_in.at[:, at(c)], d_in.at[:, at(c)], out_sem.at[0, c]),
            pltpu.make_async_copy(wide_out.at[at(c)], d_out.at[at(c)], out_sem.at[1, c]),
        )
        for c in range(chunks)
    ]
    load_last = [
        pltpu.make_async_copy(summed.at[m, chunks, :, pl.ds(0, last.shape[2])], last.at[m], last_sem.at[m]) for m in (0, 1)
    ]
    ins, outs = [], []
    for b in range(images):
        ins.append(pltpu.make_async_copy(mixed_in.at[b], hold_mixed.at[b], through_sem.at[0, b]))
        outs.append(pltpu.make_async_copy(hold_mixed.at[b], mixed.at[b], through_sem.at[2, b]))
    for b in range(images):
        ins.append(pltpu.make_async_copy(grad_in.at[pl.ds(b * high, high)], hold_grad.at[b], through_sem.at[1, b]))
        outs.append(pltpu.make_async_copy(wide_grad.at[b], inputs_grad.at[b], through_sem.at[3, b]))

    def pass_on(i):
        ins[i].wait()
        if i >= images:
            wide_grad[i - images] = hold_grad[i - images, pl.ds(0, patch), :].astype(F32)
        outs[i].start()

    for pair in loads:
        for copy in pair:
            copy.start()
    for copy in load_last + ins:
        copy.start()
    through = iter(range(2 * images))
    for c in range(chunks):
        for copy in loads[c]:
            copy.wait()
        wide_in[:, c * LANES : (c + 1) * LANES] = sums[0, c].reshape(width, LANES).astype(F32)
        stores[c][0].start()
        wide_out[c * LANES : (c + 1) * LANES, :] = sums[1, c].reshape(width, LANES).T.astype(F32)
        stores[c][1].start()
        for i in [i for i in (next(through, None),) if i is not None]:
            pass_on(i)
    for i in through:
        pass_on(i)
    for copy in load_last:
        copy.wait()

    def token_block(m):
        halves = [last[m, j, pl.ds(0, token_half), :] for j in (0, 1)]
        return jnp.concatenate(halves, axis=1).astype(F32)

    grad = token_block(0)
    d_tin[...] = grad[:, :patch]
    d_tbias[...] = grad.T[patch : patch + 1].reshape(token_half)
    d_tout[...] = token_block(1)[:, :patch]
    blocks = width // LANES
    rows = last[0, 0, pl.ds(token_half, 64), :].astype(F32)

    def vector(first, count):
        return jnp.concatenate([rows[first + j : first + j + 1] for j in range(count)], axis=1)

    for v, ref in enumerate((d_gain1, d_shift1, d_gain2, d_shift2, d_cshift)):
        ref[...] = vector(v * blocks, blocks).reshape(width)
    d_tshift[...] = vector(5 * blocks, 2)[:, :patch].reshape(patch)
    d_cbias[...] = vector(5 * blocks + 2, chunks).reshape(chunks * LANES)
    for pair in stores:
        for copy in pair:
            copy.wait()
    for copy in outs:
        copy.wait()


def per_device(
    dp_size,
    patches, cotangent, gain_one, shift_one, token_in, token_bias, token_out, token_shift,
    gain_two, shift_two, channel_in, channel_bias, channel_out, channel_shift,
):
    images, patch, width = patches.shape
    token_half = token_in.shape[1]
    hidden_half = channel_in.shape[1]
    step = 2 * LANES
    ticks = hidden_half // step
    chunks = 2 * ticks
    high = -(-(patch + 3) // 16) * 16
    rows = -(-images * high // LANES) * LANES
    wide = -(-patch // LANES) * LANES
    tokens = 2 * token_half
    far = max(sum(1 for b in range(4, 20) if 2**b < dp_size), 1)
    far_chunks = chunks + 1 if dp_size > 16 else 1
    last_half = -(-(token_half + 64) // 64) * 64
    sizes = (images, patch, width, token_half, hidden_half, ticks, dp_size, last_half)
    hbm = pl.BlockSpec(memory_space=pl.ANY)
    n = chunks + 1
    half = width // 2
    dma = pltpu.SemaphoreType.DMA
    mixed, inputs_grad, summed, _, _ = pl.pallas_call(
        functools.partial(layer, sizes),
        out_shape=(
            jax.ShapeDtypeStruct((images, patch, width), BF16),
            jax.ShapeDtypeStruct((images * high, width), BF16),
            jax.ShapeDtypeStruct((2, n, 2, half, LANES), BF16),
            jax.ShapeDtypeStruct((images, tokens, width), BF16),
            jax.ShapeDtypeStruct((images, tokens, width), BF16),
        ),
        in_specs=[hbm] * 14,
        out_specs=(hbm,) * 5,
        scratch_shapes=[
            pltpu.VMEM((width, 2 * hidden_half), BF16),
            pltpu.VMEM((2 * hidden_half, width), BF16),
            pltpu.VMEM((8, width), F32),
            pltpu.VMEM((1, hidden_half), F32),
            pltpu.VMEM((1, hidden_half), F32),
            pltpu.VMEM((token_half,), F32),
            pltpu.VMEM((patch,), F32),
            pltpu.VMEM((token_half, patch), BF16),
            pltpu.VMEM((token_half, patch), BF16),
            pltpu.VMEM((2, tokens + 16, wide), BF16),
            pltpu.VMEM((wide, tokens), BF16),
            pltpu.VMEM((wide, tokens + 16), BF16),
            pltpu.VMEM((images, patch, width), F32),
            pltpu.VMEM((rows, width), BF16),
            pltpu.VMEM((width, rows), BF16),
            pltpu.VMEM((rows, width), BF16),
            pltpu.VMEM((width + 16, rows), BF16),
            pltpu.VMEM((images, high, width), BF16),
            pltpu.VMEM((rows, 2 * hidden_half), BF16),
            pltpu.VMEM((rows, 2 * hidden_half), BF16),
            pltpu.VMEM((high, width), BF16),
            pltpu.VMEM((2, patch, width), BF16),
            pltpu.VMEM((2, patch, width), BF16),
            pltpu.VMEM((2, tokens + 16, width), BF16),
            pltpu.VMEM((2, tokens, width), BF16),
            pltpu.VMEM((images, patch, 4), F32),
            pltpu.VMEM((8, width), F32),
            pltpu.VMEM((1, 2 * hidden_half), F32),
            pltpu.VMEM((tokens, wide), F32),
            pltpu.VMEM((tokens + 16, wide), F32),
            pltpu.VMEM((2, 64, LANES), F32),
            pltpu.VMEM((2, 2, 2, 2, 2, half, LANES), BF16),
            pltpu.VMEM((2, 2, 2, 2, half, LANES), BF16),
            pltpu.VMEM((n, 2, 2, half, LANES), BF16),
            pltpu.VMEM((n, 2, half, LANES), BF16),
            pltpu.VMEM((n, half, LANES), BF16),
            pltpu.VMEM((n, 3 * (half // 4), LANES), BF16),
            pltpu.VMEM((far_chunks, far, half // 4, LANES), BF16),
            dma((ticks, 2)),
            dma((5, 2)),
            dma((10,)),
            dma((2,)),
            dma((3,)), dma((3,)),
            dma((ticks, 4)), dma((ticks, 6)),
            dma((2, 2)), dma((2, 2)),
            dma((RING,)), dma((RING,)),
            dma((2, n)), dma((len(STRAIGHT),)), dma((n,)),
            dma((n,)), dma((n,)), dma((n,)), dma((n,)), dma((len(STRAIGHT),)),
            dma((n,)), dma((n,)), dma((len(STRAIGHT),)), dma((n,)), dma((2, n)),
            dma((far_chunks, far)), dma((far_chunks, far)),
            pltpu.SemaphoreType.REGULAR((4,)),
        ],
        compiler_params=pltpu.CompilerParams(
            collective_id=0, has_side_effects=True, vmem_limit_bytes=63 * 2**20
        ),
        name="mixer_layer",
    )(
        patches, cotangent, gain_one, shift_one, token_in.T, token_bias, token_out, token_shift,
        gain_two, shift_two, channel_in, channel_bias, channel_out, channel_shift,
    )

    vmem = pl.BlockSpec(memory_space=pltpu.VMEM)
    shapes = (
        (token_half, patch), (token_half,), (token_half, patch), (patch,),
        (width,), (width,), (width,), (width,), (hidden_half,), (width,),
    )
    (
        mixed, inputs_grad, d_in, d_out, d_tin, d_tbias, d_tout, d_tshift,
        d_gain1, d_shift1, d_gain2, d_shift2, d_cbias, d_cshift,
    ) = pl.pallas_call(
        functools.partial(widen, (images, patch, high, width, token_half, chunks)),
        in_specs=[hbm] * 3,
        out_specs=(hbm,) * 4 + (vmem,) * len(shapes),
        out_shape=(
            jax.ShapeDtypeStruct((images, patch, width), BF16),
            jax.ShapeDtypeStruct((images, patch, width), F32),
            jax.ShapeDtypeStruct((width, hidden_half), F32),
            jax.ShapeDtypeStruct((hidden_half, width), F32),
        ) + tuple(jax.ShapeDtypeStruct(shape, F32) for shape in shapes),
        scratch_shapes=[
            pltpu.VMEM((2, chunks, 2, half, LANES), BF16),
            pltpu.VMEM((2, 2, last_half, LANES), BF16),
            pltpu.VMEM((width, hidden_half), F32),
            pltpu.VMEM((hidden_half, width), F32),
            pltpu.VMEM((images, patch, width), BF16),
            pltpu.VMEM((images, high, width), BF16),
            pltpu.VMEM((images, patch, width), F32),
            dma((2, chunks)), dma((2, chunks)), dma((2,)), dma((4, images)),
        ],
        compiler_params=pltpu.CompilerParams(vmem_limit_bytes=60 * 2**20),
        name="widen",
    )(summed, mixed, inputs_grad)
    return (
        mixed, inputs_grad, d_gain1, d_shift1, d_tin.T, d_tbias, d_tout, d_tshift,
        d_gain2, d_shift2, d_in, d_cbias, d_out, d_cshift,
    )


def solution(mesh):
    split = P(("dp", "mp"), None, None)
    columns, rows, vector = P(None, "mp"), P("mp", None), P("mp")
    return jax.shard_map(
        functools.partial(per_device, mesh.shape["dp"]),
        mesh=mesh,
        in_specs=(
            split, split, P(), P(), columns, vector, rows, P(), P(), P(), columns, vector, rows, P(),
        ),
        out_specs=(
            split, split, P(), P(), columns, vector, rows, P(), P(), P(), columns, vector, rows, P(),
        ),
        check_vma=False,
    )
```

```python
import functools

import jax
import jax.numpy as jnp
from jax import lax
from jax.experimental import pallas as pl
from jax.experimental.pallas import tpu as pltpu
from jax.sharding import PartitionSpec as P

MESH = pl.DeviceIdType.MESH
F32 = jnp.float32
BF16 = jnp.bfloat16
NT = (((1,), (1,)), ((), ()))
LANES = 128
RING = 4

STRAIGHT = (4, 5, 8, 9, 11, 12)
POINTS = (
    ("core_mp", ((0, 2), (2, 4), (3, 5), (4, 6), (5, 7), (6, 8), (8, 10), (9, 11), (11, 13))),
    ("core_both", ((1, 3), (7, 9), (10, 12))),
    ("mp", ((0, 6), (2, 7), (3, 10), (4, 11), (5, 13), (6, 16), (8, 17), (9, 19), (11, 21))),
    ("both", ((1, 7), (7, 12), (10, 16))),
    ("side", ((0, 10), (2, 11), (3, 13), (6, 18))),
    ("side_line", ((4, 14), (5, 17), (8, 19), (9, 21))),
    ("then_mp", ((1, 14), (7, 19), (10, 23))),
    ("low", ((0, 12), (2, 13), (3, 15), (1, 16), (6, 20), (7, 22))),
    ("high", ((0, 14), (2, 15), (3, 17), (1, 18), (6, 23))),
    ("line", ((4, 16), (5, 19), (8, 21))),
    ("high_spread", ((0, 16), (2, 17), (3, 20), (1, 21))),
    ("low_spread", ((0, 18), (2, 20), (3, 23))),
    ("spread", ((4, 20), (5, 22))),
    ("side_spread", ((0, 20), (2, 22), (4, 23))),
    ("core_spread", ((0, 21), (2, 23))),
)
REST = (
    ("side_line", 11), ("low_spread", 1), ("core_mp", 12), ("core_spread", 4), ("line", 9), ("side_spread", 5),
    ("spread", 8), ("low", 10), ("core_spread", 5), ("high_spread", 6), ("high", 7), ("line", 11),
    ("side_spread", 3), ("mp", 12), ("spread", 9), ("side_spread", 1), ("core_spread", 3), ("high", 10),
    ("core_spread", 1), ("low_spread", 6), ("high_spread", 7), ("side_spread", 8), ("side_line", 12),
    ("core_spread", 8), ("spread", 11), ("high_spread", 10), ("side_spread", 9), ("low_spread", 7),
    ("side_spread", 6), ("line", 12), ("low_spread", 10), ("side_spread", 11), ("core_spread", 9), ("spread", 12),
    ("core_spread", 6), ("side_spread", 7), ("side_spread", 10), ("core_spread", 7), ("side_spread", 12),
    ("core_spread", 11), ("core_spread", 10), ("core_spread", 12),
)


def dot(a, b):
    return jnp.dot(a, b, preferred_element_type=F32)


def dot_nt(a, b):
    return lax.dot_general(a, b, NT, preferred_element_type=F32)


def centre(values):
    centred = values - jnp.mean(values, -1, keepdims=True)
    return centred, lax.rsqrt(jnp.mean(centred * centred, -1, keepdims=True) + 1e-06)


def norm_back(grad, normed, scale, gain):
    scaled = grad * gain
    return scale * (
        scaled
        - jnp.mean(scaled, -1, keepdims=True)
        - normed * jnp.mean(scaled * normed, -1, keepdims=True)
    )


def gelu_parts(v):
    phi = 0.5 + 0.5 * lax.erf(v * 0.7071067811865476)
    return phi, phi + v * (0.3989422804014327 * jnp.exp(-0.5 * v * v))


def layer(
    sizes,
    patches, cotangent, gain_one, shift_one, token_in, token_bias, token_out, token_shift,
    gain_two, shift_two, channel_in, channel_bias, channel_out, channel_shift,
    mixed, inputs_grad, summed, hid_out, slope_out,
    wi, wo, vecs, cbs, cbo, tbs, tss, tins, touts, tw, twi_t, two_t, keep,
    dys, dys_t, u2s, u2s_t, u1s, chid, dcp, dtok,
    xs, ms, hid, slope, stats,
    row_acc, cb_acc, tin_acc, tout_acc, small,
    grads, from_core, acc, from_mp, from_x, from_z, from_far,
    load_sem, stage_sem, small_sem, grad_sem, tok_s, tok_r, w_s, w_r, wc_s, wc_r, c_s, c_r, g_s, line_s, l_sem, y_r, x_r, z_r, zh_r, zl_r,
    a_r, al_r, sl_r, xa_r, ca_r, far_s, far_r, hello,
):
    images, patch, width, token_half, hidden_half, ticks, dp_size, last_half = sizes
    rows = dys.shape[0]
    high = u1s.shape[1]
    step = hidden_half // ticks
    half = width // 2
    chunks = 2 * ticks
    eighth_in = width // 8

    dp = lax.axis_index("dp")
    mp = lax.axis_index("mp")
    core = lax.rem(dp, 2)
    side = lax.rem(lax.div(dp, 2), 2)
    near = lax.rem(lax.div(dp, 2), 4)
    line = lax.rem(lax.div(dp, 4), 4)
    part = core * 4 + near
    low = lax.rem(line, 2)

    to_mp = {"mp": 1 - mp}
    to_core = {"dp": dp + 1 - 2 * core}
    to_side = {"dp": dp + 2 - 4 * side}

    def near_of(r):
        return {"dp": dp + 2 * (lax.rem(near + r, 4) - near)}

    def line_of(r):
        return {"dp": dp + 4 * (lax.rem(line + r, 4) - line)}

    far_bits = []
    bit = 16
    while bit < dp_size:
        far_bits.append(bit)
        bit *= 2

    def far_of(i):
        b = far_bits[i]
        return {"dp": dp + b - 2 * b * lax.rem(lax.div(dp, b), 2)}

    def remote(src, dst, send, recv, device):
        return pltpu.make_async_remote_copy(
            src_ref=src, dst_ref=dst, send_sem=send, recv_sem=recv, device_id=device, device_id_type=MESH
        )

    def al(v, m):
        return pl.multiple_of(v, m)

    def own_loads(t):
        return (
            pltpu.make_async_copy(
                channel_in.at[:, pl.ds(al(t * step, step), step)],
                wi.at[:, pl.ds(al(t * 2 * step, step), step)],
                load_sem.at[t, 0],
            ),
            pltpu.make_async_copy(
                channel_out.at[pl.ds(al(t * step, step), step), :],
                wo.at[pl.ds(al(t * 2 * step, step), step), :],
                load_sem.at[t, 1],
            ),
        )

    def other_in(t, first, count):
        return wi.at[pl.ds(al(first, eighth_in), count), pl.ds(al(t * 2 * step + step, step), step)]

    def other_out(t, first, count):
        return wo.at[pl.ds(al(t * 2 * step + step + first, 16), count), :]

    which = side + core * (low - side)
    quarter_out = step // 4
    to_pair = {"dp": dp + (2 - 4 * side) * (1 - core) + (4 - 8 * low) * core}

    def gather_mp(t):
        first = core * 2 * quarter_out + which * quarter_out
        return (
            remote(
                channel_in.at[pl.ds(al(part * eighth_in, eighth_in), eighth_in), pl.ds(al(t * step, step), step)],
                other_in(t, part * eighth_in, eighth_in),
                w_s.at[t, 0], w_r.at[t, 0], to_mp,
            ),
            remote(
                channel_out.at[pl.ds(al(t * step + first, 16), quarter_out), :],
                other_out(t, first, quarter_out),
                w_s.at[t, 1], w_r.at[t, 1], to_mp,
            ),
        )

    def gather_near(t):
        a = other_in(t, part * eighth_in, eighth_in)
        b = other_out(t, core * 2 * quarter_out + which * quarter_out, quarter_out)
        copies = [remote(a, a, w_s.at[t, r - 1], w_r.at[t, r + 1], near_of(r)) for r in (1, 2, 3)]
        return copies + [remote(b, b, w_s.at[t, 3], w_r.at[t, 5], to_pair)]

    def gather_core(t):
        a = other_in(t, core * 4 * eighth_in, 4 * eighth_in)
        b = other_out(t, core * 2 * quarter_out, 2 * quarter_out)
        s = lax.rem(t, 2)
        return (
            remote(a, a, wc_s.at[s, 0], wc_r.at[s, 0], to_core),
            remote(b, b, wc_s.at[s, 1], wc_r.at[s, 1], to_core),
        )

    def token_mp():
        return (
            remote(
                tw.at[core, pl.ds(0, token_half)], tw.at[core, pl.ds(token_half, token_half)], tok_s.at[0], tok_r.at[0], to_mp
            ),
        )

    def bias_mp():
        return (remote(cbs, cbo, tok_s.at[1], tok_r.at[1], to_mp),)

    def token_core():
        ref = tw.at[core, pl.ds(token_half, token_half)]
        return (remote(ref, ref, tok_s.at[2], tok_r.at[2], to_core),)

    high_bit = lax.div(line, 2)
    to_low = {"dp": dp + 4 - 8 * low}
    to_high = {"dp": dp + 8 - 16 * high_bit}

    def rows_at(first, count):
        return pl.ds(al(first, 16), count)

    def core_copy(c, h):
        slot, q, i = lax.rem(lax.div(c, 2), 2), lax.rem(c, 2), lax.rem(c, RING)
        rng = pl.ds(0, h)
        return remote(
            grads.at[slot, 1 - core, q, :, :, rng], from_core.at[slot, q, :, :, rng], c_s.at[i], c_r.at[i], to_core
        )

    def mp_copy(c, h):
        rng = pl.ds(0, h)
        return remote(acc.at[c, 1, :, rng], from_mp.at[c, :, rng], g_s.at[0, c], y_r.at[c], to_mp)

    def side_copy(c, h):
        rng = pl.ds(0, h)
        return remote(acc.at[c, 0, 1 - side, rng], from_x.at[c, rng], g_s.at[0, c], x_r.at[c], to_side)

    def both_copy(c):
        return remote(acc.at[c, :, 1 - side], from_mp.at[c], g_s.at[0, c], x_r.at[c], to_side)

    def then_mp_copy(c):
        return remote(acc.at[c, 1, side], from_x.at[c], g_s.at[0, c], y_r.at[c], to_mp)

    def low_copy(c, h):
        n = h // 2
        src = acc.at[c, 0, side, rows_at((1 - low) * n, n)]
        return remote(src, from_z.at[c, pl.ds(0, n)], g_s.at[0, c], z_r.at[c], to_low)

    def high_copy(c, h):
        n = h // 4
        src = acc.at[c, 0, side, rows_at(low * 2 * n + (1 - high_bit) * n, n)]
        return remote(src, from_z.at[c, pl.ds(2 * n, n)], g_s.at[0, c], zh_r.at[c], to_high)

    def at_place(c, h):
        return rows_at(low * (h // 2) + high_bit * (h // 4), h // 4)

    def at_line(h, place):
        return rows_at(place * (h // 4), h // 4)

    def line_sems(c, d, first, second, third):
        return ((first.at[c], second.at[c], third.at[d])[r] for r in range(3))

    def line_copies(c, h, d):
        sends = line_sems(c, d, g_s.at[0], g_s.at[1], line_s)
        recvs = line_sems(c, d, z_r, zh_r, zl_r)
        return [
            remote(
                acc.at[c, 0, side, at_line(h, lax.rem(line + r, 4))],
                from_z.at[c, pl.ds((r - 1) * (h // 4), h // 4)], send, recv, line_of(r),
            )
            for r, send, recv in zip((1, 2, 3), sends, recvs)
        ]

    def sums_of(c, rng):
        return from_mp.at[c, 0, rng]

    def keep_copy(c, h):
        rng = pl.ds(0, h)
        return pltpu.make_async_copy(sums_of(c, rng), summed.at[core, c, side, rng], l_sem.at[c])

    def high_spread_copy(c, h):
        ref = sums_of(c, at_place(c, h))
        return remote(ref, ref, g_s.at[0, c], a_r.at[c], to_high)

    def low_spread_copy(c, h):
        ref = sums_of(c, rows_at(low * (h // 2), h // 2))
        return remote(ref, ref, g_s.at[0, c], al_r.at[c], to_low)

    def spread_copies(c, h, d):
        ref = sums_of(c, at_line(h, line))
        sends = line_sems(c, d, g_s.at[0], g_s.at[1], line_s)
        recvs = line_sems(c, d, a_r, al_r, sl_r)
        return [remote(ref, ref, send, recv, line_of(r)) for r, send, recv in zip((1, 2, 3), sends, recvs)]

    def side_spread_copy(c, h):
        rng = pl.ds(0, h)
        return remote(sums_of(c, rng), summed.at[core, c, side, rng], g_s.at[0, c], xa_r.at[c], to_side)

    def core_own_copy(c, h):
        rng = pl.ds(0, h)
        return remote(sums_of(c, rng), summed.at[core, c, side, rng], g_s.at[1, c], ca_r.at[0, c], to_core)

    def core_other_copy(c, h):
        ref = summed.at[core, c, 1 - side, pl.ds(0, h)]
        return remote(ref, ref, g_s.at[0, c], ca_r.at[1, c], to_core)

    def add(a, b):
        return (a.astype(F32) + b.astype(F32)).astype(BF16)

    def core_step(c, h, send):
        core_copy(c, h).wait()
        slot, q, rng = lax.rem(lax.div(c, 2), 2), lax.rem(c, 2), pl.ds(0, h)
        acc[c, 1, :, rng] = add(grads[slot, core, q, 1, :, rng], from_core[slot, q, 1, :, rng])
        if send is mp_copy:
            send(c, h).start()
        acc[c, 0, :, rng] = add(grads[slot, core, q, 0, :, rng], from_core[slot, q, 0, :, rng])
        if send is both_copy:
            send(c).start()

    def core_mp(c, h, d):
        core_step(c, h, mp_copy)

    def core_both(c, h, d):
        core_step(c, h, both_copy)

    def mp_step(c, h, d):
        mp_copy(c, h).wait()
        rng = pl.ds(0, h)
        acc[c, 0, 1 - side, rng] = add(acc[c, 0, 1 - side, rng], from_mp[c, 1 - side, rng])
        side_copy(c, h).start()
        acc[c, 0, side, rng] = add(acc[c, 0, side, rng], from_mp[c, side, rng])

    def side_step(c, h, d):
        side_copy(c, h).wait()
        rng = pl.ds(0, h)
        acc[c, 0, side, rng] = add(acc[c, 0, side, rng], from_x[c, rng])
        low_copy(c, h).start()

    def side_line(c, h, d):
        side_copy(c, h).wait()
        rng = pl.ds(0, h)
        acc[c, 0, side, rng] = add(acc[c, 0, side, rng], from_x[c, rng])
        for copy in line_copies(c, h, d):
            copy.start()

    def both_step(c, h, d):
        both_copy(c).wait()
        acc[c, 1, side] = add(acc[c, 1, side], from_mp[c, 1])
        then_mp_copy(c).start()
        acc[c, 0, side] = add(acc[c, 0, side], from_mp[c, 0])

    def then_mp_step(c, h, d):
        then_mp_copy(c).wait()
        acc[c, 0, side] = add(acc[c, 0, side], from_x[c])
        low_copy(c, h).start()

    def low_step(c, h, d):
        low_copy(c, h).wait()
        rng = rows_at(low * (h // 2), h // 2)
        acc[c, 0, side, rng] = add(acc[c, 0, side, rng], from_z[c, pl.ds(0, h // 2)])
        high_copy(c, h).start()

    def over_far(c, rng, count):
        for i in range(len(far_bits)):
            dst = from_far.at[c, i, pl.ds(0, count)]
            copy = remote(sums_of(c, rng), dst, far_s.at[c, i], far_r.at[c, i], far_of(i))
            copy.start()
            copy.wait()
            from_mp[c, 0, rng] = add(from_mp[c, 0, rng], from_far[c, i, pl.ds(0, count)])

    def high_step(c, h, d):
        high_copy(c, h).wait()
        rng = at_place(c, h)
        from_mp[c, 0, rng] = add(acc[c, 0, side, rng], from_z[c, pl.ds(h // 2, h // 4)])
        over_far(c, rng, h // 4)
        high_spread_copy(c, h).start()

    def high_spread_step(c, h, d):
        high_spread_copy(c, h).wait()
        low_spread_copy(c, h).start()

    def low_spread_step(c, h, d):
        low_spread_copy(c, h).wait()
        side_spread_copy(c, h).start()
        core_own_copy(c, h).start()
        keep_copy(c, h).start()

    def line_step(c, h, d):
        for copy in line_copies(c, h, d):
            copy.wait()
        rng = at_line(h, line)
        total = acc[c, 0, side, rng].astype(F32)
        for r in range(3):
            total = total + from_z[c, pl.ds(r * (h // 4), h // 4)].astype(F32)
        from_mp[c, 0, rng] = total.astype(BF16)
        over_far(c, rng, h // 4)
        for copy in spread_copies(c, h, d):
            copy.start()

    def spread_step(c, h, d):
        for copy in spread_copies(c, h, d):
            copy.wait()
        side_spread_copy(c, h).start()
        core_own_copy(c, h).start()
        keep_copy(c, h).start()

    def side_spread_step(c, h, d):
        side_spread_copy(c, h).wait()
        core_other_copy(c, h).start()

    def core_spread_step(c, h, d):
        core_own_copy(c, h).wait()
        keep_copy(c, h).wait()
        core_other_copy(c, h).wait()

    steps = {
        "core_mp": core_mp, "core_both": core_both, "mp": mp_step, "side": side_step, "side_line": side_line, "both": both_step,
        "then_mp": then_mp_step, "low": low_step, "high": high_step, "high_spread": high_spread_step,
        "low_spread": low_spread_step, "line": line_step, "spread": spread_step,
        "side_spread": side_spread_step, "core_spread": core_spread_step,
    }

    def point(p, places):
        for name, entries in POINTS:
            here = [(c, at) for c, at in entries if at in places]
            if here:
                now = [(p == at).astype(jnp.int32) for _, at in here]
                c = sum(c * one for (c, _), one in zip(here, now))
                d = sum(STRAIGHT.index(c) * one for (c, _), one in zip(here, now) if c in STRAIGHT)

                @pl.when(sum(now) > 0)
                def _(c=c, d=d, name=name):
                    steps[name](c, half, d)

    barrier = pltpu.get_barrier_semaphore()
    to_mid = {"dp": dp + 4 * (3 - 2 * line)}
    is_mid = lax.rem(lax.div(line + 1, 2), 2)
    greet = [to_mp, to_core, to_side, to_low] + [far_of(i) for i in range(len(far_bits))]
    for device in greet:
        pl.semaphore_signal(barrier, inc=1, device_id=device, device_id_type=MESH)

    @pl.when(is_mid == 1)
    def _():
        pl.semaphore_signal(barrier, inc=1, device_id=to_mid, device_id_type=MESH)

    def tell(i, device):
        pl.semaphore_signal(hello.at[i], inc=1, device_id=device, device_id_type=MESH)

    def first_word():
        tell(0, to_side)
        tell(1, to_low)

        @pl.when(is_mid == 1)
        def _():
            tell(2, to_mid)

    def second_word():
        for i in (0, 1):
            pl.semaphore_wait(hello.at[i], 1)

        @pl.when(is_mid == 1)
        def _():
            pl.semaphore_wait(hello.at[2], 1)

        tell(3, to_low)

    def last_word():
        pl.semaphore_wait(hello.at[3], 1)


    def patch_copy(b):
        return pltpu.make_async_copy(patches.at[b], xs.at[lax.rem(b, 2)], stage_sem.at[0, lax.rem(b, 2)])

    def cot_copy(b):
        return pltpu.make_async_copy(cotangent.at[b], ms.at[lax.rem(b, 2)], stage_sem.at[1, lax.rem(b, 2)])

    def hid_save(b):
        s = lax.rem(b, 2)
        return (
            pltpu.make_async_copy(hid.at[s, pl.ds(0, 2 * token_half)], hid_out.at[b], stage_sem.at[2, s]),
            pltpu.make_async_copy(slope.at[s], slope_out.at[b], stage_sem.at[3, s]),
        )

    def hid_load(b):
        s = lax.rem(b, 2)
        return (
            pltpu.make_async_copy(hid_out.at[b], hid.at[s, pl.ds(0, 2 * token_half)], stage_sem.at[2, s]),
            pltpu.make_async_copy(slope_out.at[b], slope.at[s], stage_sem.at[3, s]),
        )

    def grad_save(b):
        rng = pl.ds(al(b * high, 16), high)
        return pltpu.make_async_copy(u2s.at[rng], inputs_grad.at[rng], grad_sem.at[lax.rem(b, 2)])

    def mixed_save(b):
        s = lax.rem(b, 2)
        return pltpu.make_async_copy(ms.at[s], mixed.at[b], stage_sem.at[4, s])

    def both(copies, what):
        for copy in copies:
            getattr(copy, what)()

    def small_loads():
        pairs = [(token_in, tins), (token_out, touts), (token_bias, tbs), (token_shift, tss), (channel_bias, cbs.at[0])]
        vectors = (gain_one, shift_one, gain_two, shift_two, channel_shift)
        pairs += [(ref, vecs.at[i]) for i, ref in enumerate(vectors)]
        return [pltpu.make_async_copy(src, dst, small_sem.at[i]) for i, (src, dst) in enumerate(pairs)]

    both(small_loads(), "start")
    for b in (0, 1):
        patch_copy(b).start()
        cot_copy(b).start()

    wide = tw.shape[2]
    twi, two = tw.at[0], tw.at[1]

    def three(row):
        hi = row.astype(BF16).astype(F32)
        mid = (row - hi).astype(BF16).astype(F32)
        return hi, mid, row - hi - mid

    twi[pl.ds(0, token_half), :] = jnp.zeros((token_half, wide), BF16)
    two[pl.ds(0, token_half), :] = jnp.zeros((token_half, wide), BF16)
    at_row = lax.broadcasted_iota(jnp.int32, (16, wide), 0)
    at_lane = lax.broadcasted_iota(jnp.int32, (token_half, wide), 1)
    both(small_loads(), "wait")
    twi[pl.ds(0, token_half), pl.ds(0, patch)] = tins[...]
    two[pl.ds(0, token_half), pl.ds(0, patch)] = touts[...]
    padded = jnp.zeros((1, wide - token_half), F32)
    bias_row = jnp.concatenate([tbs[...].reshape(1, token_half), padded], axis=1)
    column = jnp.broadcast_to(bias_row, (LANES, wide)).T[:token_half, 0:1]
    filled = twi[pl.ds(0, token_half), :].astype(F32)
    for i, value in enumerate(three(column)):
        filled = jnp.where(at_lane == patch + i, value, filled)
    twi[pl.ds(0, token_half), :] = filled.astype(BF16)
    shift_row = jnp.concatenate([tss[...].reshape(1, patch), jnp.zeros((1, wide - patch), F32)], axis=1)
    extra = jnp.zeros((16, wide), F32)
    for i, value in enumerate(three(shift_row)):
        extra = jnp.where(at_row == i, value, extra)
    tokens = 2 * token_half
    two[pl.ds(tokens, 16), :] = extra.astype(BF16)

    pl.semaphore_wait(barrier, len(greet) + is_mid)
    both(token_mp(), "start")
    both(gather_mp(0), "start")
    first_word()
    both(bias_mp(), "start")

    def start_own(t, _):
        both(own_loads(t), "start")
        return 0

    lax.fori_loop(0, ticks, start_own, 0)

    dys[...] = jnp.zeros_like(dys)
    u2s[...] = jnp.zeros_like(u2s)
    dtok[...] = jnp.zeros_like(dtok)
    rest_rows = rows - images * high
    if rest_rows:
        chid[pl.ds(images * high, rest_rows), :] = jnp.zeros((rest_rows, chid.shape[1]), BF16)
        dcp[pl.ds(images * high, rest_rows), :] = jnp.zeros((rest_rows, dcp.shape[1]), BF16)
    row_acc[...] = jnp.zeros_like(row_acc)
    tin_acc[...] = jnp.zeros_like(tin_acc)
    tout_acc[...] = jnp.zeros_like(tout_acc)
    small[...] = jnp.zeros_like(small)
    u2s_t[pl.ds(width, 16), :] = jnp.ones((16, rows), BF16)
    for s in (0, 1):
        hid[s, pl.ds(tokens, 16), :] = jnp.ones((16, width), BF16)

    below = lax.broadcasted_iota(jnp.int32, (high, width), 0)
    ones = jnp.where(jnp.logical_and(below >= patch, below < patch + 3), 1.0, 0.0).astype(BF16)
    for b in range(images):
        u1s[b] = ones

    gain1, shift1, gain2, shift2 = (vecs[i : i + 1] for i in range(4))

    def first_norm(b, _):
        s = lax.rem(b, 2)
        patch_copy(b).wait()
        x = xs[s].astype(F32)

        @pl.when(b + 2 < images)
        def _():
            patch_copy(b + 2).start()

        keep[b] = x
        mean = jnp.mean(x, -1, keepdims=True)
        centred = x - mean
        scale = lax.rsqrt(jnp.mean(centred * centred, -1, keepdims=True) + 1e-06)
        stats[b, :, 0:1] = mean
        stats[b, :, 1:2] = scale
        u1s[b, pl.ds(0, patch), :] = (centred * scale * gain1 + shift1).astype(BF16)
        pre = dot(twi[pl.ds(0, token_half), pl.ds(0, high)], u1s[b])
        phi, deriv = gelu_parts(pre)
        at = pl.ds(al(b * token_half, 16), token_half)
        chid[at, pl.ds(0, width)] = (pre * phi).astype(BF16)
        dcp[at, pl.ds(0, width)] = deriv.astype(BF16)
        cot_copy(b).wait()
        value = ms[s]

        @pl.when(b + 2 < images)
        def _():
            cot_copy(b + 2).start()

        @pl.when(b + 1 < ticks)
        def _():
            both(gather_mp(b + 1), "start")

        @pl.when(b == images // 2)
        def _():
            both(token_mp(), "wait")
            both(token_core(), "start")

        dys[pl.ds(al(b * high, 16), patch), :] = value
        row_acc[pl.ds(4, 1), :] += jnp.sum(value.astype(F32), 0, keepdims=True)
        return 0

    lax.fori_loop(0, images, first_norm, 0)
    for t in range(images + 1, ticks):
        both(gather_mp(t), "start")

    def turn_dy(j, _):
        at = pl.ds(al(j * LANES, LANES), LANES)
        dys_t[:, at] = dys[at, :].T
        return 0

    lax.fori_loop(0, rows // LANES, turn_dy, 0)

    second_word()
    both(token_core(), "wait")
    two_t[...] = two[...].T

    def token_forward(b, _):
        s = lax.rem(b, 2)
        pre = dot(twi[pl.ds(token_half, token_half), pl.ds(0, high)], u1s[b])
        phi, deriv = gelu_parts(pre)

        @pl.when(b >= 2)
        def _():
            both(hid_save(b - 2), "wait")

        at = pl.ds(al(b * token_half, 16), token_half)
        hid[s, pl.ds(0, token_half), :] = chid[at, pl.ds(0, width)]
        slope[s, pl.ds(0, token_half), :] = dcp[at, pl.ds(0, width)]
        hid[s, pl.ds(token_half, token_half), :] = (pre * phi).astype(BF16)
        slope[s, pl.ds(token_half, token_half), :] = deriv.astype(BF16)
        both(hid_save(b), "start")
        x1 = keep[b] + dot(two_t[pl.ds(0, high), :], hid[s])[:patch]
        keep[b] = x1
        mean = jnp.mean(x1, -1, keepdims=True)
        centred = x1 - mean
        scale = lax.rsqrt(jnp.mean(centred * centred, -1, keepdims=True) + 1e-06)
        stats[b, :, 2:3] = mean
        stats[b, :, 3:4] = scale
        u2s[pl.ds(al(b * high, 16), patch), :] = (centred * scale * gain2 + shift2).astype(BF16)

        for t, when in enumerate((0, images // 2, images - 1)):

            @pl.when(b == when)
            def _(t=t):
                both(gather_mp(t), "wait")
                both(gather_near(t), "start")

        return 0

    lax.fori_loop(0, images, token_forward, 0)
    both(gather_near(0), "wait")
    both(gather_core(0), "start")
    both(bias_mp(), "wait")
    last_word()

    def turn_u2(j, _):
        at = pl.ds(al(j * LANES, LANES), LANES)
        u2s_t[pl.ds(0, width), at] = u2s[at, :].T
        return 0

    lax.fori_loop(0, rows // LANES, turn_u2, 0)
    for b in range(max(images - 2, 0), images):
        both(hid_save(b), "wait")

    live = images * high
    tiles = 2 if live % 32 == 0 else 1
    tall = live // tiles

    def channel(t, _):
        both(own_loads(t), "wait")
        both(gather_core(t), "wait")
        at = pl.ds(al(t * 2 * step, 2 * step), 2 * step)
        weight_in, weight_out = wi[:, at], wo[at, :]
        here = pl.ds(al(t * step, step), step)
        bias = jnp.concatenate([cbs[:, here], cbo[:, here]], axis=1)
        for i in range(tiles):
            rng = pl.ds(i * tall, tall)
            pre = dot(u2s[rng, :], weight_in) + bias
            back = dot_nt(dys[rng, :], weight_out)
            phi, deriv = gelu_parts(pre)
            chid[rng, at] = (pre * phi).astype(BF16)
            dcp[rng, at] = (back * deriv).astype(BF16)

        @pl.when(t + 3 < ticks)
        def _():
            both(gather_mp(t + 3), "wait")
            both(gather_near(t + 3), "start")

        @pl.when(t + 1 < ticks)
        def _():
            both(gather_near(t + 1), "wait")
            both(gather_core(t + 1), "start")

        point(2 * t, range(0, chunks, 2))
        slot = lax.rem(t, 2)
        grad_in = dot(u2s_t[...], dcp[:, at])
        cb_acc[:, at] = grad_in[width : width + 1]
        grad_in = grad_in[:width].astype(BF16)
        grad_out = dot(dys_t[...], chid[:, at]).astype(BF16)
        for m, value in ((0, grad_in), (1, grad_out)):
            for o in (0, 1):
                for q in (0, 1):
                    first = o * step + q * LANES
                    for k in (0, 1):
                        grads[slot, m, q, o, k] = value[k * half : (k + 1) * half, first : first + LANES]
        point(2 * t + 1, range(1, chunks, 2))
        core_copy(2 * t, width // 2).start()
        core_copy(2 * t + 1, width // 2).start()
        return 0

    lax.fori_loop(0, ticks, channel, 0)

    both(hid_load(0), "start")
    patch_copy(0).start()
    twi_t[...] = twi[pl.ds(0, tokens), :].T
    gain1, gain2, out_shift = vecs[0:1], vecs[2:3], vecs[4:5]

    def backward(b, _):
        s = lax.rem(b, 2)
        rng = pl.ds(al(b * high, 16), high)

        @pl.when(b + 1 < images)
        def _():
            both(hid_load(b + 1), "start")
            patch_copy(b + 1).start()

        @pl.when(b >= 2)
        def _():
            mixed_save(b - 2).wait()
            grad_save(b - 2).wait()

        x1 = keep[b]
        ms[s] = (x1 + dot(chid[rng, :], wo[...])[:patch] + out_shift).astype(BF16)
        mixed_save(b).start()
        du2 = dot_nt(dcp[rng, :], wi[...])[:patch]
        n2 = (x1 - stats[b, :, 2:3]) * stats[b, :, 3:4]
        row_acc[pl.ds(2, 1), :] += jnp.sum(du2 * n2, 0, keepdims=True)
        row_acc[pl.ds(3, 1), :] += jnp.sum(du2, 0, keepdims=True)
        dy = dys[pl.ds(al(b * high, 16), patch), :].astype(F32)
        dx1 = dy + norm_back(du2, n2, stats[b, :, 3:4], gain2)
        keep[b] = dx1
        dtok[pl.ds(0, patch), :] = dx1.astype(BF16)
        point(chunks + 2 * b, range(chunks, chunks + 2 * images, 2))
        both(hid_load(b), "wait")
        dtk = dtok[...]
        hidden = hid[s]
        tout_acc[:, pl.ds(0, high)] += dot_nt(hidden, dtk)
        dpre = (dot(two[pl.ds(0, tokens), pl.ds(0, high)], dtk) * slope[s].astype(F32)).astype(BF16)
        tin_acc[:, pl.ds(0, high)] += dot_nt(dpre, u1s[b])
        du1 = dot(twi_t[pl.ds(0, high), :], dpre)[:patch]
        patch_copy(b).wait()
        n1 = (xs[s].astype(F32) - stats[b, :, 0:1]) * stats[b, :, 1:2]
        row_acc[pl.ds(0, 1), :] += jnp.sum(du1 * n1, 0, keepdims=True)
        row_acc[pl.ds(1, 1), :] += jnp.sum(du1, 0, keepdims=True)
        dx = keep[b] + norm_back(du1, n1, stats[b, :, 1:2], gain1)
        u2s[pl.ds(al(b * high, 16), patch), :] = dx.astype(BF16)
        grad_save(b).start()
        point(chunks + 2 * b + 1, range(chunks + 1, chunks + 2 * images, 2))
        return 0

    lax.fori_loop(0, images, backward, 0)

    blocks = width // LANES
    for o in (0, 1):
        for v in range(5):
            for j in range(blocks):
                small[o, pl.ds(v * blocks + j, 1), :] = row_acc[pl.ds(v, 1), pl.ds(j * LANES, LANES)]
        for j in range(2):
            small[o, pl.ds(5 * blocks + j, 1), :] = tout_acc[pl.ds(tokens, 1), pl.ds(j * LANES, LANES)]
        for c in range(chunks):
            first = (c // 2) * 2 * step + o * step + (c % 2) * LANES
            small[o, pl.ds(5 * blocks + 2 + c, 1), :] = cb_acc[pl.ds(0, 1), pl.ds(first, LANES)]
    last_slot = ticks % 2
    for o in (0, 1):
        for m, total in ((0, tin_acc), (1, tout_acc)):
            for j in range(2):
                grads[last_slot, m, 0, o, j, pl.ds(0, token_half), :] = total[
                    pl.ds(o * token_half, token_half), pl.ds(j * LANES, LANES)
                ].astype(BF16)
        grads[last_slot, 0, 0, o, 0, pl.ds(token_half, small.shape[1]), :] = small[o].astype(BF16)
    core_copy(chunks, last_half).start()
    for name, c in REST:
        steps[name](c, half if c < chunks else last_half, STRAIGHT.index(c) if c in STRAIGHT else 0)
    for b in range(max(images - 2, 0), images):
        mixed_save(b).wait()
        grad_save(b).wait()


def widen(
    sizes, summed, mixed_in, grad_in,
    mixed, inputs_grad, d_in, d_out, d_tin, d_tbias, d_tout, d_tshift, d_gain1, d_shift1, d_gain2, d_shift2, d_cbias, d_cshift,
    sums, last, wide_in, wide_out, hold_mixed, hold_grad, wide_grad, in_sem, out_sem, last_sem, through_sem,
):
    images, patch, high, width, token_half, chunks = sizes

    group = 3 if chunks % 3 == 0 else 1

    def span(c):
        return pl.ds(c * LANES, group * LANES)

    loads = {
        c: [
            pltpu.make_async_copy(summed.at[m, pl.ds(c, group)], sums.at[m, pl.ds(c, group)], in_sem.at[m, c]) for m in (0, 1)
        ]
        for c in range(0, chunks, group)
    }
    stores = {
        c: (
            pltpu.make_async_copy(wide_in.at[:, span(c)], d_in.at[:, span(c)], out_sem.at[0, c]),
            pltpu.make_async_copy(wide_out.at[span(c)], d_out.at[span(c)], out_sem.at[1, c]),
        )
        for c in range(0, chunks, group)
    }
    load_last = [
        pltpu.make_async_copy(summed.at[m, chunks, :, pl.ds(0, last.shape[2])], last.at[m], last_sem.at[m]) for m in (0, 1)
    ]
    ins, outs = [], []
    for b in range(images):
        ins.append(pltpu.make_async_copy(mixed_in.at[b], hold_mixed.at[b], through_sem.at[0, b]))
        outs.append(pltpu.make_async_copy(hold_mixed.at[b], mixed.at[b], through_sem.at[2, b]))
    for b in range(images):
        ins.append(pltpu.make_async_copy(grad_in.at[pl.ds(b * high, high)], hold_grad.at[b], through_sem.at[1, b]))
        outs.append(pltpu.make_async_copy(wide_grad.at[b], inputs_grad.at[b], through_sem.at[3, b]))

    def pass_on(i):
        ins[i].wait()
        if i >= images:
            wide_grad[i - images] = hold_grad[i - images, pl.ds(0, patch), :].astype(F32)
        outs[i].start()

    for pair in loads.values():
        for copy in pair:
            copy.start()
    for copy in load_last + ins:
        copy.start()
    through = iter(range(2 * images))
    for c in range(chunks):
        for copy in loads.get(c, ()):
            copy.wait()
        wide_in[:, c * LANES : (c + 1) * LANES] = sums[0, c].reshape(width, LANES).astype(F32)
        wide_out[c * LANES : (c + 1) * LANES, :] = sums[1, c].reshape(width, LANES).T.astype(F32)
        if (c + 1) % group == 0:
            for copy in stores[c + 1 - group]:
                copy.start()
        for i in [i for i in (next(through, None),) if i is not None]:
            pass_on(i)
    for i in through:
        pass_on(i)
    for copy in load_last:
        copy.wait()

    def token_block(m):
        halves = [last[m, j, pl.ds(0, token_half), :] for j in (0, 1)]
        return jnp.concatenate(halves, axis=1).astype(F32)

    grad = token_block(0)
    d_tin[...] = grad[:, :patch]
    d_tbias[...] = grad.T[patch : patch + 1].reshape(token_half)
    d_tout[...] = token_block(1)[:, :patch]
    blocks = width // LANES
    rows = last[0, 0, pl.ds(token_half, 64), :].astype(F32)

    def vector(first, count):
        return jnp.concatenate([rows[first + j : first + j + 1] for j in range(count)], axis=1)

    for v, ref in enumerate((d_gain1, d_shift1, d_gain2, d_shift2, d_cshift)):
        ref[...] = vector(v * blocks, blocks).reshape(width)
    d_tshift[...] = vector(5 * blocks, 2)[:, :patch].reshape(patch)
    d_cbias[...] = vector(5 * blocks + 2, chunks).reshape(chunks * LANES)
    for pair in stores.values():
        for copy in pair:
            copy.wait()
    for copy in outs:
        copy.wait()


def per_device(
    dp_size,
    patches, cotangent, gain_one, shift_one, token_in, token_bias, token_out, token_shift,
    gain_two, shift_two, channel_in, channel_bias, channel_out, channel_shift,
):
    images, patch, width = patches.shape
    token_half = token_in.shape[1]
    hidden_half = channel_in.shape[1]
    step = 2 * LANES
    ticks = hidden_half // step
    chunks = 2 * ticks
    high = -(-(patch + 3) // 16) * 16
    rows = -(-images * high // LANES) * LANES
    wide = -(-patch // LANES) * LANES
    tokens = 2 * token_half
    far = max(sum(1 for b in range(4, 20) if 2**b < dp_size), 1)
    far_chunks = chunks + 1 if dp_size > 16 else 1
    last_half = -(-(token_half + 64) // 64) * 64
    sizes = (images, patch, width, token_half, hidden_half, ticks, dp_size, last_half)
    hbm = pl.BlockSpec(memory_space=pl.ANY)
    n = chunks + 1
    half = width // 2
    dma = pltpu.SemaphoreType.DMA
    mixed, inputs_grad, summed, _, _ = pl.pallas_call(
        functools.partial(layer, sizes),
        out_shape=(
            jax.ShapeDtypeStruct((images, patch, width), BF16),
            jax.ShapeDtypeStruct((images * high, width), BF16),
            jax.ShapeDtypeStruct((2, n, 2, half, LANES), BF16),
            jax.ShapeDtypeStruct((images, tokens, width), BF16),
            jax.ShapeDtypeStruct((images, tokens, width), BF16),
        ),
        in_specs=[hbm] * 14,
        out_specs=(hbm,) * 5,
        scratch_shapes=[
            pltpu.VMEM((width, 2 * hidden_half), BF16),
            pltpu.VMEM((2 * hidden_half, width), BF16),
            pltpu.VMEM((8, width), F32),
            pltpu.VMEM((1, hidden_half), F32),
            pltpu.VMEM((1, hidden_half), F32),
            pltpu.VMEM((token_half,), F32),
            pltpu.VMEM((patch,), F32),
            pltpu.VMEM((token_half, patch), BF16),
            pltpu.VMEM((token_half, patch), BF16),
            pltpu.VMEM((2, tokens + 16, wide), BF16),
            pltpu.VMEM((wide, tokens), BF16),
            pltpu.VMEM((wide, tokens + 16), BF16),
            pltpu.VMEM((images, patch, width), F32),
            pltpu.VMEM((rows, width), BF16),
            pltpu.VMEM((width, rows), BF16),
            pltpu.VMEM((rows, width), BF16),
            pltpu.VMEM((width + 16, rows), BF16),
            pltpu.VMEM((images, high, width), BF16),
            pltpu.VMEM((rows, 2 * hidden_half), BF16),
            pltpu.VMEM((rows, 2 * hidden_half), BF16),
            pltpu.VMEM((high, width), BF16),
            pltpu.VMEM((2, patch, width), BF16),
            pltpu.VMEM((2, patch, width), BF16),
            pltpu.VMEM((2, tokens + 16, width), BF16),
            pltpu.VMEM((2, tokens, width), BF16),
            pltpu.VMEM((images, patch, 4), F32),
            pltpu.VMEM((8, width), F32),
            pltpu.VMEM((1, 2 * hidden_half), F32),
            pltpu.VMEM((tokens, wide), F32),
            pltpu.VMEM((tokens + 16, wide), F32),
            pltpu.VMEM((2, 64, LANES), F32),
            pltpu.VMEM((2, 2, 2, 2, 2, half, LANES), BF16),
            pltpu.VMEM((2, 2, 2, 2, half, LANES), BF16),
            pltpu.VMEM((n, 2, 2, half, LANES), BF16),
            pltpu.VMEM((n, 2, half, LANES), BF16),
            pltpu.VMEM((n, half, LANES), BF16),
            pltpu.VMEM((n, 3 * (half // 4), LANES), BF16),
            pltpu.VMEM((far_chunks, far, half // 4, LANES), BF16),
            dma((ticks, 2)),
            dma((5, 2)),
            dma((10,)),
            dma((2,)),
            dma((3,)), dma((3,)),
            dma((ticks, 4)), dma((ticks, 6)),
            dma((2, 2)), dma((2, 2)),
            dma((RING,)), dma((RING,)),
            dma((2, n)), dma((len(STRAIGHT),)), dma((n,)),
            dma((n,)), dma((n,)), dma((n,)), dma((n,)), dma((len(STRAIGHT),)),
            dma((n,)), dma((n,)), dma((len(STRAIGHT),)), dma((n,)), dma((2, n)),
            dma((far_chunks, far)), dma((far_chunks, far)),
            pltpu.SemaphoreType.REGULAR((4,)),
        ],
        compiler_params=pltpu.CompilerParams(
            collective_id=0, has_side_effects=True, vmem_limit_bytes=63 * 2**20
        ),
        name="mixer_layer",
    )(
        patches, cotangent, gain_one, shift_one, token_in.T, token_bias, token_out, token_shift,
        gain_two, shift_two, channel_in, channel_bias, channel_out, channel_shift,
    )

    vmem = pl.BlockSpec(memory_space=pltpu.VMEM)
    shapes = (
        (token_half, patch), (token_half,), (token_half, patch), (patch,),
        (width,), (width,), (width,), (width,), (hidden_half,), (width,),
    )
    (
        mixed, inputs_grad, d_in, d_out, d_tin, d_tbias, d_tout, d_tshift,
        d_gain1, d_shift1, d_gain2, d_shift2, d_cbias, d_cshift,
    ) = pl.pallas_call(
        functools.partial(widen, (images, patch, high, width, token_half, chunks)),
        in_specs=[hbm] * 3,
        out_specs=(hbm,) * 4 + (vmem,) * len(shapes),
        out_shape=(
            jax.ShapeDtypeStruct((images, patch, width), BF16),
            jax.ShapeDtypeStruct((images, patch, width), F32),
            jax.ShapeDtypeStruct((width, hidden_half), F32),
            jax.ShapeDtypeStruct((hidden_half, width), F32),
        ) + tuple(jax.ShapeDtypeStruct(shape, F32) for shape in shapes),
        scratch_shapes=[
            pltpu.VMEM((2, chunks, 2, half, LANES), BF16),
            pltpu.VMEM((2, 2, last_half, LANES), BF16),
            pltpu.VMEM((width, hidden_half), F32),
            pltpu.VMEM((hidden_half, width), F32),
            pltpu.VMEM((images, patch, width), BF16),
            pltpu.VMEM((images, high, width), BF16),
            pltpu.VMEM((images, patch, width), F32),
            dma((2, chunks)), dma((2, chunks)), dma((2,)), dma((4, images)),
        ],
        compiler_params=pltpu.CompilerParams(vmem_limit_bytes=60 * 2**20),
        name="widen",
    )(summed, mixed, inputs_grad)
    return (
        mixed, inputs_grad, d_gain1, d_shift1, d_tin.T, d_tbias, d_tout, d_tshift,
        d_gain2, d_shift2, d_in, d_cbias, d_out, d_cshift,
    )


def solution(mesh):
    split = P(("dp", "mp"), None, None)
    columns, rows, vector = P(None, "mp"), P("mp", None), P("mp")
    return jax.shard_map(
        functools.partial(per_device, mesh.shape["dp"]),
        mesh=mesh,
        in_specs=(
            split, split, P(), P(), columns, vector, rows, P(), P(), P(), columns, vector, rows, P(),
        ),
        out_specs=(
            split, split, P(), P(), columns, vector, rows, P(), P(), P(), columns, vector, rows, P(),
        ),
        check_vma=False,
    )
```

```python
import functools

import jax
import jax.numpy as jnp
from jax import lax
from jax.experimental import pallas as pl
from jax.experimental.pallas import tpu as pltpu
from jax.sharding import PartitionSpec as P

MESH = pl.DeviceIdType.MESH
F32 = jnp.float32
BF16 = jnp.bfloat16
NT = (((1,), (1,)), ((), ()))
LANES = 128
RING = 4

STRAIGHT = (4, 5, 8, 9, 11, 12)
POINTS = (
    ("core_mp", ((0, 2), (2, 4), (3, 5), (4, 6), (5, 7), (6, 8), (8, 10), (9, 11), (11, 13))),
    ("core_both", ((1, 3), (7, 9), (10, 12))),
    ("mp", ((0, 6), (2, 7), (3, 10), (4, 11), (5, 13), (6, 16), (8, 17), (9, 19), (11, 21))),
    ("both", ((1, 7), (7, 12), (10, 16))),
    ("side", ((0, 10), (2, 11), (3, 13), (6, 18))),
    ("side_line", ((4, 14), (5, 17), (8, 19), (9, 21))),
    ("then_mp", ((1, 14), (7, 19), (10, 23))),
    ("low", ((0, 12), (2, 13), (3, 15), (1, 16), (6, 20), (7, 22))),
    ("high", ((0, 14), (2, 15), (3, 17), (1, 18), (6, 23))),
    ("line", ((4, 16), (5, 19), (8, 21))),
    ("high_spread", ((0, 16), (2, 17), (3, 20), (1, 21))),
    ("low_spread", ((0, 18), (2, 20), (3, 23))),
    ("spread", ((4, 20), (5, 22))),
    ("side_spread", ((0, 20), (2, 22), (4, 23))),
    ("core_spread", ((0, 21), (2, 23))),
)
REST = (
    ("side_line", 11), ("low_spread", 1), ("core_mp", 12), ("core_spread", 4), ("line", 9), ("side_spread", 5),
    ("spread", 8), ("low", 10), ("core_spread", 5), ("high_spread", 6), ("high", 7), ("line", 11),
    ("side_spread", 3), ("mp", 12), ("spread", 9), ("side_spread", 1), ("core_spread", 3), ("high", 10),
    ("core_spread", 1), ("low_spread", 6), ("high_spread", 7), ("side_spread", 8), ("side_line", 12),
    ("core_spread", 8), ("spread", 11), ("high_spread", 10), ("side_spread", 9), ("low_spread", 7),
    ("side_spread", 6), ("line", 12), ("low_spread", 10), ("side_spread", 11), ("core_spread", 9), ("spread", 12),
    ("core_spread", 6), ("side_spread", 7), ("side_spread", 10), ("core_spread", 7), ("side_spread", 12),
    ("core_spread", 11), ("core_spread", 10), ("core_spread", 12),
)


def dot(a, b):
    return jnp.dot(a, b, preferred_element_type=F32)


def dot_nt(a, b):
    return lax.dot_general(a, b, NT, preferred_element_type=F32)


def centre(values):
    centred = values - jnp.mean(values, -1, keepdims=True)
    return centred, lax.rsqrt(jnp.mean(centred * centred, -1, keepdims=True) + 1e-06)


def norm_back(grad, normed, scale, gain):
    scaled = grad * gain
    return scale * (
        scaled
        - jnp.mean(scaled, -1, keepdims=True)
        - normed * jnp.mean(scaled * normed, -1, keepdims=True)
    )


def phi_of(v):
    return 0.5 + 0.5 * lax.erf(v * 0.7071067811865476)


def gelu_parts(v):
    phi = phi_of(v)
    return phi, phi + v * (0.3989422804014327 * jnp.exp(-0.5 * v * v))


def layer(
    sizes,
    patches, cotangent, gain_one, shift_one, token_in, token_bias, token_out, token_shift,
    gain_two, shift_two, channel_in, channel_bias, channel_out, channel_shift,
    mixed, inputs_grad, summed, hid_out, before_out,
    wi, wo, vecs, cbs, cbo, tbs, tss, tins, touts, tw, twi_t, two_t, keep,
    dys, dys_t, u2s, u2s_t, u1s, chid, dcp, dtok,
    xs, ms, hid, before, stats,
    row_acc, cb_acc, tin_acc, tout_acc, small,
    grads, from_core, acc, from_mp, from_x, from_z, from_far,
    load_sem, stage_sem, small_sem, grad_sem, tok_s, tok_r, w_s, w_r, wc_s, wc_r, c_s, c_r, g_s, line_s, l_sem, y_r, x_r, z_r, zh_r, zl_r,
    a_r, al_r, sl_r, xa_r, ca_r, far_s, far_r, hello,
):
    images, patch, width, token_half, hidden_half, ticks, dp_size, last_half = sizes
    rows = dys.shape[0]
    high = u1s.shape[1]
    step = hidden_half // ticks
    half = width // 2
    chunks = 2 * ticks
    eighth_in = width // 8

    dp = lax.axis_index("dp")
    mp = lax.axis_index("mp")
    core = lax.rem(dp, 2)
    side = lax.rem(lax.div(dp, 2), 2)
    near = lax.rem(lax.div(dp, 2), 4)
    line = lax.rem(lax.div(dp, 4), 4)
    part = core * 4 + near
    low = lax.rem(line, 2)

    to_mp = {"mp": 1 - mp}
    to_core = {"dp": dp + 1 - 2 * core}
    to_side = {"dp": dp + 2 - 4 * side}

    def near_of(r):
        return {"dp": dp + 2 * (lax.rem(near + r, 4) - near)}

    def line_of(r):
        return {"dp": dp + 4 * (lax.rem(line + r, 4) - line)}

    far_bits = []
    bit = 16
    while bit < dp_size:
        far_bits.append(bit)
        bit *= 2

    def far_of(i):
        b = far_bits[i]
        return {"dp": dp + b - 2 * b * lax.rem(lax.div(dp, b), 2)}

    def remote(src, dst, send, recv, device):
        return pltpu.make_async_remote_copy(
            src_ref=src, dst_ref=dst, send_sem=send, recv_sem=recv, device_id=device, device_id_type=MESH
        )

    def al(v, m):
        return pl.multiple_of(v, m)

    def own_loads(t):
        return (
            pltpu.make_async_copy(
                channel_in.at[:, pl.ds(al(t * step, step), step)],
                wi.at[:, pl.ds(al(t * 2 * step, step), step)],
                load_sem.at[t, 0],
            ),
            pltpu.make_async_copy(
                channel_out.at[pl.ds(al(t * step, step), step), :],
                wo.at[pl.ds(al(t * 2 * step, step), step), :],
                load_sem.at[t, 1],
            ),
        )

    def other_in(t, first, count):
        return wi.at[pl.ds(al(first, eighth_in), count), pl.ds(al(t * 2 * step + step, step), step)]

    def other_out(t, first, count):
        return wo.at[pl.ds(al(t * 2 * step + step + first, 16), count), :]

    which = side + core * (low - side)
    quarter_out = step // 4
    to_pair = {"dp": dp + (2 - 4 * side) * (1 - core) + (4 - 8 * low) * core}

    def gather_mp(t):
        first = core * 2 * quarter_out + which * quarter_out
        return (
            remote(
                channel_in.at[pl.ds(al(part * eighth_in, eighth_in), eighth_in), pl.ds(al(t * step, step), step)],
                other_in(t, part * eighth_in, eighth_in),
                w_s.at[t, 0], w_r.at[t, 0], to_mp,
            ),
            remote(
                channel_out.at[pl.ds(al(t * step + first, 16), quarter_out), :],
                other_out(t, first, quarter_out),
                w_s.at[t, 1], w_r.at[t, 1], to_mp,
            ),
        )

    def gather_near(t):
        a = other_in(t, part * eighth_in, eighth_in)
        b = other_out(t, core * 2 * quarter_out + which * quarter_out, quarter_out)
        copies = [remote(a, a, w_s.at[t, r - 1], w_r.at[t, r + 1], near_of(r)) for r in (1, 2, 3)]
        return copies + [remote(b, b, w_s.at[t, 3], w_r.at[t, 5], to_pair)]

    def gather_core(t):
        a = other_in(t, core * 4 * eighth_in, 4 * eighth_in)
        b = other_out(t, core * 2 * quarter_out, 2 * quarter_out)
        s = lax.rem(t, 2)
        return (
            remote(a, a, wc_s.at[s, 0], wc_r.at[s, 0], to_core),
            remote(b, b, wc_s.at[s, 1], wc_r.at[s, 1], to_core),
        )

    def token_mp():
        return (
            remote(
                tw.at[core, pl.ds(0, token_half)], tw.at[core, pl.ds(token_half, token_half)], tok_s.at[0], tok_r.at[0], to_mp
            ),
        )

    def bias_mp():
        return (remote(cbs, cbo, tok_s.at[1], tok_r.at[1], to_mp),)

    def token_core():
        ref = tw.at[core, pl.ds(token_half, token_half)]
        return (remote(ref, ref, tok_s.at[2], tok_r.at[2], to_core),)

    high_bit = lax.div(line, 2)
    to_low = {"dp": dp + 4 - 8 * low}
    to_high = {"dp": dp + 8 - 16 * high_bit}

    def rows_at(first, count):
        return pl.ds(al(first, 16), count)

    def core_copy(c, h):
        slot, q, i = lax.rem(lax.div(c, 2), 2), lax.rem(c, 2), lax.rem(c, RING)
        rng = pl.ds(0, h)
        return remote(
            grads.at[slot, 1 - core, q, :, :, rng], from_core.at[slot, q, :, :, rng], c_s.at[i], c_r.at[i], to_core
        )

    def mp_copy(c, h):
        rng = pl.ds(0, h)
        return remote(acc.at[c, 1, :, rng], from_mp.at[c, :, rng], g_s.at[0, c], y_r.at[c], to_mp)

    def side_copy(c, h):
        rng = pl.ds(0, h)
        return remote(acc.at[c, 0, 1 - side, rng], from_x.at[c, rng], g_s.at[0, c], x_r.at[c], to_side)

    def both_copy(c):
        return remote(acc.at[c, :, 1 - side], from_mp.at[c], g_s.at[0, c], x_r.at[c], to_side)

    def then_mp_copy(c):
        return remote(acc.at[c, 1, side], from_x.at[c], g_s.at[0, c], y_r.at[c], to_mp)

    def low_copy(c, h):
        n = h // 2
        src = acc.at[c, 0, side, rows_at((1 - low) * n, n)]
        return remote(src, from_z.at[c, pl.ds(0, n)], g_s.at[0, c], z_r.at[c], to_low)

    def high_copy(c, h):
        n = h // 4
        src = acc.at[c, 0, side, rows_at(low * 2 * n + (1 - high_bit) * n, n)]
        return remote(src, from_z.at[c, pl.ds(2 * n, n)], g_s.at[0, c], zh_r.at[c], to_high)

    def at_place(c, h):
        return rows_at(low * (h // 2) + high_bit * (h // 4), h // 4)

    def at_line(h, place):
        return rows_at(place * (h // 4), h // 4)

    def line_sems(c, d, first, second, third):
        return ((first.at[c], second.at[c], third.at[d])[r] for r in range(3))

    def line_copies(c, h, d):
        sends = line_sems(c, d, g_s.at[0], g_s.at[1], line_s)
        recvs = line_sems(c, d, z_r, zh_r, zl_r)
        return [
            remote(
                acc.at[c, 0, side, at_line(h, lax.rem(line + r, 4))],
                from_z.at[c, pl.ds((r - 1) * (h // 4), h // 4)], send, recv, line_of(r),
            )
            for r, send, recv in zip((1, 2, 3), sends, recvs)
        ]

    def sums_of(c, rng):
        return from_mp.at[c, 0, rng]

    def keep_copy(c, h):
        rng = pl.ds(0, h)
        return pltpu.make_async_copy(sums_of(c, rng), summed.at[core, c, side, rng], l_sem.at[c])

    def high_spread_copy(c, h):
        ref = sums_of(c, at_place(c, h))
        return remote(ref, ref, g_s.at[0, c], a_r.at[c], to_high)

    def low_spread_copy(c, h):
        ref = sums_of(c, rows_at(low * (h // 2), h // 2))
        return remote(ref, ref, g_s.at[0, c], al_r.at[c], to_low)

    def spread_copies(c, h, d):
        ref = sums_of(c, at_line(h, line))
        sends = line_sems(c, d, g_s.at[0], g_s.at[1], line_s)
        recvs = line_sems(c, d, a_r, al_r, sl_r)
        return [remote(ref, ref, send, recv, line_of(r)) for r, send, recv in zip((1, 2, 3), sends, recvs)]

    def side_spread_copy(c, h):
        rng = pl.ds(0, h)
        return remote(sums_of(c, rng), summed.at[core, c, side, rng], g_s.at[0, c], xa_r.at[c], to_side)

    def core_own_copy(c, h):
        rng = pl.ds(0, h)
        return remote(sums_of(c, rng), summed.at[core, c, side, rng], g_s.at[1, c], ca_r.at[0, c], to_core)

    def core_other_copy(c, h):
        ref = summed.at[core, c, 1 - side, pl.ds(0, h)]
        return remote(ref, ref, g_s.at[0, c], ca_r.at[1, c], to_core)

    def add(a, b):
        return (a.astype(F32) + b.astype(F32)).astype(BF16)

    def core_step(c, h, send):
        core_copy(c, h).wait()
        slot, q, rng = lax.rem(lax.div(c, 2), 2), lax.rem(c, 2), pl.ds(0, h)
        acc[c, 1, :, rng] = add(grads[slot, core, q, 1, :, rng], from_core[slot, q, 1, :, rng])
        if send is mp_copy:
            send(c, h).start()
        acc[c, 0, :, rng] = add(grads[slot, core, q, 0, :, rng], from_core[slot, q, 0, :, rng])
        if send is both_copy:
            send(c).start()

    def core_mp(c, h, d):
        core_step(c, h, mp_copy)

    def core_both(c, h, d):
        core_step(c, h, both_copy)

    def mp_step(c, h, d):
        mp_copy(c, h).wait()
        rng = pl.ds(0, h)
        acc[c, 0, 1 - side, rng] = add(acc[c, 0, 1 - side, rng], from_mp[c, 1 - side, rng])
        side_copy(c, h).start()
        acc[c, 0, side, rng] = add(acc[c, 0, side, rng], from_mp[c, side, rng])

    def side_step(c, h, d):
        side_copy(c, h).wait()
        rng = pl.ds(0, h)
        acc[c, 0, side, rng] = add(acc[c, 0, side, rng], from_x[c, rng])
        low_copy(c, h).start()

    def side_line(c, h, d):
        side_copy(c, h).wait()
        rng = pl.ds(0, h)
        acc[c, 0, side, rng] = add(acc[c, 0, side, rng], from_x[c, rng])
        for copy in line_copies(c, h, d):
            copy.start()

    def both_step(c, h, d):
        both_copy(c).wait()
        acc[c, 1, side] = add(acc[c, 1, side], from_mp[c, 1])
        then_mp_copy(c).start()
        acc[c, 0, side] = add(acc[c, 0, side], from_mp[c, 0])

    def then_mp_step(c, h, d):
        then_mp_copy(c).wait()
        acc[c, 0, side] = add(acc[c, 0, side], from_x[c])
        low_copy(c, h).start()

    def low_step(c, h, d):
        low_copy(c, h).wait()
        rng = rows_at(low * (h // 2), h // 2)
        acc[c, 0, side, rng] = add(acc[c, 0, side, rng], from_z[c, pl.ds(0, h // 2)])
        high_copy(c, h).start()

    def over_far(c, rng, count):
        for i in range(len(far_bits)):
            dst = from_far.at[c, i, pl.ds(0, count)]
            copy = remote(sums_of(c, rng), dst, far_s.at[c, i], far_r.at[c, i], far_of(i))
            copy.start()
            copy.wait()
            from_mp[c, 0, rng] = add(from_mp[c, 0, rng], from_far[c, i, pl.ds(0, count)])

    def high_step(c, h, d):
        high_copy(c, h).wait()
        rng = at_place(c, h)
        from_mp[c, 0, rng] = add(acc[c, 0, side, rng], from_z[c, pl.ds(h // 2, h // 4)])
        over_far(c, rng, h // 4)
        high_spread_copy(c, h).start()

    def high_spread_step(c, h, d):
        high_spread_copy(c, h).wait()
        low_spread_copy(c, h).start()

    def low_spread_step(c, h, d):
        low_spread_copy(c, h).wait()
        side_spread_copy(c, h).start()
        core_own_copy(c, h).start()
        keep_copy(c, h).start()

    def line_step(c, h, d):
        for copy in line_copies(c, h, d):
            copy.wait()
        rng = at_line(h, line)
        total = acc[c, 0, side, rng].astype(F32)
        for r in range(3):
            total = total + from_z[c, pl.ds(r * (h // 4), h // 4)].astype(F32)
        from_mp[c, 0, rng] = total.astype(BF16)
        over_far(c, rng, h // 4)
        for copy in spread_copies(c, h, d):
            copy.start()

    def spread_step(c, h, d):
        for copy in spread_copies(c, h, d):
            copy.wait()
        side_spread_copy(c, h).start()
        core_own_copy(c, h).start()
        keep_copy(c, h).start()

    def side_spread_step(c, h, d):
        side_spread_copy(c, h).wait()
        core_other_copy(c, h).start()

    def core_spread_step(c, h, d):
        core_own_copy(c, h).wait()
        keep_copy(c, h).wait()
        core_other_copy(c, h).wait()

    steps = {
        "core_mp": core_mp, "core_both": core_both, "mp": mp_step, "side": side_step, "side_line": side_line, "both": both_step,
        "then_mp": then_mp_step, "low": low_step, "high": high_step, "high_spread": high_spread_step,
        "low_spread": low_spread_step, "line": line_step, "spread": spread_step,
        "side_spread": side_spread_step, "core_spread": core_spread_step,
    }

    def point(p, places):
        for name, entries in POINTS:
            here = [(c, at) for c, at in entries if at in places]
            if here:
                now = [(p == at).astype(jnp.int32) for _, at in here]
                c = sum(c * one for (c, _), one in zip(here, now))
                d = sum(STRAIGHT.index(c) * one for (c, _), one in zip(here, now) if c in STRAIGHT)

                @pl.when(sum(now) > 0)
                def _(c=c, d=d, name=name):
                    steps[name](c, half, d)

    barrier = pltpu.get_barrier_semaphore()
    to_mid = {"dp": dp + 4 * (3 - 2 * line)}
    is_mid = lax.rem(lax.div(line + 1, 2), 2)
    greet = [to_mp, to_core, to_side, to_low] + [far_of(i) for i in range(len(far_bits))]
    for device in greet:
        pl.semaphore_signal(barrier, inc=1, device_id=device, device_id_type=MESH)

    @pl.when(is_mid == 1)
    def _():
        pl.semaphore_signal(barrier, inc=1, device_id=to_mid, device_id_type=MESH)

    def tell(i, device):
        pl.semaphore_signal(hello.at[i], inc=1, device_id=device, device_id_type=MESH)

    def first_word():
        tell(0, to_side)
        tell(1, to_low)

        @pl.when(is_mid == 1)
        def _():
            tell(2, to_mid)

    def second_word():
        for i in (0, 1):
            pl.semaphore_wait(hello.at[i], 1)

        @pl.when(is_mid == 1)
        def _():
            pl.semaphore_wait(hello.at[2], 1)

        tell(3, to_low)

    def last_word():
        pl.semaphore_wait(hello.at[3], 1)


    def patch_copy(b):
        return pltpu.make_async_copy(patches.at[b], xs.at[lax.rem(b, 2)], stage_sem.at[0, lax.rem(b, 2)])

    def cot_copy(b):
        return pltpu.make_async_copy(cotangent.at[b], ms.at[lax.rem(b, 2)], stage_sem.at[1, lax.rem(b, 2)])

    def hid_save(b):
        s = lax.rem(b, 2)
        return (
            pltpu.make_async_copy(hid.at[s, pl.ds(0, 2 * token_half)], hid_out.at[b], stage_sem.at[2, s]),
            pltpu.make_async_copy(before.at[s], before_out.at[b], stage_sem.at[3, s]),
        )

    def hid_load(b):
        s = lax.rem(b, 2)
        return (
            pltpu.make_async_copy(hid_out.at[b], hid.at[s, pl.ds(0, 2 * token_half)], stage_sem.at[2, s]),
            pltpu.make_async_copy(before_out.at[b], before.at[s], stage_sem.at[3, s]),
        )

    def grad_save(b):
        rng = pl.ds(al(b * high, 16), high)
        return pltpu.make_async_copy(u2s.at[rng], inputs_grad.at[rng], grad_sem.at[lax.rem(b, 2)])

    def mixed_save(b):
        s = lax.rem(b, 2)
        return pltpu.make_async_copy(ms.at[s], mixed.at[b], stage_sem.at[4, s])

    def both(copies, what):
        for copy in copies:
            getattr(copy, what)()

    def small_loads():
        pairs = [(token_in, tins), (token_out, touts), (token_bias, tbs), (token_shift, tss), (channel_bias, cbs.at[0])]
        vectors = (gain_one, shift_one, gain_two, shift_two, channel_shift)
        pairs += [(ref, vecs.at[i]) for i, ref in enumerate(vectors)]
        return [pltpu.make_async_copy(src, dst, small_sem.at[i]) for i, (src, dst) in enumerate(pairs)]

    both(small_loads(), "start")
    for b in (0, 1):
        patch_copy(b).start()
        cot_copy(b).start()

    wide = tw.shape[2]
    twi, two = tw.at[0], tw.at[1]

    def three(row):
        hi = row.astype(BF16).astype(F32)
        mid = (row - hi).astype(BF16).astype(F32)
        return hi, mid, row - hi - mid

    twi[pl.ds(0, token_half), :] = jnp.zeros((token_half, wide), BF16)
    two[pl.ds(0, token_half), :] = jnp.zeros((token_half, wide), BF16)
    at_row = lax.broadcasted_iota(jnp.int32, (16, wide), 0)
    at_lane = lax.broadcasted_iota(jnp.int32, (token_half, wide), 1)
    both(small_loads(), "wait")
    twi[pl.ds(0, token_half), pl.ds(0, patch)] = tins[...]
    two[pl.ds(0, token_half), pl.ds(0, patch)] = touts[...]
    padded = jnp.zeros((1, wide - token_half), F32)
    bias_row = jnp.concatenate([tbs[...].reshape(1, token_half), padded], axis=1)
    column = jnp.broadcast_to(bias_row, (LANES, wide)).T[:token_half, 0:1]
    filled = twi[pl.ds(0, token_half), :].astype(F32)
    for i, value in enumerate(three(column)):
        filled = jnp.where(at_lane == patch + i, value, filled)
    twi[pl.ds(0, token_half), :] = filled.astype(BF16)
    shift_row = jnp.concatenate([tss[...].reshape(1, patch), jnp.zeros((1, wide - patch), F32)], axis=1)
    extra = jnp.zeros((16, wide), F32)
    for i, value in enumerate(three(shift_row)):
        extra = jnp.where(at_row == i, value, extra)
    tokens = 2 * token_half
    two[pl.ds(tokens, 16), :] = extra.astype(BF16)

    pl.semaphore_wait(barrier, len(greet) + is_mid)
    both(token_mp(), "start")
    both(gather_mp(0), "start")
    first_word()
    both(bias_mp(), "start")

    def start_own(t, _):
        both(own_loads(t), "start")
        return 0

    lax.fori_loop(0, ticks, start_own, 0)

    dys[...] = jnp.zeros_like(dys)
    u2s[...] = jnp.zeros_like(u2s)
    dtok[...] = jnp.zeros_like(dtok)
    rest_rows = rows - images * high
    if rest_rows:
        chid[pl.ds(images * high, rest_rows), :] = jnp.zeros((rest_rows, chid.shape[1]), BF16)
        dcp[pl.ds(images * high, rest_rows), :] = jnp.zeros((rest_rows, dcp.shape[1]), BF16)
    row_acc[...] = jnp.zeros_like(row_acc)
    tin_acc[...] = jnp.zeros_like(tin_acc)
    tout_acc[...] = jnp.zeros_like(tout_acc)
    small[...] = jnp.zeros_like(small)
    u2s_t[pl.ds(width, 16), :] = jnp.ones((16, rows), BF16)
    for s in (0, 1):
        hid[s, pl.ds(tokens, 16), :] = jnp.ones((16, width), BF16)

    below = lax.broadcasted_iota(jnp.int32, (high, width), 0)
    ones = jnp.where(jnp.logical_and(below >= patch, below < patch + 3), 1.0, 0.0).astype(BF16)
    for b in range(images):
        u1s[b] = ones

    gain1, shift1, gain2, shift2 = (vecs[i : i + 1] for i in range(4))

    def first_norm(b, _):
        s = lax.rem(b, 2)
        patch_copy(b).wait()
        x = xs[s].astype(F32)

        @pl.when(b + 2 < images)
        def _():
            patch_copy(b + 2).start()

        keep[b] = x
        mean = jnp.mean(x, -1, keepdims=True)
        centred = x - mean
        scale = lax.rsqrt(jnp.mean(centred * centred, -1, keepdims=True) + 1e-06)
        stats[b, :, 0:1] = mean
        stats[b, :, 1:2] = scale
        u1s[b, pl.ds(0, patch), :] = (centred * scale * gain1 + shift1).astype(BF16)
        pre = dot(twi[pl.ds(0, token_half), pl.ds(0, high)], u1s[b])
        at = pl.ds(al(b * token_half, 16), token_half)
        chid[at, pl.ds(0, width)] = (pre * phi_of(pre)).astype(BF16)
        dcp[at, pl.ds(0, width)] = pre.astype(BF16)
        cot_copy(b).wait()
        value = ms[s]

        @pl.when(b + 2 < images)
        def _():
            cot_copy(b + 2).start()

        @pl.when(b + 1 < ticks)
        def _():
            both(gather_mp(b + 1), "start")

        @pl.when(b == images // 2)
        def _():
            both(token_mp(), "wait")
            both(token_core(), "start")

        dys[pl.ds(al(b * high, 16), patch), :] = value
        row_acc[pl.ds(4, 1), :] += jnp.sum(value.astype(F32), 0, keepdims=True)
        return 0

    lax.fori_loop(0, images, first_norm, 0)
    for t in range(images + 1, ticks):
        both(gather_mp(t), "start")

    def turn_dy(j, _):
        at = pl.ds(al(j * LANES, LANES), LANES)
        dys_t[:, at] = dys[at, :].T
        return 0

    lax.fori_loop(0, rows // LANES, turn_dy, 0)

    second_word()
    both(token_core(), "wait")
    two_t[...] = two[...].T

    def token_forward(b, _):
        s = lax.rem(b, 2)
        pre = dot(twi[pl.ds(token_half, token_half), pl.ds(0, high)], u1s[b])

        @pl.when(b >= 2)
        def _():
            both(hid_save(b - 2), "wait")

        at = pl.ds(al(b * token_half, 16), token_half)
        hid[s, pl.ds(0, token_half), :] = chid[at, pl.ds(0, width)]
        before[s, pl.ds(0, token_half), :] = dcp[at, pl.ds(0, width)]
        hid[s, pl.ds(token_half, token_half), :] = (pre * phi_of(pre)).astype(BF16)
        before[s, pl.ds(token_half, token_half), :] = pre.astype(BF16)
        both(hid_save(b), "start")
        x1 = keep[b] + dot(two_t[pl.ds(0, high), :], hid[s])[:patch]
        keep[b] = x1
        mean = jnp.mean(x1, -1, keepdims=True)
        centred = x1 - mean
        scale = lax.rsqrt(jnp.mean(centred * centred, -1, keepdims=True) + 1e-06)
        stats[b, :, 2:3] = mean
        stats[b, :, 3:4] = scale
        u2s[pl.ds(al(b * high, 16), patch), :] = (centred * scale * gain2 + shift2).astype(BF16)

        for t, when in enumerate((0, images // 2, images - 1)):

            @pl.when(b == when)
            def _(t=t):
                both(gather_mp(t), "wait")
                both(gather_near(t), "start")

        return 0

    lax.fori_loop(0, images, token_forward, 0)
    both(gather_near(0), "wait")
    both(gather_core(0), "start")
    both(bias_mp(), "wait")
    last_word()

    def turn_u2(j, _):
        at = pl.ds(al(j * LANES, LANES), LANES)
        u2s_t[pl.ds(0, width), at] = u2s[at, :].T
        return 0

    lax.fori_loop(0, rows // LANES, turn_u2, 0)
    for b in range(max(images - 2, 0), images):
        both(hid_save(b), "wait")

    live = images * high
    tiles = 2 if live % 32 == 0 else 1
    tall = live // tiles

    def channel(t, _):
        both(own_loads(t), "wait")
        both(gather_core(t), "wait")
        at = pl.ds(al(t * 2 * step, 2 * step), 2 * step)
        weight_in, weight_out = wi[:, at], wo[at, :]
        here = pl.ds(al(t * step, step), step)
        bias = jnp.concatenate([cbs[:, here], cbo[:, here]], axis=1)
        for i in range(tiles):
            rng = pl.ds(i * tall, tall)
            pre = dot(u2s[rng, :], weight_in) + bias
            back = dot_nt(dys[rng, :], weight_out)
            phi, deriv = gelu_parts(pre)
            chid[rng, at] = (pre * phi).astype(BF16)
            dcp[rng, at] = (back * deriv).astype(BF16)

        @pl.when(t + 3 < ticks)
        def _():
            both(gather_mp(t + 3), "wait")
            both(gather_near(t + 3), "start")

        @pl.when(t + 1 < ticks)
        def _():
            both(gather_near(t + 1), "wait")
            both(gather_core(t + 1), "start")

        point(2 * t, range(0, chunks, 2))
        slot = lax.rem(t, 2)
        grad_in = dot(u2s_t[...], dcp[:, at])
        cb_acc[:, at] = grad_in[width : width + 1]
        grad_in = grad_in[:width].astype(BF16)
        grad_out = dot(dys_t[...], chid[:, at]).astype(BF16)
        for m, value in ((0, grad_in), (1, grad_out)):
            for o in (0, 1):
                for q in (0, 1):
                    first = o * step + q * LANES
                    for k in (0, 1):
                        grads[slot, m, q, o, k] = value[k * half : (k + 1) * half, first : first + LANES]
        point(2 * t + 1, range(1, chunks, 2))
        core_copy(2 * t, width // 2).start()
        core_copy(2 * t + 1, width // 2).start()
        return 0

    lax.fori_loop(0, ticks, channel, 0)

    both(hid_load(0), "start")
    patch_copy(0).start()
    twi_t[...] = twi[pl.ds(0, tokens), :].T
    gain1, gain2, out_shift = vecs[0:1], vecs[2:3], vecs[4:5]

    def backward(b, _):
        s = lax.rem(b, 2)
        rng = pl.ds(al(b * high, 16), high)

        @pl.when(b + 1 < images)
        def _():
            both(hid_load(b + 1), "start")
            patch_copy(b + 1).start()

        @pl.when(b >= 2)
        def _():
            mixed_save(b - 2).wait()
            grad_save(b - 2).wait()

        x1 = keep[b]
        ms[s] = (x1 + dot(chid[rng, :], wo[...])[:patch] + out_shift).astype(BF16)
        mixed_save(b).start()
        du2 = dot_nt(dcp[rng, :], wi[...])[:patch]
        n2 = (x1 - stats[b, :, 2:3]) * stats[b, :, 3:4]
        row_acc[pl.ds(2, 1), :] += jnp.sum(du2 * n2, 0, keepdims=True)
        row_acc[pl.ds(3, 1), :] += jnp.sum(du2, 0, keepdims=True)
        dy = dys[pl.ds(al(b * high, 16), patch), :].astype(F32)
        dx1 = dy + norm_back(du2, n2, stats[b, :, 3:4], gain2)
        keep[b] = dx1
        dtok[pl.ds(0, patch), :] = dx1.astype(BF16)
        point(chunks + 2 * b, range(chunks, chunks + 2 * images, 2))
        both(hid_load(b), "wait")
        dtk = dtok[...]
        hidden = hid[s]
        tout_acc[:, pl.ds(0, high)] += dot_nt(hidden, dtk)
        dpre = (dot(two[pl.ds(0, tokens), pl.ds(0, high)], dtk) * gelu_parts(before[s].astype(F32))[1]).astype(BF16)
        tin_acc[:, pl.ds(0, high)] += dot_nt(dpre, u1s[b])
        du1 = dot(twi_t[pl.ds(0, high), :], dpre)[:patch]
        patch_copy(b).wait()
        n1 = (xs[s].astype(F32) - stats[b, :, 0:1]) * stats[b, :, 1:2]
        row_acc[pl.ds(0, 1), :] += jnp.sum(du1 * n1, 0, keepdims=True)
        row_acc[pl.ds(1, 1), :] += jnp.sum(du1, 0, keepdims=True)
        dx = keep[b] + norm_back(du1, n1, stats[b, :, 1:2], gain1)
        u2s[pl.ds(al(b * high, 16), patch), :] = dx.astype(BF16)
        grad_save(b).start()
        point(chunks + 2 * b + 1, range(chunks + 1, chunks + 2 * images, 2))
        return 0

    lax.fori_loop(0, images, backward, 0)

    blocks = width // LANES
    for o in (0, 1):
        for v in range(5):
            for j in range(blocks):
                small[o, pl.ds(v * blocks + j, 1), :] = row_acc[pl.ds(v, 1), pl.ds(j * LANES, LANES)]
        for j in range(2):
            small[o, pl.ds(5 * blocks + j, 1), :] = tout_acc[pl.ds(tokens, 1), pl.ds(j * LANES, LANES)]
        for c in range(chunks):
            first = (c // 2) * 2 * step + o * step + (c % 2) * LANES
            small[o, pl.ds(5 * blocks + 2 + c, 1), :] = cb_acc[pl.ds(0, 1), pl.ds(first, LANES)]
    last_slot = ticks % 2
    for o in (0, 1):
        for m, total in ((0, tin_acc), (1, tout_acc)):
            for j in range(2):
                grads[last_slot, m, 0, o, j, pl.ds(0, token_half), :] = total[
                    pl.ds(o * token_half, token_half), pl.ds(j * LANES, LANES)
                ].astype(BF16)
        grads[last_slot, 0, 0, o, 0, pl.ds(token_half, small.shape[1]), :] = small[o].astype(BF16)
    core_copy(chunks, last_half).start()
    for name, c in REST:
        steps[name](c, half if c < chunks else last_half, STRAIGHT.index(c) if c in STRAIGHT else 0)
    for b in range(max(images - 2, 0), images):
        mixed_save(b).wait()
        grad_save(b).wait()


def widen(
    sizes, summed, mixed_in, grad_in,
    mixed, inputs_grad, d_in, d_out, d_tin, d_tbias, d_tout, d_tshift, d_gain1, d_shift1, d_gain2, d_shift2, d_cbias, d_cshift,
    sums, last, wide_in, wide_out, hold_mixed, hold_grad, wide_grad, in_sem, out_sem, last_sem, through_sem,
):
    images, patch, high, width, token_half, chunks = sizes

    group = 3 if chunks % 3 == 0 else 1

    def span(c):
        return pl.ds(c * LANES, group * LANES)

    loads = {
        c: [
            pltpu.make_async_copy(summed.at[m, pl.ds(c, group)], sums.at[m, pl.ds(c, group)], in_sem.at[m, c]) for m in (0, 1)
        ]
        for c in range(0, chunks, group)
    }
    stores = {
        c: (
            pltpu.make_async_copy(wide_in.at[:, span(c)], d_in.at[:, span(c)], out_sem.at[0, c]),
            pltpu.make_async_copy(wide_out.at[span(c)], d_out.at[span(c)], out_sem.at[1, c]),
        )
        for c in range(0, chunks, group)
    }
    load_last = [
        pltpu.make_async_copy(summed.at[m, chunks, :, pl.ds(0, last.shape[2])], last.at[m], last_sem.at[m]) for m in (0, 1)
    ]
    ins, outs = [], []
    for b in range(images):
        ins.append(pltpu.make_async_copy(mixed_in.at[b], hold_mixed.at[b], through_sem.at[0, b]))
        outs.append(pltpu.make_async_copy(hold_mixed.at[b], mixed.at[b], through_sem.at[2, b]))
    for b in range(images):
        ins.append(pltpu.make_async_copy(grad_in.at[pl.ds(b * high, high)], hold_grad.at[b], through_sem.at[1, b]))
        outs.append(pltpu.make_async_copy(wide_grad.at[b], inputs_grad.at[b], through_sem.at[3, b]))

    def pass_on(i):
        ins[i].wait()
        if i >= images:
            wide_grad[i - images] = hold_grad[i - images, pl.ds(0, patch), :].astype(F32)
        outs[i].start()

    for pair in loads.values():
        for copy in pair:
            copy.start()
    for copy in load_last + ins:
        copy.start()
    through = iter(range(2 * images))
    for c in range(chunks):
        for copy in loads.get(c, ()):
            copy.wait()
        wide_in[:, c * LANES : (c + 1) * LANES] = sums[0, c].reshape(width, LANES).astype(F32)
        wide_out[c * LANES : (c + 1) * LANES, :] = sums[1, c].reshape(width, LANES).T.astype(F32)
        if (c + 1) % group == 0:
            for copy in stores[c + 1 - group]:
                copy.start()
        for i in [i for i in (next(through, None),) if i is not None]:
            pass_on(i)
    for i in through:
        pass_on(i)
    for copy in load_last:
        copy.wait()

    def token_block(m):
        halves = [last[m, j, pl.ds(0, token_half), :] for j in (0, 1)]
        return jnp.concatenate(halves, axis=1).astype(F32)

    grad = token_block(0)
    d_tin[...] = grad[:, :patch]
    d_tbias[...] = grad.T[patch : patch + 1].reshape(token_half)
    d_tout[...] = token_block(1)[:, :patch]
    blocks = width // LANES
    rows = last[0, 0, pl.ds(token_half, 64), :].astype(F32)

    def vector(first, count):
        return jnp.concatenate([rows[first + j : first + j + 1] for j in range(count)], axis=1)

    for v, ref in enumerate((d_gain1, d_shift1, d_gain2, d_shift2, d_cshift)):
        ref[...] = vector(v * blocks, blocks).reshape(width)
    d_tshift[...] = vector(5 * blocks, 2)[:, :patch].reshape(patch)
    d_cbias[...] = vector(5 * blocks + 2, chunks).reshape(chunks * LANES)
    for pair in stores.values():
        for copy in pair:
            copy.wait()
    for copy in outs:
        copy.wait()


def per_device(
    dp_size,
    patches, cotangent, gain_one, shift_one, token_in, token_bias, token_out, token_shift,
    gain_two, shift_two, channel_in, channel_bias, channel_out, channel_shift,
):
    images, patch, width = patches.shape
    token_half = token_in.shape[1]
    hidden_half = channel_in.shape[1]
    step = 2 * LANES
    ticks = hidden_half // step
    chunks = 2 * ticks
    high = -(-(patch + 3) // 16) * 16
    rows = -(-images * high // LANES) * LANES
    wide = -(-patch // LANES) * LANES
    tokens = 2 * token_half
    far = max(sum(1 for b in range(4, 20) if 2**b < dp_size), 1)
    far_chunks = chunks + 1 if dp_size > 16 else 1
    last_half = -(-(token_half + 64) // 64) * 64
    sizes = (images, patch, width, token_half, hidden_half, ticks, dp_size, last_half)
    hbm = pl.BlockSpec(memory_space=pl.ANY)
    n = chunks + 1
    half = width // 2
    dma = pltpu.SemaphoreType.DMA
    mixed, inputs_grad, summed, _, _ = pl.pallas_call(
        functools.partial(layer, sizes),
        out_shape=(
            jax.ShapeDtypeStruct((images, patch, width), BF16),
            jax.ShapeDtypeStruct((images * high, width), BF16),
            jax.ShapeDtypeStruct((2, n, 2, half, LANES), BF16),
            jax.ShapeDtypeStruct((images, tokens, width), BF16),
            jax.ShapeDtypeStruct((images, tokens, width), BF16),
        ),
        in_specs=[hbm] * 14,
        out_specs=(hbm,) * 5,
        scratch_shapes=[
            pltpu.VMEM((width, 2 * hidden_half), BF16),
            pltpu.VMEM((2 * hidden_half, width), BF16),
            pltpu.VMEM((8, width), F32),
            pltpu.VMEM((1, hidden_half), F32),
            pltpu.VMEM((1, hidden_half), F32),
            pltpu.VMEM((token_half,), F32),
            pltpu.VMEM((patch,), F32),
            pltpu.VMEM((token_half, patch), BF16),
            pltpu.VMEM((token_half, patch), BF16),
            pltpu.VMEM((2, tokens + 16, wide), BF16),
            pltpu.VMEM((wide, tokens), BF16),
            pltpu.VMEM((wide, tokens + 16), BF16),
            pltpu.VMEM((images, patch, width), F32),
            pltpu.VMEM((rows, width), BF16),
            pltpu.VMEM((width, rows), BF16),
            pltpu.VMEM((rows, width), BF16),
            pltpu.VMEM((width + 16, rows), BF16),
            pltpu.VMEM((images, high, width), BF16),
            pltpu.VMEM((rows, 2 * hidden_half), BF16),
            pltpu.VMEM((rows, 2 * hidden_half), BF16),
            pltpu.VMEM((high, width), BF16),
            pltpu.VMEM((2, patch, width), BF16),
            pltpu.VMEM((2, patch, width), BF16),
            pltpu.VMEM((2, tokens + 16, width), BF16),
            pltpu.VMEM((2, tokens, width), BF16),
            pltpu.VMEM((images, patch, 4), F32),
            pltpu.VMEM((8, width), F32),
            pltpu.VMEM((1, 2 * hidden_half), F32),
            pltpu.VMEM((tokens, wide), F32),
            pltpu.VMEM((tokens + 16, wide), F32),
            pltpu.VMEM((2, 64, LANES), F32),
            pltpu.VMEM((2, 2, 2, 2, 2, half, LANES), BF16),
            pltpu.VMEM((2, 2, 2, 2, half, LANES), BF16),
            pltpu.VMEM((n, 2, 2, half, LANES), BF16),
            pltpu.VMEM((n, 2, half, LANES), BF16),
            pltpu.VMEM((n, half, LANES), BF16),
            pltpu.VMEM((n, 3 * (half // 4), LANES), BF16),
            pltpu.VMEM((far_chunks, far, half // 4, LANES), BF16),
            dma((ticks, 2)),
            dma((5, 2)),
            dma((10,)),
            dma((2,)),
            dma((3,)), dma((3,)),
            dma((ticks, 4)), dma((ticks, 6)),
            dma((2, 2)), dma((2, 2)),
            dma((RING,)), dma((RING,)),
            dma((2, n)), dma((len(STRAIGHT),)), dma((n,)),
            dma((n,)), dma((n,)), dma((n,)), dma((n,)), dma((len(STRAIGHT),)),
            dma((n,)), dma((n,)), dma((len(STRAIGHT),)), dma((n,)), dma((2, n)),
            dma((far_chunks, far)), dma((far_chunks, far)),
            pltpu.SemaphoreType.REGULAR((4,)),
        ],
        compiler_params=pltpu.CompilerParams(
            collective_id=0, has_side_effects=True, vmem_limit_bytes=63 * 2**20
        ),
        name="mixer_layer",
    )(
        patches, cotangent, gain_one, shift_one, token_in.T, token_bias, token_out, token_shift,
        gain_two, shift_two, channel_in, channel_bias, channel_out, channel_shift,
    )

    vmem = pl.BlockSpec(memory_space=pltpu.VMEM)
    shapes = (
        (token_half, patch), (token_half,), (token_half, patch), (patch,),
        (width,), (width,), (width,), (width,), (hidden_half,), (width,),
    )
    (
        mixed, inputs_grad, d_in, d_out, d_tin, d_tbias, d_tout, d_tshift,
        d_gain1, d_shift1, d_gain2, d_shift2, d_cbias, d_cshift,
    ) = pl.pallas_call(
        functools.partial(widen, (images, patch, high, width, token_half, chunks)),
        in_specs=[hbm] * 3,
        out_specs=(hbm,) * 4 + (vmem,) * len(shapes),
        out_shape=(
            jax.ShapeDtypeStruct((images, patch, width), BF16),
            jax.ShapeDtypeStruct((images, patch, width), F32),
            jax.ShapeDtypeStruct((width, hidden_half), F32),
            jax.ShapeDtypeStruct((hidden_half, width), F32),
        ) + tuple(jax.ShapeDtypeStruct(shape, F32) for shape in shapes),
        scratch_shapes=[
            pltpu.VMEM((2, chunks, 2, half, LANES), BF16),
            pltpu.VMEM((2, 2, last_half, LANES), BF16),
            pltpu.VMEM((width, hidden_half), F32),
            pltpu.VMEM((hidden_half, width), F32),
            pltpu.VMEM((images, patch, width), BF16),
            pltpu.VMEM((images, high, width), BF16),
            pltpu.VMEM((images, patch, width), F32),
            dma((2, chunks)), dma((2, chunks)), dma((2,)), dma((4, images)),
        ],
        compiler_params=pltpu.CompilerParams(vmem_limit_bytes=60 * 2**20),
        name="widen",
    )(summed, mixed, inputs_grad)
    return (
        mixed, inputs_grad, d_gain1, d_shift1, d_tin.T, d_tbias, d_tout, d_tshift,
        d_gain2, d_shift2, d_in, d_cbias, d_out, d_cshift,
    )


def solution(mesh):
    split = P(("dp", "mp"), None, None)
    columns, rows, vector = P(None, "mp"), P("mp", None), P("mp")
    return jax.shard_map(
        functools.partial(per_device, mesh.shape["dp"]),
        mesh=mesh,
        in_specs=(
            split, split, P(), P(), columns, vector, rows, P(), P(), P(), columns, vector, rows, P(),
        ),
        out_specs=(
            split, split, P(), P(), columns, vector, rows, P(), P(), P(), columns, vector, rows, P(),
        ),
        check_vma=False,
    )
```
